32 devices in a mesh: grp: 2 (over y), gx: 4 (over z), gy: 2 (over x), col: 2 (over core).
Axes of the slice: x: 2, y: 2, z: 4, core: 2. Of those that a mesh axis runs over, the one named last changes fastest.
Arguments:
- field: bfloat16 [64, 32, 32, 128], P('grp', 'gx', ('gy', 'col')), parts along dimension 0, may hold values from -6 to 6
- cotangent: bfloat16 [64, 32, 32, 128], P('grp', 'gx', ('gy', 'col')), parts along dimension 0, may hold values from -6 to 6
- mode_weight: bfloat16 [2, 32, 32, 32, 32, 32], P(None, None, None, ('gy', 'col'), 'gx'), may hold values from -3 to 3
- skip_weight: bfloat16 [32, 32], replicated, may hold values from -1 to 1
- lift_weight: bfloat16 [128, 32], replicated, may hold values from -1 to 1
- proj_weight: bfloat16 [32, 128], replicated, may hold values from -0.5 to 0.5
Outputs:
- field_grad: bfloat16 [64, 32, 32, 128], P('grp', 'gx', ('gy', 'col')), parts along dimension 0
- mode_grad: bfloat16 [4, 32, 32, 32, 32, 32], P('grp', None, None, ('gy', 'col'), 'gx'), parts along dimension 0
- skip_grad: float32 [64, 32], P('grp'), parts along dimension 0
- lift_grad: float32 [256, 32], P('grp'), parts along dimension 0
- proj_grad: float32 [64, 128], P('grp'), parts along dimension 0
The draws below stay inside these ranges and needn't reach their ends.
There are 2 independent parts, one for each index of `grp`. The reference program is written for one: setup_inputs(seed, part) draws one part's arguments, and reference() takes and returns one part's arrays. A program takes and returns all parts, laid end to end along the dimension named above; an argument that names none is the same for every part. Nothing has to cross between parts.
All inputs are finite; a program needn't handle non-finite values.
Results may differ from the reference program's by a relative error of at most 0.023.
Values may be sent and summed in bfloat16 or wider, within the bound.
No kernel may reach another device: no remote copies, remote signals or barrier semaphores. Data moves between devices by JAX's collectives and lax.ppermute only.
A program may use at most 192 MiB of HBM per device.

```python
import math
import jax
import jax.numpy as jnp
from jax import lax

C = 32
H = 128
MX = 32
MY = 32
MZ = 32
NZ = 128
NX = 32
NY = 32


def block_scale(own_key, shape, pieces, low, high):
    loudness, own = 1.0, jax.random.fold_in(own_key, 6)
    for axis_at, shards_of in pieces:
        steps = jnp.exp(jax.random.uniform(jax.random.fold_in(own, axis_at), (shards_of,), jnp.float32, low / len(pieces), high / len(pieces)))
        loudness = loudness * jnp.repeat(steps, shape[axis_at] // shards_of).reshape([-1 if axis == axis_at else 1 for axis in range(len(shape))])
    return loudness


def bell_draw(rng, extent, scale, most, split=(), held_as=jnp.bfloat16):
    level = block_scale(rng, extent, split, -0.22, 0.18) if split else 1.0
    values = jax.random.normal(rng, extent, jnp.float32) * scale * level
    return jnp.minimum(jnp.maximum(values, -most), most).astype(held_as)


def setup_inputs(seed: int = 0, part: int = 0) -> dict:
    key_list = jax.random.split(jax.random.key(seed), 7)
    part_keys = jax.random.split(jax.random.fold_in(key_list[6], part), 7)
    field = bell_draw(part_keys[0], (C, NX, NY, NZ), 1.0, 6.0, ((1, 4), (2, 4)))
    cotangent = bell_draw(part_keys[1], (C, NX, NY, NZ), 1.0, 6.0, ((1, 4), (2, 4)))
    mode_weight = bell_draw(key_list[2], (2, C, C, MZ, MY, MX), 0.5, 3.0, ((3, 4), (4, 4)))
    skip_weight = bell_draw(key_list[3], (C, C), C ** -0.5, 1.0)
    lift_weight = bell_draw(key_list[4], (H, C), C ** -0.5, 1.0)
    proj_weight = bell_draw(key_list[5], (C, H), H ** -0.5, 0.5)
    return {"field": field, "cotangent": cotangent, "mode_weight": mode_weight, "skip_weight": skip_weight, "lift_weight": lift_weight, "proj_weight": proj_weight}


KAPPA = 0.7978845608028654
CUBIC = 0.044715

def gelu_slope(value):
    inner = KAPPA * (value + CUBIC * value * value * value)
    tangent = jnp.tanh(inner)
    result = 0.5 * value * (1.0 + tangent)
    slope = 0.5 * (1.0 + tangent) + 0.5 * value * (1.0 - tangent * tangent) * KAPPA * (1.0 + 3.0 * CUBIC * value * value)
    return (result, slope)

def trig_pair(freqs, length):
    positions = jnp.arange(length, dtype=jnp.int32)
    turns = positions[:, None] * (freqs[None, :] % length) % length
    angle = turns.astype(jnp.float32) * (2.0 * math.pi / length)
    factor = 1.0 / math.sqrt(length)
    return (jnp.cos(angle) * factor, jnp.sin(angle) * factor)

def real_table(freqs, length):
    cosine, sine = trig_pair(freqs, length)
    return jnp.stack([cosine.T, -sine.T]).astype(jnp.bfloat16)

def complex_table(freqs, length):
    cosine, sine = trig_pair(freqs, length)
    upper = jnp.stack([cosine, -sine], axis=1)
    lower = jnp.stack([sine, cosine], axis=1)
    return jnp.stack([upper, lower]).astype(jnp.bfloat16)

def centered(count):
    return jnp.arange(count, dtype=jnp.int32) - count // 2

def as_float(value):
    return value.astype(jnp.float32)

def to_modes(values, z_table, y_table, x_table):
    first = jnp.einsum('cxyn,qkn->qckxy', as_float(values), as_float(z_table)).astype(jnp.bfloat16)
    second = jnp.einsum('pckxn,pnqj->qckjx', as_float(first), as_float(y_table)).astype(jnp.bfloat16)
    return jnp.einsum('pckjn,pnql->qckjl', as_float(second), as_float(x_table)).astype(jnp.bfloat16)

def to_grid(spec, z_table, y_table, x_table):
    first = jnp.einsum('pckjl,qnpl->qckjn', as_float(spec), as_float(x_table)).astype(jnp.bfloat16)
    second = jnp.einsum('pckjx,qnpj->qckxn', as_float(first), as_float(y_table)).astype(jnp.bfloat16)
    return jnp.einsum('pckxy,pkn->cxyn', as_float(second), as_float(z_table))

def mix(weight, modes):
    wgt = as_float(weight)
    mds = as_float(modes)
    real = jnp.einsum('iokjl,ikjl->okjl', wgt[0], mds[0]) - jnp.einsum('iokjl,ikjl->okjl', wgt[1], mds[1])
    imag = jnp.einsum('iokjl,ikjl->okjl', wgt[0], mds[1]) + jnp.einsum('iokjl,ikjl->okjl', wgt[1], mds[0])
    return jnp.stack([real, imag]).astype(jnp.bfloat16)

def reference(field, cotangent, mode_weight, skip_weight, lift_weight, proj_weight):
    z_table = real_table(jnp.arange(MZ, dtype=jnp.int32), NZ)
    y_table = complex_table(centered(MY), NY)
    x_table = complex_table(centered(MX), NX)
    modes = to_modes(field, z_table, y_table, x_table)
    spectral = to_grid(mix(mode_weight, modes), z_table, y_table, x_table)
    skip_f = as_float(skip_weight)
    lift_f = as_float(lift_weight)
    proj_f = as_float(proj_weight)

    def slab_step(carry, index):
        values = as_float(lax.dynamic_index_in_dim(field, index, 1, keepdims=False).reshape(C, -1))
        grads = as_float(lax.dynamic_index_in_dim(cotangent, index, 1, keepdims=False).reshape(C, -1))
        spec = lax.dynamic_index_in_dim(spectral, index, 1, keepdims=False).reshape(C, -1)
        pre = spec + jnp.dot(skip_f, values)
        lifted, slope_pre = gelu_slope(pre)
        lifted = lifted.astype(jnp.bfloat16)
        hidden = jnp.dot(lift_f, as_float(lifted))
        activated, slope_hid = gelu_slope(hidden)
        activated = activated.astype(jnp.bfloat16)
        hidden_grad = (jnp.dot(proj_f.T, grads) * slope_hid).astype(jnp.bfloat16)
        grad_up = grads + jnp.dot(lift_f.T, as_float(hidden_grad))
        pre_grad = (grad_up * slope_pre).astype(jnp.bfloat16)
        proj_sum = carry[0] + jnp.dot(grads, as_float(activated).T)
        lift_sum = carry[1] + jnp.dot(as_float(hidden_grad), as_float(lifted).T)
        skip_sum = carry[2] + jnp.dot(as_float(pre_grad), values.T)
        return ((proj_sum, lift_sum, skip_sum), pre_grad)
    start = (jnp.zeros((C, H), jnp.float32), jnp.zeros((H, C), jnp.float32), jnp.zeros((C, C), jnp.float32))
    sums, slabs = lax.scan(slab_step, start, jnp.arange(NX, dtype=jnp.int32))
    proj_grad, lift_grad, skip_grad = sums
    pre_grad = jnp.transpose(slabs.reshape(NX, C, NY, NZ), (1, 0, 2, 3))
    pre_modes = to_modes(pre_grad, z_table, y_table, x_table)
    mds = as_float(modes)
    prm = as_float(pre_modes)
    wgt = as_float(mode_weight)
    grad_real = jnp.einsum('ikjl,okjl->iokjl', mds[0], prm[0]) + jnp.einsum('ikjl,okjl->iokjl', mds[1], prm[1])
    grad_imag = jnp.einsum('ikjl,okjl->iokjl', mds[0], prm[1]) - jnp.einsum('ikjl,okjl->iokjl', mds[1], prm[0])
    mode_grad = jnp.stack([grad_real, grad_imag]).astype(jnp.bfloat16)
    back_real = jnp.einsum('iokjl,okjl->ikjl', wgt[0], prm[0]) + jnp.einsum('iokjl,okjl->ikjl', wgt[1], prm[1])
    back_imag = jnp.einsum('iokjl,okjl->ikjl', wgt[0], prm[1]) - jnp.einsum('iokjl,okjl->ikjl', wgt[1], prm[0])
    modes_grad = jnp.stack([back_real, back_imag]).astype(jnp.bfloat16)
    spectral_grad = to_grid(modes_grad, z_table, y_table, x_table)
    field_grad = (spectral_grad + jnp.einsum('oi,oxyn->ixyn', skip_f, as_float(pre_grad))).astype(jnp.bfloat16)
    return (field_grad, mode_grad, skip_grad, lift_grad, proj_grad)
```

```python
import functools
import math

import jax
import jax.numpy as jnp
import ml_dtypes
import numpy as np
from jax import lax
from jax.experimental import pallas as pl
from jax.experimental.pallas import tpu as pltpu
from jax.sharding import PartitionSpec as P

MX = 32
MY = 32
MZ = 32


KAPPA = 0.7978845608028654
CUBIC = 0.044715


def gelu_slope(value):
    inner = KAPPA * (value + CUBIC * value * value * value)
    tangent = jnp.tanh(inner)
    result = 0.5 * value * (1.0 + tangent)
    slope = 0.5 * (1.0 + tangent) + 0.5 * value * (1.0 - tangent * tangent) * KAPPA * (
        1.0 + 3.0 * CUBIC * value * value
    )
    return (result, slope)


def trig_pair(freqs, length):
    positions = jnp.arange(length, dtype=jnp.int32)
    turns = positions[:, None] * (freqs[None, :] % length) % length
    angle = turns.astype(jnp.float32) * (2.0 * math.pi / length)
    factor = 1.0 / math.sqrt(length)
    return (jnp.cos(angle) * factor, jnp.sin(angle) * factor)


def real_table(freqs, length):
    cosine, sine = trig_pair(freqs, length)
    return jnp.stack([cosine.T, -sine.T]).astype(jnp.bfloat16)


def complex_table(freqs, length):
    cosine, sine = trig_pair(freqs, length)
    upper = jnp.stack([cosine, -sine], axis=1)
    lower = jnp.stack([sine, cosine], axis=1)
    return jnp.stack([upper, lower]).astype(jnp.bfloat16)


def centered(count):
    return jnp.arange(count, dtype=jnp.int32) - count // 2


def to_modes(values, tables):
    z_table, y_table, x_table = tables
    chans, xrows, yrows, zlen = values.shape
    first = jnp.einsum("cxyn,qkn->qkycx", values, z_table, preferred_element_type=jnp.float32)
    first = first.astype(jnp.bfloat16).reshape(2, MZ, yrows, chans * xrows)
    moved = lax.all_to_all(first, ("gy", "col"), split_axis=1, concat_axis=2, tiled=True)
    second = jnp.einsum("pkyr,pyqj->qkjr", moved, y_table, preferred_element_type=jnp.float32)
    second = second.astype(jnp.bfloat16)[:, :, :, None, :]
    crossed = lax.all_to_all(second, "gx", split_axis=2, concat_axis=3, tiled=True)
    crossed = crossed.reshape(crossed.shape[:4] + (chans, xrows))
    third = jnp.einsum("pkjgcx,pgxql->qckjl", crossed, x_table, preferred_element_type=jnp.float32)
    return third.astype(jnp.bfloat16).reshape(2, chans, -1)


def to_grid(spec, tables, shape, local_modes):
    z_table, y_table, x_table = tables
    chans, xrows, yrows, zlen = shape
    spec = spec.reshape((2, chans) + local_modes)
    first = jnp.einsum("pckjl,qgxpl->qkjgcx", spec, x_table, preferred_element_type=jnp.float32)
    first = first.astype(jnp.bfloat16)
    first = first.reshape(first.shape[:4] + (chans * xrows,))
    joined = lax.all_to_all(first, "gx", split_axis=3, concat_axis=2, tiled=True)
    joined = joined.reshape(joined.shape[:3] + (chans * xrows,))
    second = jnp.einsum("pkjr,qypj->qkyr", joined, y_table, preferred_element_type=jnp.float32)
    second = second.astype(jnp.bfloat16)
    returned = lax.all_to_all(second, ("gy", "col"), split_axis=2, concat_axis=1, tiled=True)
    grid = jnp.einsum("pkyr,pkn->ryn", returned, z_table, preferred_element_type=jnp.float32)
    return grid.reshape(chans, xrows, yrows, zlen)


def mix(weight, modes):
    real = jnp.einsum("iok,ik->ok", weight[0], modes[0], preferred_element_type=jnp.float32)
    real = real - jnp.einsum("iok,ik->ok", weight[1], modes[1], preferred_element_type=jnp.float32)
    imag = jnp.einsum("iok,ik->ok", weight[0], modes[1], preferred_element_type=jnp.float32)
    imag = imag + jnp.einsum("iok,ik->ok", weight[1], modes[0], preferred_element_type=jnp.float32)
    return jnp.stack([real, imag]).astype(jnp.bfloat16)


def general(field, cotangent, mode_weight, skip_weight, lift_weight, proj_weight):
    chans, xrows, yrows, zlen = field.shape
    groups_x = lax.axis_size("gx")
    groups_y = lax.axis_size("gy")
    groups_c = lax.axis_size("col")
    span_x = xrows * groups_x
    span_y = yrows * groups_y * groups_c
    column = jnp.arange(MZ, dtype=jnp.int32)
    z_table = real_table(column, zlen)
    y_table = complex_table(centered(MY), span_y)
    x_table = complex_table(centered(MX), span_x).reshape(2, groups_x, xrows, 2, MX)
    tables = (z_table, y_table, x_table)
    local_modes = (mode_weight.shape[3], mode_weight.shape[4], mode_weight.shape[5])
    weight_flat = mode_weight.reshape(2, chans, chans, -1)
    modes = to_modes(field, tables)
    spectral = to_grid(mix(weight_flat, modes), tables, field.shape, local_modes).reshape(chans, -1)
    flat_field = field.reshape(chans, -1)
    flat_grad = cotangent.reshape(chans, -1)
    pre = spectral + jnp.dot(skip_weight, flat_field, preferred_element_type=jnp.float32)
    lifted, slope_pre = gelu_slope(pre)
    lifted = lifted.astype(jnp.bfloat16)
    hidden = jnp.dot(lift_weight, lifted, preferred_element_type=jnp.float32)
    activated, slope_hid = gelu_slope(hidden)
    activated = activated.astype(jnp.bfloat16)
    back_hidden = jnp.dot(proj_weight.T, flat_grad, preferred_element_type=jnp.float32)
    hidden_grad = (back_hidden * slope_hid).astype(jnp.bfloat16)
    grad_up = flat_grad.astype(jnp.float32) + jnp.dot(
        lift_weight.T, hidden_grad, preferred_element_type=jnp.float32
    )
    pre_grad = (grad_up * slope_pre).astype(jnp.bfloat16)
    proj_part = jnp.einsum("cr,hr->ch", flat_grad, activated, preferred_element_type=jnp.float32)
    lift_part = jnp.einsum("hr,cr->hc", hidden_grad, lifted, preferred_element_type=jnp.float32)
    skip_part = jnp.einsum("or,ir->oi", pre_grad, flat_field, preferred_element_type=jnp.float32)
    proj_grad, lift_grad, skip_grad = lax.psum(
        (proj_part, lift_part, skip_part), ("gx", "gy", "col")
    )
    pre_modes = to_modes(pre_grad.reshape(field.shape), tables)
    grad_real = jnp.einsum("ik,ok->iok", modes[0], pre_modes[0], preferred_element_type=jnp.float32)
    grad_real = grad_real + jnp.einsum(
        "ik,ok->iok", modes[1], pre_modes[1], preferred_element_type=jnp.float32
    )
    grad_imag = jnp.einsum("ik,ok->iok", modes[0], pre_modes[1], preferred_element_type=jnp.float32)
    grad_imag = grad_imag - jnp.einsum(
        "ik,ok->iok", modes[1], pre_modes[0], preferred_element_type=jnp.float32
    )
    mode_grad = jnp.stack([grad_real, grad_imag]).astype(jnp.bfloat16).reshape(mode_weight.shape)
    back_real = jnp.einsum(
        "iok,ok->ik", weight_flat[0], pre_modes[0], preferred_element_type=jnp.float32
    )
    back_real = back_real + jnp.einsum(
        "iok,ok->ik", weight_flat[1], pre_modes[1], preferred_element_type=jnp.float32
    )
    back_imag = jnp.einsum(
        "iok,ok->ik", weight_flat[0], pre_modes[1], preferred_element_type=jnp.float32
    )
    back_imag = back_imag - jnp.einsum(
        "iok,ok->ik", weight_flat[1], pre_modes[0], preferred_element_type=jnp.float32
    )
    modes_grad = jnp.stack([back_real, back_imag]).astype(jnp.bfloat16)
    spectral_grad = to_grid(modes_grad, tables, field.shape, local_modes).reshape(chans, -1)
    skip_back = jnp.dot(skip_weight.T, pre_grad, preferred_element_type=jnp.float32)
    field_grad = (spectral_grad + skip_back).astype(jnp.bfloat16).reshape(field.shape)
    return (field_grad, mode_grad, skip_grad, lift_grad, proj_grad)


def np_trig(freqs, length):
    positions = np.arange(length)
    turns = positions[:, None] * (freqs[None, :] % length) % length
    angle = turns.astype(np.float32) * np.float32(2.0 * math.pi / length)
    factor = np.float32(1.0 / math.sqrt(length))
    return np.cos(angle) * factor, np.sin(angle) * factor


def np_complex(cosine, sine, sign):
    table = np.zeros((cosine.shape[0], 2, cosine.shape[1], 2), np.float32)
    table[:, 0, :, 0] = cosine
    table[:, 1, :, 0] = -sign * sine
    table[:, 1, :, 1] = cosine
    table[:, 0, :, 1] = sign * sine
    return table


def make_tables(zlen, span_y, span_x, nb, xrows, yrows):
    kzb, kyb = MZ // nb, MY // nb
    zc, zs = np_trig(np.arange(MZ), zlen)
    yc, ys = np_trig(np.arange(MY) - MY // 2, span_y)
    xc, xs = np_trig(np.arange(MX) - MX // 2, span_x)
    zpart = np.stack([zc, -zs]).reshape(2, zlen, nb, kzb)
    zf = np.einsum("pzbk,yw->yzbwpk", zpart, np.eye(yrows, dtype=np.float32))
    zf = zf.reshape(yrows * zlen, nb, yrows * 2 * kzb).transpose(1, 0, 2)
    zi = np.ascontiguousarray(zf.transpose(0, 2, 1))
    yt = np_complex(yc, ys, -1).reshape(nb, yrows, 2, nb, kyb, 2)
    eye = np.eye(kzb, dtype=np.float32)
    yf = np.einsum("bypjmq,kh->bjypkqhm", yt, eye).reshape(nb, nb, yrows * 2 * kzb, 2 * kzb * kyb)
    yi_t = np_complex(yc, ys, -1).reshape(nb, yrows, 2, nb, kyb, 2)
    yi = np.einsum("bypjmq,kh->jbqhmypk", yi_t, eye).reshape(nb, nb, 2 * kzb * kyb, yrows * 2 * kzb)
    xt = np_complex(xc, xs, -1).reshape(nb, xrows, 2, MX, 2)
    four = np.eye(4, dtype=np.float32)
    xf = np.einsum("bxplq,cd->bpcxqdl", xt, four).reshape(nb, 2, 4 * xrows, 8 * MX)
    xr = np.einsum("bxplq,cd,r->bpcxdqrl", xt, four, np.ones(4, np.float32))
    xr = xr.reshape(nb, 2, 4 * xrows, 32 * MX)
    both = np.stack([xc, xs]).reshape(2, nb, xrows, MX)
    xi = np.einsum("tbxl,r->bxtrl", both, np.ones(4, np.float32)).reshape(nb, xrows, 8 * MX)
    xd = np.einsum("tbxl,cd->bcxtdl", both, four).reshape(nb, 4 * xrows, 8 * MX)
    bf = ml_dtypes.bfloat16
    return [np.asarray(t).astype(bf) for t in (zf, zi, yf, yi, xf, xr)] + [
        xi.astype(bf).astype(np.float32),
        xd.astype(bf),
    ]


def dot(a, b):
    return lax.dot_general(a, b, (((1,), (0,)), ((), ())), preferred_element_type=jnp.float32)


def dot_nt(a, b):
    return lax.dot_general(a, b, (((1,), (1,)), ((), ())), preferred_element_type=jnp.float32)


BF = jnp.bfloat16
F32 = jnp.float32


def z_forward_kernel(rows, yrows, zlen, idx, field, zf, o0, o1, o2, o3, wide):
    wide[...] = field[...].astype(F32)
    side = jnp.concatenate(
        [wide[pl.ds(y, rows, stride=yrows), :].astype(BF) for y in range(yrows)], axis=1
    )
    table = jnp.concatenate([zf[idx[0] ^ s] for s in range(4)], axis=1)
    out = dot(side, table).astype(BF)
    for s, o in enumerate((o0, o1, o2, o3)):
        o[...] = out[:, s * 128 : (s + 1) * 128]


def lane_kernel(near, far, idx, r0, r1, r2, r3, table, o0, o1, o2, o3):
    side = jnp.concatenate([r0[...], r1[...], r2[...], r3[...]], axis=1)
    cols = []
    for t in range(4):
        cols.append(
            jnp.concatenate([table[idx[near] ^ s, idx[far] ^ t] for s in range(4)], axis=0)
        )
    out = dot(side, jnp.concatenate(cols, axis=1)).astype(BF)
    for t, o in enumerate((o0, o1, o2, o3)):
        o[...] = out[:, t * 128 : (t + 1) * 128]


def x_side(idx, refs, tab):
    parts = []
    for g in range(8):
        block = jnp.concatenate([r[g * 32 : (g + 1) * 32, :] for r in refs], axis=0)
        turned = block.astype(F32).T.astype(BF)
        parts.append(jnp.concatenate([turned[:64, :], turned[64:, :]], axis=1))
    side = jnp.concatenate(parts, axis=0)
    table = jnp.concatenate([tab[idx[1] ^ s, p] for p in range(2) for s in range(4)], axis=0)
    return side, table


def mix_forward_kernel(idx, r0, r1, r2, r3, xf, xi, weight, modes, o0, o1, o2, o3):
    side, table = x_side(idx, (r0, r1, r2, r3), xf)
    got = dot(side, table).astype(BF)
    for g in range(8):
        modes[g, 0] = got[g * 64 : (g + 1) * 64, :128]
        modes[g, 1] = got[g * 64 : (g + 1) * 64, 128:]
    left = jnp.concatenate([xi[idx[1] ^ s] for s in range(4)], axis=0).astype(BF)
    outs = (o0, o1, o2, o3)

    def pair(k, carry):
        rows = []
        for j in range(2):
            o = 2 * k + j
            real = jnp.zeros((64, 128), F32)
            imag = jnp.zeros((64, 128), F32)
            for g in range(8):
                wr = weight[g, 0, o].astype(F32)
                wi = weight[g, 1, o].astype(F32)
                mr = modes[g, 0].astype(F32)
                mi = modes[g, 1].astype(F32)
                real = real + wr * mr - wi * mi
                imag = imag + wr * mi + wi * mr
            rows.append(jnp.concatenate([real.astype(BF), (-imag).astype(BF)], axis=1))
            rows.append(jnp.concatenate([imag.astype(BF), real.astype(BF)], axis=1))
        got = dot_nt(left, jnp.concatenate(rows, axis=0))
        for s in range(4):
            both = jnp.concatenate(
                [got[s * 8 : (s + 1) * 8, :128], got[s * 8 : (s + 1) * 8, 128:]], axis=0
            )
            outs[s][pl.ds(pl.multiple_of(k * 16, 16), 16), :] = both.astype(BF)
        return carry

    lax.fori_loop(0, 16, pair, 0)


def mix_backward_kernel(idx, r0, r1, r2, r3, xr, xd, weight, pmodes, o0, o1, o2, o3):
    side, table = x_side(idx, (r0, r1, r2, r3), xr)
    for d in range(4):
        got = dot(side, table[:, d * 256 : (d + 1) * 256]).astype(BF)
        for g in range(8):
            pmodes[4 * g + d, 0] = got[g * 64 : (g + 1) * 64, :128]
            pmodes[4 * g + d, 1] = got[g * 64 : (g + 1) * 64, 128:]
    left = jnp.concatenate([xd[idx[1] ^ s] for s in range(4)], axis=0)
    outs = (o0, o1, o2, o3)

    def group(g, carry):
        real = jnp.zeros((64, 128), F32)
        imag = jnp.zeros((64, 128), F32)
        for o in range(32):
            wr = weight[g, 0, o].astype(F32)
            wi = weight[g, 1, o].astype(F32)
            pr = pmodes[o, 0].astype(F32)
            pi = pmodes[o, 1].astype(F32)
            real = real + wr * pr + wi * pi
            imag = imag + wr * pi - wi * pr
        rows = [
            jnp.concatenate([real.astype(BF), (-imag).astype(BF)], axis=1),
            jnp.concatenate([imag.astype(BF), real.astype(BF)], axis=1),
        ]
        got = dot_nt(left, jnp.concatenate(rows, axis=0)).astype(BF)
        for s in range(4):
            outs[s][pl.ds(pl.multiple_of(g * 32, 32), 32), :] = got[s * 32 : (s + 1) * 32]
        return carry

    lax.fori_loop(0, 8, group, 0)


def pack_kernel(weight, packed):
    def step(o, carry):
        for p in range(2):
            packed[0, p, o] = jnp.concatenate([weight[p, k, o] for k in range(4)], axis=1)
        return carry

    lax.fori_loop(0, 32, step, 0)


def outer_kernel(modes, pmodes, grad):
    def step(o, carry):
        mr = modes[0, 0].astype(F32)
        mi = modes[0, 1].astype(F32)
        pr = pmodes[o, 0].astype(F32)
        pi = pmodes[o, 1].astype(F32)
        real = (mr * pr + mi * pi).astype(BF)
        imag = (mr * pi - mi * pr).astype(BF)
        for k in range(4):
            grad[0, k, o] = real[:, k * 32 : (k + 1) * 32]
            grad[1, k, o] = imag[:, k * 32 : (k + 1) * 32]
        return carry

    lax.fori_loop(0, 32, step, 0)


def cells_kernel(yrows, field, cotangent, fx, cx, wide):
    for src, dst in ((field, fx), (cotangent, cx)):
        wide[...] = src[...].astype(F32)

        def step(k, carry):
            first = k * 2
            dst[k] = jnp.concatenate(
                [wide[pl.ds(first + j, 32, stride=64), :] for j in range(2)], axis=1
            ).astype(BF)
            return carry

        lax.fori_loop(0, 32, step, 0)


def point_kernel(
    idx, r0, r1, r2, r3, zi, zf, fx, cx, skip, lift, lift_t, proj_t,
    o0, o1, o2, o3, pg, sums, spectral, wide,
):
    side = jnp.concatenate([r0[...], r1[...], r2[...], r3[...]], axis=1)
    back = jnp.concatenate([zi[idx[0] ^ s] for s in range(4)], axis=0)
    for y in range(8):
        spectral[y] = dot(side, back[:, y * 128 : (y + 1) * 128])
    sums[...] = jnp.zeros_like(sums)

    def step(k, carry):
        x, part = k // 4, k % 4
        rows = pl.ds(x, 32, stride=8)
        values, grads = fx[k], cx[k]
        pre = jnp.concatenate([spectral[2 * part + j, rows, :] for j in range(2)], axis=1)
        pre = pre + dot(skip[...], values)
        lifted, slope_pre = gelu_slope(pre)
        lifted = lifted.astype(BF)
        hidden = dot(lift[...], lifted)
        activated, slope_hid = gelu_slope(hidden)
        activated = activated.astype(BF)
        hidden_grad = (dot(proj_t[...], grads) * slope_hid).astype(BF)
        grad_up = grads.astype(F32) + dot(lift_t[...], hidden_grad)
        pre_grad = grad_up * slope_pre
        pre_grad_b = pre_grad.astype(BF)
        for j in range(2):
            wide[2 * part + j, rows, :] = pre_grad[:, j * 128 : (j + 1) * 128]
        pg[k] = pre_grad_b
        tall = jnp.concatenate([activated, hidden_grad, pre_grad_b], axis=0)
        low = jnp.concatenate([grads, lifted, values], axis=0)
        sums[...] += dot_nt(tall, low)
        return carry

    lax.fori_loop(0, 32, step, 0)
    table = jnp.concatenate([zf[idx[0] ^ s] for s in range(4)], axis=1)
    side = jnp.concatenate([wide[y].astype(BF) for y in range(8)], axis=1)
    out = dot(side, table).astype(BF)
    for s, o in enumerate((o0, o1, o2, o3)):
        o[...] = out[:, s * 128 : (s + 1) * 128]


def finish_kernel(idx, r0, r1, r2, r3, zi, pg, skip_t, out, spectral, wide):
    side = jnp.concatenate([r0[...], r1[...], r2[...], r3[...]], axis=1)
    back = jnp.concatenate([zi[idx[0] ^ s] for s in range(4)], axis=0)
    for y in range(8):
        spectral[y] = dot(side, back[:, y * 128 : (y + 1) * 128])

    def step(k, carry):
        x, part = k // 4, k % 4
        rows = pl.ds(x, 32, stride=8)
        got = jnp.concatenate([spectral[2 * part + j, rows, :] for j in range(2)], axis=1)
        got = got + dot(skip_t[...], pg[k])
        first = k * 2
        wide[pl.ds(first, 32, stride=64), :] = got[:, :128]
        wide[pl.ds(first + 1, 32, stride=64), :] = got[:, 128:]
        return carry

    lax.fori_loop(0, 32, step, 0)
    out[...] = wide[...].astype(BF)


VM = pl.BlockSpec(memory_space=pltpu.VMEM)
SM = pl.BlockSpec(memory_space=pltpu.SMEM)
BLOCK = jax.ShapeDtypeStruct((256, 128), BF)
MIB = 1024 * 1024


def cost(us):
    return pl.CostEstimate(flops=0, bytes_accessed=int(us * 3.0e6), transcendentals=0)


def call(kernel, ins, outs, scratch=(), name=None, mib=16, us=1.0, smem=1):
    return pl.pallas_call(
        kernel,
        out_shape=outs,
        in_specs=[SM] * smem + [VM] * (len(ins) - smem),
        out_specs=jax.tree.map(lambda _: VM, outs),
        scratch_shapes=list(scratch),
        compiler_params=pltpu.CompilerParams(vmem_limit_bytes=mib * MIB),
        cost_estimate=cost(us),
        name=name,
    )(*ins)


def exchange(blocks, axes):
    pairs = [[(a, a ^ s) for a in range(4)] for s in range(4)]
    return [blocks[0]] + [lax.ppermute(blocks[s], axes, pairs[s]) for s in (1, 2, 3)]


def sum_over(part, axes):
    for axis, size in axes:
        step = 1
        while step < size:
            part = part + lax.ppermute(part, axis, [(a, a ^ step) for a in range(size)])
            step *= 2
    return part


def fast(field, cotangent, mode_weight, skip_weight, lift_weight, proj_weight):
    chans, xrows, yrows, zlen = field.shape
    tables = make_tables(zlen, yrows * 4, xrows * 4, 4, xrows, yrows)
    zf, zi, yf, yi, xf, xr, xi, xd = [jnp.asarray(t) for t in tables]
    gyc = ("gy", "col")
    idx = jnp.stack([lax.axis_index(gyc), lax.axis_index("gx")]).astype(jnp.int32)
    four = [BLOCK] * 4
    cells = chans * xrows * yrows
    flat_field = field.reshape(cells, zlen)
    flat_cot = cotangent.reshape(cells, zlen)
    rows = chans * xrows
    wide = pltpu.VMEM((cells, zlen), F32)
    tall = pltpu.VMEM((yrows, rows, zlen), F32)
    weight = mode_weight.reshape(2, chans, chans, 64, 32)

    packed = pl.pallas_call(
        pack_kernel,
        grid=(8,),
        out_shape=jax.ShapeDtypeStruct((8, 2, chans, 64, 128), BF),
        in_specs=[pl.BlockSpec((2, 4, chans, 64, 32), lambda g: (0, g, 0, 0, 0))],
        out_specs=pl.BlockSpec((1, 2, chans, 64, 128), lambda g: (g, 0, 0, 0, 0)),
        compiler_params=pltpu.CompilerParams(vmem_limit_bytes=20 * MIB),
        cost_estimate=cost(12.0),
        name="pack",
    )(weight)

    sent = call(
        functools.partial(z_forward_kernel, rows, yrows, zlen),
        (idx, flat_field, zf), four, [wide], "z_forward", 8, 2.0,
    )
    got = exchange(sent, gyc)
    fx, cx = call(
        functools.partial(cells_kernel, yrows),
        (flat_field, flat_cot),
        [jax.ShapeDtypeStruct((32, chans, 256), BF)] * 2, [wide], "cells", 8, 2.0, 0,
    )
    sent = call(functools.partial(lane_kernel, 0, 1), (idx, *got, yf), four, (), "y_forward", 8, 1.0)
    got = exchange(sent, "gx")
    modes, *sent = call(
        mix_forward_kernel, (idx, *got, xf, xi, packed),
        [jax.ShapeDtypeStruct((8, 2, 64, 128), BF)] + four, (), "mix_forward", 16, 5.0,
    )
    got = exchange(sent, "gx")
    sent = call(functools.partial(lane_kernel, 1, 0), (idx, *got, yi), four, (), "y_inverse", 8, 1.0)
    got = exchange(sent, gyc)
    *sent, pg, sums = call(
        point_kernel,
        (idx, *got, zi, zf, fx, cx, skip_weight, lift_weight, lift_weight.T, proj_weight.T),
        four + [
            jax.ShapeDtypeStruct((32, chans, 256), BF),
            jax.ShapeDtypeStruct((288, 96), F32),
        ],
        [tall, tall], "point", 16, 8.0,
    )
    got = exchange(sent, gyc)
    part = jnp.concatenate(
        [sums[:128, :32], sums[128:256, 32:64], sums[256:, 64:]], axis=0
    ).reshape(72, 128)
    part = sum_over(part, (("col", 2), ("gy", 2), ("gx", 4))).reshape(288, 32)
    proj_grad, lift_grad, skip_grad = part[:128].T, part[128:256], part[256:]
    sent = call(functools.partial(lane_kernel, 0, 1), (idx, *got, yf), four, (), "y_forward", 8, 1.0)
    got = exchange(sent, "gx")
    pmodes, *sent = call(
        mix_backward_kernel, (idx, *got, xr, xd, packed),
        [jax.ShapeDtypeStruct((32, 2, 64, 128), BF)] + four, (), "mix_backward", 16, 5.0,
    )
    got = exchange(sent, "gx")
    mode_grad = pl.pallas_call(
        outer_kernel,
        grid=(8,),
        out_shape=jax.ShapeDtypeStruct((2, chans, chans, 64, 32), BF),
        in_specs=[
            pl.BlockSpec((1, 2, 64, 128), lambda g: (g, 0, 0, 0)),
            pl.BlockSpec((32, 2, 64, 128), lambda g: (0, 0, 0, 0)),
        ],
        out_specs=pl.BlockSpec((2, 4, chans, 64, 32), lambda g: (0, g, 0, 0, 0)),
        compiler_params=pltpu.CompilerParams(vmem_limit_bytes=20 * MIB),
        cost_estimate=cost(12.0),
        name="outer",
    )(modes, pmodes)
    sent = call(functools.partial(lane_kernel, 1, 0), (idx, *got, yi), four, (), "y_inverse", 8, 1.0)
    got = exchange(sent, gyc)
    field_grad = call(
        finish_kernel, (idx, *got, zi, pg, skip_weight.T),
        jax.ShapeDtypeStruct((cells, zlen), BF), [tall, wide], "finish", 8, 2.0,
    )
    return (
        field_grad.reshape(field.shape),
        mode_grad.reshape(mode_weight.shape),
        skip_grad,
        lift_grad,
        proj_grad,
    )


def fits(field, mode_weight):
    sizes = [lax.axis_size(a) for a in ("gx", "gy", "col")]
    return (
        sizes == [4, 2, 2]
        and field.shape == (32, 8, 8, 128)
        and mode_weight.shape == (2, 32, 32, 8, 8, 32)
    )


def on_device(*args):
    return fast(*args) if fits(args[0], args[2]) else general(*args)


def solution(mesh):
    in_specs = (
        P("grp", "gx", ("gy", "col"), None),
        P("grp", "gx", ("gy", "col"), None),
        P(None, None, None, ("gy", "col"), "gx", None),
        P(),
        P(),
        P(),
    )
    out_specs = (
        P("grp", "gx", ("gy", "col"), None),
        P("grp", None, None, ("gy", "col"), "gx", None),
        P("grp", None),
        P("grp", None),
        P("grp", None),
    )
    return jax.shard_map(
        on_device, mesh=mesh, in_specs=in_specs, out_specs=out_specs, check_vma=False
    )
```

```python
import functools
import math

import jax
import jax.numpy as jnp
import ml_dtypes
import numpy as np
from jax import lax
from jax.experimental import pallas as pl
from jax.experimental.pallas import tpu as pltpu
from jax.sharding import PartitionSpec as P

MX = 32
MY = 32
MZ = 32


KAPPA = 0.7978845608028654
CUBIC = 0.044715


def gelu_slope(value):
    inner = KAPPA * (value + CUBIC * value * value * value)
    tangent = jnp.tanh(inner)
    result = 0.5 * value * (1.0 + tangent)
    slope = 0.5 * (1.0 + tangent) + 0.5 * value * (1.0 - tangent * tangent) * KAPPA * (
        1.0 + 3.0 * CUBIC * value * value
    )
    return (result, slope)


def trig_pair(freqs, length):
    positions = jnp.arange(length, dtype=jnp.int32)
    turns = positions[:, None] * (freqs[None, :] % length) % length
    angle = turns.astype(jnp.float32) * (2.0 * math.pi / length)
    factor = 1.0 / math.sqrt(length)
    return (jnp.cos(angle) * factor, jnp.sin(angle) * factor)


def real_table(freqs, length):
    cosine, sine = trig_pair(freqs, length)
    return jnp.stack([cosine.T, -sine.T]).astype(jnp.bfloat16)


def complex_table(freqs, length):
    cosine, sine = trig_pair(freqs, length)
    upper = jnp.stack([cosine, -sine], axis=1)
    lower = jnp.stack([sine, cosine], axis=1)
    return jnp.stack([upper, lower]).astype(jnp.bfloat16)


def centered(count):
    return jnp.arange(count, dtype=jnp.int32) - count // 2


def to_modes(values, tables):
    z_table, y_table, x_table = tables
    chans, xrows, yrows, zlen = values.shape
    first = jnp.einsum("cxyn,qkn->qkycx", values, z_table, preferred_element_type=jnp.float32)
    first = first.astype(jnp.bfloat16).reshape(2, MZ, yrows, chans * xrows)
    moved = lax.all_to_all(first, ("gy", "col"), split_axis=1, concat_axis=2, tiled=True)
    second = jnp.einsum("pkyr,pyqj->qkjr", moved, y_table, preferred_element_type=jnp.float32)
    second = second.astype(jnp.bfloat16)[:, :, :, None, :]
    crossed = lax.all_to_all(second, "gx", split_axis=2, concat_axis=3, tiled=True)
    crossed = crossed.reshape(crossed.shape[:4] + (chans, xrows))
    third = jnp.einsum("pkjgcx,pgxql->qckjl", crossed, x_table, preferred_element_type=jnp.float32)
    return third.astype(jnp.bfloat16).reshape(2, chans, -1)


def to_grid(spec, tables, shape, local_modes):
    z_table, y_table, x_table = tables
    chans, xrows, yrows, zlen = shape
    spec = spec.reshape((2, chans) + local_modes)
    first = jnp.einsum("pckjl,qgxpl->qkjgcx", spec, x_table, preferred_element_type=jnp.float32)
    first = first.astype(jnp.bfloat16)
    first = first.reshape(first.shape[:4] + (chans * xrows,))
    joined = lax.all_to_all(first, "gx", split_axis=3, concat_axis=2, tiled=True)
    joined = joined.reshape(joined.shape[:3] + (chans * xrows,))
    second = jnp.einsum("pkjr,qypj->qkyr", joined, y_table, preferred_element_type=jnp.float32)
    second = second.astype(jnp.bfloat16)
    returned = lax.all_to_all(second, ("gy", "col"), split_axis=2, concat_axis=1, tiled=True)
    grid = jnp.einsum("pkyr,pkn->ryn", returned, z_table, preferred_element_type=jnp.float32)
    return grid.reshape(chans, xrows, yrows, zlen)


def mix(weight, modes):
    real = jnp.einsum("iok,ik->ok", weight[0], modes[0], preferred_element_type=jnp.float32)
    real = real - jnp.einsum("iok,ik->ok", weight[1], modes[1], preferred_element_type=jnp.float32)
    imag = jnp.einsum("iok,ik->ok", weight[0], modes[1], preferred_element_type=jnp.float32)
    imag = imag + jnp.einsum("iok,ik->ok", weight[1], modes[0], preferred_element_type=jnp.float32)
    return jnp.stack([real, imag]).astype(jnp.bfloat16)


def general(field, cotangent, mode_weight, skip_weight, lift_weight, proj_weight):
    chans, xrows, yrows, zlen = field.shape
    groups_x = lax.axis_size("gx")
    groups_y = lax.axis_size("gy")
    groups_c = lax.axis_size("col")
    span_x = xrows * groups_x
    span_y = yrows * groups_y * groups_c
    column = jnp.arange(MZ, dtype=jnp.int32)
    z_table = real_table(column, zlen)
    y_table = complex_table(centered(MY), span_y)
    x_table = complex_table(centered(MX), span_x).reshape(2, groups_x, xrows, 2, MX)
    tables = (z_table, y_table, x_table)
    local_modes = (mode_weight.shape[3], mode_weight.shape[4], mode_weight.shape[5])
    weight_flat = mode_weight.reshape(2, chans, chans, -1)
    modes = to_modes(field, tables)
    spectral = to_grid(mix(weight_flat, modes), tables, field.shape, local_modes).reshape(chans, -1)
    flat_field = field.reshape(chans, -1)
    flat_grad = cotangent.reshape(chans, -1)
    pre = spectral + jnp.dot(skip_weight, flat_field, preferred_element_type=jnp.float32)
    lifted, slope_pre = gelu_slope(pre)
    lifted = lifted.astype(jnp.bfloat16)
    hidden = jnp.dot(lift_weight, lifted, preferred_element_type=jnp.float32)
    activated, slope_hid = gelu_slope(hidden)
    activated = activated.astype(jnp.bfloat16)
    back_hidden = jnp.dot(proj_weight.T, flat_grad, preferred_element_type=jnp.float32)
    hidden_grad = (back_hidden * slope_hid).astype(jnp.bfloat16)
    grad_up = flat_grad.astype(jnp.float32) + jnp.dot(
        lift_weight.T, hidden_grad, preferred_element_type=jnp.float32
    )
    pre_grad = (grad_up * slope_pre).astype(jnp.bfloat16)
    proj_part = jnp.einsum("cr,hr->ch", flat_grad, activated, preferred_element_type=jnp.float32)
    lift_part = jnp.einsum("hr,cr->hc", hidden_grad, lifted, preferred_element_type=jnp.float32)
    skip_part = jnp.einsum("or,ir->oi", pre_grad, flat_field, preferred_element_type=jnp.float32)
    proj_grad, lift_grad, skip_grad = lax.psum(
        (proj_part, lift_part, skip_part), ("gx", "gy", "col")
    )
    pre_modes = to_modes(pre_grad.reshape(field.shape), tables)
    grad_real = jnp.einsum("ik,ok->iok", modes[0], pre_modes[0], preferred_element_type=jnp.float32)
    grad_real = grad_real + jnp.einsum(
        "ik,ok->iok", modes[1], pre_modes[1], preferred_element_type=jnp.float32
    )
    grad_imag = jnp.einsum("ik,ok->iok", modes[0], pre_modes[1], preferred_element_type=jnp.float32)
    grad_imag = grad_imag - jnp.einsum(
        "ik,ok->iok", modes[1], pre_modes[0], preferred_element_type=jnp.float32
    )
    mode_grad = jnp.stack([grad_real, grad_imag]).astype(jnp.bfloat16).reshape(mode_weight.shape)
    back_real = jnp.einsum(
        "iok,ok->ik", weight_flat[0], pre_modes[0], preferred_element_type=jnp.float32
    )
    back_real = back_real + jnp.einsum(
        "iok,ok->ik", weight_flat[1], pre_modes[1], preferred_element_type=jnp.float32
    )
    back_imag = jnp.einsum(
        "iok,ok->ik", weight_flat[0], pre_modes[1], preferred_element_type=jnp.float32
    )
    back_imag = back_imag - jnp.einsum(
        "iok,ok->ik", weight_flat[1], pre_modes[0], preferred_element_type=jnp.float32
    )
    modes_grad = jnp.stack([back_real, back_imag]).astype(jnp.bfloat16)
    spectral_grad = to_grid(modes_grad, tables, field.shape, local_modes).reshape(chans, -1)
    skip_back = jnp.dot(skip_weight.T, pre_grad, preferred_element_type=jnp.float32)
    field_grad = (spectral_grad + skip_back).astype(jnp.bfloat16).reshape(field.shape)
    return (field_grad, mode_grad, skip_grad, lift_grad, proj_grad)


def np_trig(freqs, length):
    positions = np.arange(length)
    turns = positions[:, None] * (freqs[None, :] % length) % length
    angle = turns.astype(np.float32) * np.float32(2.0 * math.pi / length)
    factor = np.float32(1.0 / math.sqrt(length))
    return np.cos(angle) * factor, np.sin(angle) * factor


def np_complex(cosine, sine, sign):
    table = np.zeros((cosine.shape[0], 2, cosine.shape[1], 2), np.float32)
    table[:, 0, :, 0] = cosine
    table[:, 1, :, 0] = -sign * sine
    table[:, 1, :, 1] = cosine
    table[:, 0, :, 1] = sign * sine
    return table


def make_tables(zlen, span_y, span_x, nb, xrows, yrows):
    kzb, kyb = MZ // nb, MY // nb
    zc, zs = np_trig(np.arange(MZ), zlen)
    yc, ys = np_trig(np.arange(MY) - MY // 2, span_y)
    xc, xs = np_trig(np.arange(MX) - MX // 2, span_x)
    zpart = np.stack([zc, -zs]).reshape(2, zlen, nb, kzb)
    zf = np.einsum("pzbk,yw->yzbwpk", zpart, np.eye(yrows, dtype=np.float32))
    zf = zf.reshape(yrows * zlen, nb, yrows * 2 * kzb).transpose(1, 0, 2)
    zi = np.ascontiguousarray(zf.transpose(0, 2, 1))
    yt = np_complex(yc, ys, -1).reshape(nb, yrows, 2, nb, kyb, 2)
    eye = np.eye(kzb, dtype=np.float32)
    yf = np.einsum("bypjmq,kh->bjypkqhm", yt, eye).reshape(nb, nb, yrows * 2 * kzb, 2 * kzb * kyb)
    yi_t = np_complex(yc, ys, -1).reshape(nb, yrows, 2, nb, kyb, 2)
    yi = np.einsum("bypjmq,kh->jbqhmypk", yi_t, eye).reshape(nb, nb, 2 * kzb * kyb, yrows * 2 * kzb)
    xt = np_complex(xc, xs, -1).reshape(nb, xrows, 2, MX, 2)
    four = np.eye(4, dtype=np.float32)
    xf = np.einsum("bxplq,cd->bpcxqdl", xt, four).reshape(nb, 2, 4 * xrows, 8 * MX)
    xr = np.einsum("bxplq,cd,r->bpcxdqrl", xt, four, np.ones(4, np.float32))
    xr = xr.reshape(nb, 2, 4 * xrows, 32 * MX)
    both = np.stack([xc, xs]).reshape(2, nb, xrows, MX)
    xi = np.einsum("tbxl,r->bxtrl", both, np.ones(4, np.float32)).reshape(nb, xrows, 8 * MX)
    xd = np.einsum("tbxl,cd->bcxtdl", both, four).reshape(nb, 4 * xrows, 8 * MX)
    bf = ml_dtypes.bfloat16
    return [np.asarray(t).astype(bf) for t in (zf, zi, yf, yi, xf, xr)] + [
        xi.astype(bf).astype(np.float32),
        xd.astype(bf),
    ]


def dot(a, b):
    return lax.dot_general(a, b, (((1,), (0,)), ((), ())), preferred_element_type=jnp.float32)


def dot_nt(a, b):
    return lax.dot_general(a, b, (((1,), (1,)), ((), ())), preferred_element_type=jnp.float32)


BF = jnp.bfloat16
F32 = jnp.float32


def z_forward_kernel(rows, yrows, zlen, idx, field, zf, o0, o1, o2, o3, held, tab, wide, sem):
    first = pltpu.make_async_copy(field, held, sem.at[0])
    first.start()
    second = pltpu.make_async_copy(zf, tab, sem.at[1])
    second.start()
    first.wait()
    wide[...] = held[...].astype(F32)
    side = jnp.concatenate(
        [wide[pl.ds(y, rows, stride=yrows), :].astype(BF) for y in range(yrows)], axis=1
    )
    second.wait()
    table = jnp.concatenate([tab[idx[0] ^ s] for s in range(4)], axis=1)
    out = dot(side, table).astype(BF)
    for s, o in enumerate((o0, o1, o2, o3)):
        o[...] = out[:, s * 128 : (s + 1) * 128]


def lane_kernel(near, far, idx, r0, r1, r2, r3, table, after, o0, o1, o2, o3):
    side = jnp.concatenate([r0[...], r1[...], r2[...], r3[...]], axis=1)
    cols = []
    for t in range(4):
        cols.append(
            jnp.concatenate([table[idx[near] ^ s, idx[far] ^ t] for s in range(4)], axis=0)
        )
    out = dot(side, jnp.concatenate(cols, axis=1)).astype(BF)
    for t, o in enumerate((o0, o1, o2, o3)):
        o[...] = out[:, t * 128 : (t + 1) * 128]


def x_side(idx, refs, tab):
    parts = []
    for g in range(8):
        block = jnp.concatenate([r[g * 32 : (g + 1) * 32, :] for r in refs], axis=0)
        turned = block.astype(F32).T.astype(BF)
        parts.append(jnp.concatenate([turned[:64, :], turned[64:, :]], axis=1))
    side = jnp.concatenate(parts, axis=0)
    table = jnp.concatenate([tab[idx[1] ^ s, p] for p in range(2) for s in range(4)], axis=0)
    return side, table


def mix_forward_kernel(idx, r0, r1, r2, r3, xf, xi, early, late, modes, o0, o1, o2, o3):
    side, table = x_side(idx, (r0, r1, r2, r3), xf)
    got = dot(side, table).astype(BF)
    for g in range(8):
        modes[g, 0] = got[g * 64 : (g + 1) * 64, :128]
        modes[g, 1] = got[g * 64 : (g + 1) * 64, 128:]
    left = jnp.concatenate([xi[idx[1] ^ s] for s in range(4)], axis=0).astype(BF)
    outs = (o0, o1, o2, o3)

    def pair(k, carry):
        rows = []
        for j in range(2):
            o = 2 * k + j
            real = jnp.zeros((64, 128), F32)
            imag = jnp.zeros((64, 128), F32)
            for g in range(8):
                weight, at = (early, g) if g < EARLY else (late, g - EARLY)
                wr = weight[at, 0, o].astype(F32)
                wi = weight[at, 1, o].astype(F32)
                mr = modes[g, 0].astype(F32)
                mi = modes[g, 1].astype(F32)
                real = real + wr * mr - wi * mi
                imag = imag + wr * mi + wi * mr
            rows.append(jnp.concatenate([real.astype(BF), (-imag).astype(BF)], axis=1))
            rows.append(jnp.concatenate([imag.astype(BF), real.astype(BF)], axis=1))
        got = dot_nt(left, jnp.concatenate(rows, axis=0))
        for s in range(4):
            both = jnp.concatenate(
                [got[s * 8 : (s + 1) * 8, :128], got[s * 8 : (s + 1) * 8, 128:]], axis=0
            )
            outs[s][pl.ds(pl.multiple_of(k * 16, 16), 16), :] = both.astype(BF)
        return carry

    lax.fori_loop(0, 16, pair, 0)


def mix_backward_kernel(idx, r0, r1, r2, r3, xr, xd, early, late, pmodes, o0, o1, o2, o3):
    side, table = x_side(idx, (r0, r1, r2, r3), xr)
    for d in range(4):
        got = dot(side, table[:, d * 256 : (d + 1) * 256]).astype(BF)
        for g in range(8):
            pmodes[4 * g + d, 0] = got[g * 64 : (g + 1) * 64, :128]
            pmodes[4 * g + d, 1] = got[g * 64 : (g + 1) * 64, 128:]
    left = jnp.concatenate([xd[idx[1] ^ s] for s in range(4)], axis=0)
    outs = (o0, o1, o2, o3)

    def group(weight, first, at, carry):
        g = first + at
        real = jnp.zeros((64, 128), F32)
        imag = jnp.zeros((64, 128), F32)
        for o in range(32):
            wr = weight[at, 0, o].astype(F32)
            wi = weight[at, 1, o].astype(F32)
            pr = pmodes[o, 0].astype(F32)
            pi = pmodes[o, 1].astype(F32)
            real = real + wr * pr + wi * pi
            imag = imag + wr * pi - wi * pr
        rows = [
            jnp.concatenate([real.astype(BF), (-imag).astype(BF)], axis=1),
            jnp.concatenate([imag.astype(BF), real.astype(BF)], axis=1),
        ]
        got = dot_nt(left, jnp.concatenate(rows, axis=0)).astype(BF)
        for s in range(4):
            outs[s][pl.ds(pl.multiple_of(g * 32, 32), 32), :] = got[s * 32 : (s + 1) * 32]
        return carry

    lax.fori_loop(0, EARLY, functools.partial(group, early, 0), 0)
    lax.fori_loop(0, 8 - EARLY, functools.partial(group, late, EARLY), 0)


def pack_kernel(first, weight, after, packed, token, held, sem):
    count, half = packed.shape[0], packed.shape[2] // 2

    def copy(g, h):
        part = pl.ds(h * half, half)
        return pltpu.make_async_copy(
            weight.at[:, pl.ds(4 * (first + g), 4), part], held.at[g, :, :, part], sem.at[g, h]
        )

    for g in range(count):
        for h in range(2):
            copy(g, h).start()
    for g in range(count):
        for h in range(2):
            copy(g, h).wait()

            def step(o, carry):
                for p in range(2):
                    packed[g, p, o] = jnp.concatenate(
                        [held[g, p, k, o] for k in range(4)], axis=1
                    )
                return carry

            lax.fori_loop(h * half, (h + 1) * half, step, 0, unroll=8)
    token[...] = jnp.zeros_like(token)


def outer_kernel(start, count, modes, pmodes, *rest):
    grad, token, held, turned, sem = rest[-5:]
    half = pmodes.shape[0] // 2
    copies = []
    for g in range(count):
        for p in range(2):
            m = modes[start + g, p].astype(F32)
            for k in range(4):
                turned[k, p] = (pltpu.roll(m, (128 - 32 * k) % 128, 1) if k else m).astype(BF)
        for h in range(2):

            def step(o, carry):
                pr, pi = pmodes[o, 0], pmodes[o, 1]
                for k in range(4):
                    mr, mi = turned[k, 0], turned[k, 1]
                    held[g, 0, k, o] = (mr * pr + mi * pi)[:, :32]
                    held[g, 1, k, o] = (mr * pi - mi * pr)[:, :32]
                return carry

            lax.fori_loop(h * half, (h + 1) * half, step, 0, unroll=4)
            part = pl.ds(h * half, half)
            copies.append(
                pltpu.make_async_copy(
                    held.at[g, :, :, part],
                    grad.at[:, pl.ds(4 * (start + g), 4), part],
                    sem.at[g, h],
                )
            )
            copies[-1].start()
    for copy in copies:
        copy.wait()
    token[...] = jnp.zeros_like(token)


def gelu_pair(value):
    square = value * value
    half = 0.5 + 0.5 * jnp.tanh(value * (KAPPA + (KAPPA * CUBIC) * square))
    tail = (1.0 - half) * value * (2.0 * KAPPA + (6.0 * KAPPA * CUBIC) * square)
    return value * half, half + half * tail


def turn(value):
    return value.astype(F32).T.astype(BF)


def spread(block, count):
    rows, lanes = block.shape
    wide = jnp.concatenate([block.astype(F32)] * count, axis=1)
    tall = jnp.concatenate([wide] * count, axis=0)
    at_row = lax.broadcasted_iota(jnp.int32, tall.shape, 0) // rows
    at_lane = lax.broadcasted_iota(jnp.int32, tall.shape, 1) // lanes
    return jnp.where(at_row == at_lane, tall, 0.0).astype(BF)


def cells_kernel(field, cotangent, skip, lift_t, proj, fx, cx, dskip, dskip_t, dlift, dlift_t, dproj, wide):
    for src, dst in ((field, fx), (cotangent, cx)):
        wide[...] = src[...].astype(F32)

        def step(k, carry):
            parts = []
            for sub in range(8):
                first = 16 * k + 2 * sub
                parts.append(
                    jnp.concatenate(
                        [wide[pl.ds(first + j, 32, stride=64), :] for j in range(2)], axis=1
                    ).astype(BF)
                )
            dst[k] = jnp.concatenate(parts, axis=0)
            return carry

        lax.fori_loop(0, 4, step, 0)
    dskip[...] = spread(skip[...], 8)
    dskip_t[...] = spread(turn(skip[...]), 8)
    dlift[...] = spread(turn(lift_t[...]), 8)
    dlift_t[...] = spread(lift_t[...], 2)
    dproj[...] = spread(turn(proj[...]), 8)


def inverse_z(idx, refs, zi, spectral):
    side = jnp.concatenate([r[...] for r in refs], axis=1)
    back = jnp.concatenate([zi[idx[0] ^ s] for s in range(4)], axis=0)
    for y in range(4):
        got = dot(side, back[:, y * 256 : (y + 1) * 256])
        spectral[2 * y] = got[:, :128]
        spectral[2 * y + 1] = got[:, 128:]


def cell_rows(spectral, k):
    parts = []
    for sub in range(8):
        rows = pl.ds(2 * k + sub // 4, 32, stride=8)
        parts.append(
            jnp.concatenate([spectral[2 * (sub % 4) + j, rows, :] for j in range(2)], axis=1)
        )
    return jnp.concatenate(parts, axis=0)


def point_kernel(
    idx, r0, r1, r2, r3, zi, zf, fx, cx, dskip, dlift, dlift_t, dproj,
    o0, o1, o2, o3, pg, act, hid, lif, spectral, wide,
):
    inverse_z(idx, (r0, r1, r2, r3), zi, spectral)

    def step(k, carry):
        values, grads = fx[k], cx[k]
        pre = cell_rows(spectral, k) + dot(dskip[...], values)
        lifted, slope_pre = gelu_pair(pre)
        lifted = lifted.astype(BF)
        lif[k] = lifted
        hidden = dot(dlift[...], lifted)
        backed = dot(dproj[...], grads)
        up = []
        for q in range(4):
            part = slice(q * 256, (q + 1) * 256)
            activated, slope_hid = gelu_pair(hidden[part])
            hidden_grad = (backed[part] * slope_hid).astype(BF)
            act[k, part] = activated.astype(BF)
            hid[k, part] = hidden_grad
            up.append(dot(dlift_t[...], hidden_grad))
        pre_grad = (grads.astype(F32) + jnp.concatenate(up, axis=0)) * slope_pre
        pg[k] = pre_grad.astype(BF)
        for sub in range(8):
            rows = pl.ds(2 * k + sub // 4, 32, stride=8)
            for j in range(2):
                wide[2 * (sub % 4) + j, rows, :] = pre_grad[
                    sub * 32 : (sub + 1) * 32, j * 128 : (j + 1) * 128
                ]
        return carry

    lax.fori_loop(0, 4, step, 0, unroll=2)
    table = jnp.concatenate([zf[idx[0] ^ s] for s in range(4)], axis=1)
    side = jnp.concatenate([wide[y].astype(BF) for y in range(8)], axis=1)
    out = dot(side, table).astype(BF)
    for s, o in enumerate((o0, o1, o2, o3)):
        o[...] = out[:, s * 128 : (s + 1) * 128]


def sums_kernel(fx, cx, pg, act, hid, lif, sums):
    def step(k, carry):
        proj, lift, skip = carry
        for sub in range(8):
            c = slice(sub * 32, (sub + 1) * 32)
            h = slice(sub * 128, (sub + 1) * 128)
            proj = proj + dot_nt(cx[k, c], act[k, h])
            lift = lift + dot_nt(lif[k, c], hid[k, h])
            skip = skip + dot_nt(pg[k, c], fx[k, c])
        return proj, lift, skip

    zero = jnp.zeros((32, 128), F32)
    got = lax.fori_loop(0, 4, step, (zero, zero, jnp.zeros((32, 32), F32)))
    sums[0:32] = got[0]
    sums[32:64] = got[1]
    sums[64:96] = jnp.concatenate([got[2]] * 4, axis=1)


def finish_kernel(idx, r0, r1, r2, r3, zi, pg, dskip_t, out, spectral, wide):
    inverse_z(idx, (r0, r1, r2, r3), zi, spectral)

    def step(k, carry):
        got = cell_rows(spectral, k) + dot(dskip_t[...], pg[k])
        for sub in range(8):
            first = 16 * k + 2 * sub
            for j in range(2):
                wide[pl.ds(first + j, 32, stride=64), :] = got[
                    sub * 32 : (sub + 1) * 32, j * 128 : (j + 1) * 128
                ]
        return carry

    lax.fori_loop(0, 4, step, 0, unroll=2)
    out[...] = wide[...].astype(BF)


EARLY = 3
VM = pl.BlockSpec(memory_space=pltpu.VMEM)
ANY = pl.BlockSpec(memory_space=pl.ANY)
HBM = pl.BlockSpec(memory_space=pltpu.HBM)
SM = pl.BlockSpec(memory_space=pltpu.SMEM)
BLOCK = jax.ShapeDtypeStruct((256, 128), BF)
MIB = 1024 * 1024


def cost(us):
    return pl.CostEstimate(flops=0, bytes_accessed=int(us * 3.0e6), transcendentals=0)


def call(kernel, ins, outs, scratch=(), name=None, mib=8, us=1.0, smem=1, free=0, hbm=()):
    specs = [SM] * smem + [VM] * (len(ins) - smem - free) + [ANY] * free
    for at in hbm:
        specs[at] = HBM
    return pl.pallas_call(
        kernel,
        out_shape=outs,
        in_specs=specs,
        out_specs=jax.tree.map(lambda _: VM, outs),
        scratch_shapes=list(scratch),
        compiler_params=pltpu.CompilerParams(vmem_limit_bytes=mib * MIB),
        cost_estimate=cost(us),
        name=name,
    )(*ins)


TOKEN = jax.ShapeDtypeStruct((8, 128), F32)


def pack(weight, first, count, after, us):
    chans = weight.shape[1]
    return pl.pallas_call(
        functools.partial(pack_kernel, first),
        out_shape=[jax.ShapeDtypeStruct((count, 2, chans, 64, 128), BF), TOKEN],
        in_specs=[ANY, ANY],
        out_specs=[VM, VM],
        scratch_shapes=[
            pltpu.VMEM((count, 2, 4, chans, 64, 32), BF),
            pltpu.SemaphoreType.DMA((count, 2)),
        ],
        compiler_params=pltpu.CompilerParams(vmem_limit_bytes=36 * MIB),
        cost_estimate=cost(us),
        name="pack",
    )(weight, after)


def outer(modes, pmodes, first, count, so_far, after, us):
    chans = pmodes.shape[0]
    extra = [] if so_far is None else [so_far, after]
    return pl.pallas_call(
        functools.partial(outer_kernel, first, count),
        out_shape=[jax.ShapeDtypeStruct((2, chans, chans, 64, 32), BF), TOKEN],
        in_specs=[VM, VM] + [ANY] * len(extra),
        out_specs=[ANY, VM],
        scratch_shapes=[
            pltpu.VMEM((count, 2, 4, chans, 64, 32), BF),
            pltpu.VMEM((4, 2, 64, 128), BF),
            pltpu.SemaphoreType.DMA((count, 2)),
        ],
        input_output_aliases={} if so_far is None else {2: 0},
        compiler_params=pltpu.CompilerParams(vmem_limit_bytes=24 * MIB),
        cost_estimate=cost(us),
        name="outer",
    )(modes, pmodes, *extra)


def exchange(blocks, axes):
    pairs = [[(a, a ^ s) for a in range(4)] for s in range(4)]
    got = {s: lax.ppermute(blocks[s], axes, pairs[s]) for s in (2, 3, 1)}
    return [blocks[0], got[1], got[2], got[3]]


def sum_over(part, axes):
    for axis, size in axes:
        step = 1
        while step < size:
            part = part + lax.ppermute(part, axis, [(a, a ^ step) for a in range(size)])
            step *= 2
    return part


def fast(field, cotangent, mode_weight, skip_weight, lift_weight, proj_weight):
    chans, xrows, yrows, zlen = field.shape
    tables = make_tables(zlen, yrows * 4, xrows * 4, 4, xrows, yrows)
    zf, zi, yf, yi, xf, xr, xi, xd = [jnp.asarray(t) for t in tables]
    gyc = ("gy", "col")
    idx = jnp.stack([lax.axis_index(gyc), lax.axis_index("gx")]).astype(jnp.int32)
    four = [BLOCK] * 4
    cells = chans * xrows * yrows
    flat_field = field.reshape(cells, zlen)
    flat_cot = cotangent.reshape(cells, zlen)
    rows = chans * xrows
    wide = pltpu.VMEM((cells, zlen), F32)
    tall = pltpu.VMEM((yrows, rows, zlen), F32)
    weight = mode_weight.reshape(2, chans, chans, 64, 32)
    lift_t = lift_weight.T

    def bf(*shape):
        return jax.ShapeDtypeStruct(shape, BF)

    def lanes(near, far, got, table, after, name):
        return call(
            functools.partial(lane_kernel, near, far),
            (idx, *got, table, after), four, (), name, 4, 1.0, free=1,
        )

    sent = call(
        functools.partial(z_forward_kernel, rows, yrows, zlen),
        (idx, flat_field, zf), four,
        [
            pltpu.VMEM((cells, zlen), BF),
            pltpu.VMEM(zf.shape, BF),
            wide,
            pltpu.SemaphoreType.DMA((2,)),
        ],
        "z_forward", 8, 2.0, hbm=(1, 2),
    )
    got = exchange(sent, gyc)
    early, token = pack(weight, 0, EARLY, sent[0], 4.0)
    sent = lanes(0, 1, got, yf, token, "y_forward")
    got = exchange(sent, "gx")
    late, _ = pack(weight, EARLY, 8 - EARLY, sent[0], 8.0)
    modes, *sent = call(
        mix_forward_kernel, (idx, *got, xf, xi, early, late),
        [bf(8, 2, 64, 128)] + four, (), "mix_forward", 12, 5.0,
    )
    got = exchange(sent, "gx")
    fx, cx, dskip, dskip_t, dlift, dlift_t, dproj = call(
        cells_kernel,
        (flat_field, flat_cot, skip_weight, lift_t, proj_weight),
        [bf(4, 256, 256)] * 2
        + [bf(256, 256), bf(256, 256), bf(1024, 256), bf(64, 256), bf(1024, 256)],
        [wide], "cells", 8, 3.0, 0,
    )
    sent = lanes(1, 0, got, yi, fx, "y_inverse")
    got = exchange(sent, gyc)
    *sent, pg, act, hid, lif = call(
        point_kernel,
        (idx, *got, zi, zf, fx, cx, dskip, dlift, dlift_t, dproj),
        four + [bf(4, 256, 256), bf(4, 1024, 256), bf(4, 1024, 256), bf(4, 256, 256)],
        [tall, tall], "point", 16, 8.0,
    )
    got = exchange(sent, gyc)
    part = call(
        sums_kernel, (fx, cx, pg, act, hid, lif),
        jax.ShapeDtypeStruct((96, 128), F32), (), "sums", 4, 2.5, 0,
    )
    sent = lanes(0, 1, got, yf, part, "y_forward")
    got = exchange(sent, "gx")
    pmodes, *sent = call(
        mix_backward_kernel, (idx, *got, xr, xd, early, late),
        [bf(32, 2, 64, 128)] + four, (), "mix_backward", 12, 5.0,
    )
    got = exchange(sent, "gx")
    grad, token = outer(modes, pmodes, 0, 4, None, None, 6.0)
    sent = lanes(1, 0, got, yi, token, "y_inverse")
    got = exchange(sent, gyc)
    mode_grad, _ = outer(modes, pmodes, 4, 4, grad, sent[0], 6.0)
    field_grad = call(
        finish_kernel, (idx, *got, zi, pg, dskip_t),
        bf(cells, zlen), [tall, wide], "finish", 8, 2.0,
    )
    part = sum_over(part, (("col", 2), ("gy", 2), ("gx", 4)))
    return (
        field_grad.reshape(field.shape),
        mode_grad.reshape(mode_weight.shape),
        part[64:, :chans],
        part[32:64].T,
        part[:32],
    )


def fits(field, mode_weight):
    sizes = [lax.axis_size(a) for a in ("gx", "gy", "col")]
    return (
        sizes == [4, 2, 2]
        and field.shape == (32, 8, 8, 128)
        and mode_weight.shape == (2, 32, 32, 8, 8, 32)
    )


def on_device(*args):
    return fast(*args) if fits(args[0], args[2]) else general(*args)


def solution(mesh):
    in_specs = (
        P("grp", "gx", ("gy", "col"), None),
        P("grp", "gx", ("gy", "col"), None),
        P(None, None, None, ("gy", "col"), "gx", None),
        P(),
        P(),
        P(),
    )
    out_specs = (
        P("grp", "gx", ("gy", "col"), None),
        P("grp", None, None, ("gy", "col"), "gx", None),
        P("grp", None),
        P("grp", None),
        P("grp", None),
    )
    return jax.shard_map(
        on_device, mesh=mesh, in_specs=in_specs, out_specs=out_specs, check_vma=False
    )
```

```python
import functools
import math

import jax
import jax.numpy as jnp
import ml_dtypes
import numpy as np
from jax import lax
from jax.experimental import pallas as pl
from jax.experimental.pallas import tpu as pltpu
from jax.sharding import PartitionSpec as P

MX = 32
MY = 32
MZ = 32


KAPPA = 0.7978845608028654
CUBIC = 0.044715


def gelu_slope(value):
    inner = KAPPA * (value + CUBIC * value * value * value)
    tangent = jnp.tanh(inner)
    result = 0.5 * value * (1.0 + tangent)
    slope = 0.5 * (1.0 + tangent) + 0.5 * value * (1.0 - tangent * tangent) * KAPPA * (
        1.0 + 3.0 * CUBIC * value * value
    )
    return (result, slope)


def trig_pair(freqs, length):
    positions = jnp.arange(length, dtype=jnp.int32)
    turns = positions[:, None] * (freqs[None, :] % length) % length
    angle = turns.astype(jnp.float32) * (2.0 * math.pi / length)
    factor = 1.0 / math.sqrt(length)
    return (jnp.cos(angle) * factor, jnp.sin(angle) * factor)


def real_table(freqs, length):
    cosine, sine = trig_pair(freqs, length)
    return jnp.stack([cosine.T, -sine.T]).astype(jnp.bfloat16)


def complex_table(freqs, length):
    cosine, sine = trig_pair(freqs, length)
    upper = jnp.stack([cosine, -sine], axis=1)
    lower = jnp.stack([sine, cosine], axis=1)
    return jnp.stack([upper, lower]).astype(jnp.bfloat16)


def centered(count):
    return jnp.arange(count, dtype=jnp.int32) - count // 2


def to_modes(values, tables):
    z_table, y_table, x_table = tables
    chans, xrows, yrows, zlen = values.shape
    first = jnp.einsum("cxyn,qkn->qkycx", values, z_table, preferred_element_type=jnp.float32)
    first = first.astype(jnp.bfloat16).reshape(2, MZ, yrows, chans * xrows)
    moved = lax.all_to_all(first, ("gy", "col"), split_axis=1, concat_axis=2, tiled=True)
    second = jnp.einsum("pkyr,pyqj->qkjr", moved, y_table, preferred_element_type=jnp.float32)
    second = second.astype(jnp.bfloat16)[:, :, :, None, :]
    crossed = lax.all_to_all(second, "gx", split_axis=2, concat_axis=3, tiled=True)
    crossed = crossed.reshape(crossed.shape[:4] + (chans, xrows))
    third = jnp.einsum("pkjgcx,pgxql->qckjl", crossed, x_table, preferred_element_type=jnp.float32)
    return third.astype(jnp.bfloat16).reshape(2, chans, -1)


def to_grid(spec, tables, shape, local_modes):
    z_table, y_table, x_table = tables
    chans, xrows, yrows, zlen = shape
    spec = spec.reshape((2, chans) + local_modes)
    first = jnp.einsum("pckjl,qgxpl->qkjgcx", spec, x_table, preferred_element_type=jnp.float32)
    first = first.astype(jnp.bfloat16)
    first = first.reshape(first.shape[:4] + (chans * xrows,))
    joined = lax.all_to_all(first, "gx", split_axis=3, concat_axis=2, tiled=True)
    joined = joined.reshape(joined.shape[:3] + (chans * xrows,))
    second = jnp.einsum("pkjr,qypj->qkyr", joined, y_table, preferred_element_type=jnp.float32)
    second = second.astype(jnp.bfloat16)
    returned = lax.all_to_all(second, ("gy", "col"), split_axis=2, concat_axis=1, tiled=True)
    grid = jnp.einsum("pkyr,pkn->ryn", returned, z_table, preferred_element_type=jnp.float32)
    return grid.reshape(chans, xrows, yrows, zlen)


def mix(weight, modes):
    real = jnp.einsum("iok,ik->ok", weight[0], modes[0], preferred_element_type=jnp.float32)
    real = real - jnp.einsum("iok,ik->ok", weight[1], modes[1], preferred_element_type=jnp.float32)
    imag = jnp.einsum("iok,ik->ok", weight[0], modes[1], preferred_element_type=jnp.float32)
    imag = imag + jnp.einsum("iok,ik->ok", weight[1], modes[0], preferred_element_type=jnp.float32)
    return jnp.stack([real, imag]).astype(jnp.bfloat16)


def general(field, cotangent, mode_weight, skip_weight, lift_weight, proj_weight):
    chans, xrows, yrows, zlen = field.shape
    groups_x = lax.axis_size("gx")
    groups_y = lax.axis_size("gy")
    groups_c = lax.axis_size("col")
    span_x = xrows * groups_x
    span_y = yrows * groups_y * groups_c
    column = jnp.arange(MZ, dtype=jnp.int32)
    z_table = real_table(column, zlen)
    y_table = complex_table(centered(MY), span_y)
    x_table = complex_table(centered(MX), span_x).reshape(2, groups_x, xrows, 2, MX)
    tables = (z_table, y_table, x_table)
    local_modes = (mode_weight.shape[3], mode_weight.shape[4], mode_weight.shape[5])
    weight_flat = mode_weight.reshape(2, chans, chans, -1)
    modes = to_modes(field, tables)
    spectral = to_grid(mix(weight_flat, modes), tables, field.shape, local_modes).reshape(chans, -1)
    flat_field = field.reshape(chans, -1)
    flat_grad = cotangent.reshape(chans, -1)
    pre = spectral + jnp.dot(skip_weight, flat_field, preferred_element_type=jnp.float32)
    lifted, slope_pre = gelu_slope(pre)
    lifted = lifted.astype(jnp.bfloat16)
    hidden = jnp.dot(lift_weight, lifted, preferred_element_type=jnp.float32)
    activated, slope_hid = gelu_slope(hidden)
    activated = activated.astype(jnp.bfloat16)
    back_hidden = jnp.dot(proj_weight.T, flat_grad, preferred_element_type=jnp.float32)
    hidden_grad = (back_hidden * slope_hid).astype(jnp.bfloat16)
    grad_up = flat_grad.astype(jnp.float32) + jnp.dot(
        lift_weight.T, hidden_grad, preferred_element_type=jnp.float32
    )
    pre_grad = (grad_up * slope_pre).astype(jnp.bfloat16)
    proj_part = jnp.einsum("cr,hr->ch", flat_grad, activated, preferred_element_type=jnp.float32)
    lift_part = jnp.einsum("hr,cr->hc", hidden_grad, lifted, preferred_element_type=jnp.float32)
    skip_part = jnp.einsum("or,ir->oi", pre_grad, flat_field, preferred_element_type=jnp.float32)
    proj_grad, lift_grad, skip_grad = lax.psum(
        (proj_part, lift_part, skip_part), ("gx", "gy", "col")
    )
    pre_modes = to_modes(pre_grad.reshape(field.shape), tables)
    grad_real = jnp.einsum("ik,ok->iok", modes[0], pre_modes[0], preferred_element_type=jnp.float32)
    grad_real = grad_real + jnp.einsum(
        "ik,ok->iok", modes[1], pre_modes[1], preferred_element_type=jnp.float32
    )
    grad_imag = jnp.einsum("ik,ok->iok", modes[0], pre_modes[1], preferred_element_type=jnp.float32)
    grad_imag = grad_imag - jnp.einsum(
        "ik,ok->iok", modes[1], pre_modes[0], preferred_element_type=jnp.float32
    )
    mode_grad = jnp.stack([grad_real, grad_imag]).astype(jnp.bfloat16).reshape(mode_weight.shape)
    back_real = jnp.einsum(
        "iok,ok->ik", weight_flat[0], pre_modes[0], preferred_element_type=jnp.float32
    )
    back_real = back_real + jnp.einsum(
        "iok,ok->ik", weight_flat[1], pre_modes[1], preferred_element_type=jnp.float32
    )
    back_imag = jnp.einsum(
        "iok,ok->ik", weight_flat[0], pre_modes[1], preferred_element_type=jnp.float32
    )
    back_imag = back_imag - jnp.einsum(
        "iok,ok->ik", weight_flat[1], pre_modes[0], preferred_element_type=jnp.float32
    )
    modes_grad = jnp.stack([back_real, back_imag]).astype(jnp.bfloat16)
    spectral_grad = to_grid(modes_grad, tables, field.shape, local_modes).reshape(chans, -1)
    skip_back = jnp.dot(skip_weight.T, pre_grad, preferred_element_type=jnp.float32)
    field_grad = (spectral_grad + skip_back).astype(jnp.bfloat16).reshape(field.shape)
    return (field_grad, mode_grad, skip_grad, lift_grad, proj_grad)


def np_trig(freqs, length):
    positions = np.arange(length)
    turns = positions[:, None] * (freqs[None, :] % length) % length
    angle = turns.astype(np.float32) * np.float32(2.0 * math.pi / length)
    factor = np.float32(1.0 / math.sqrt(length))
    return np.cos(angle) * factor, np.sin(angle) * factor


def np_complex(cosine, sine, sign):
    table = np.zeros((cosine.shape[0], 2, cosine.shape[1], 2), np.float32)
    table[:, 0, :, 0] = cosine
    table[:, 1, :, 0] = -sign * sine
    table[:, 1, :, 1] = cosine
    table[:, 0, :, 1] = sign * sine
    return table


def make_tables(zlen, span_y, span_x, nb, xrows, yrows):
    kzb, kyb = MZ // nb, MY // nb
    zc, zs = np_trig(np.arange(MZ), zlen)
    yc, ys = np_trig(np.arange(MY) - MY // 2, span_y)
    xc, xs = np_trig(np.arange(MX) - MX // 2, span_x)
    zpart = np.stack([zc, -zs]).reshape(2, zlen, nb, kzb)
    zf = np.einsum("pzbk,yw->yzbwpk", zpart, np.eye(yrows, dtype=np.float32))
    zf = zf.reshape(yrows * zlen, nb, yrows * 2 * kzb).transpose(1, 0, 2)
    zi = np.ascontiguousarray(zf.transpose(0, 2, 1))
    yt = np_complex(yc, ys, -1).reshape(nb, yrows, 2, nb, kyb, 2)
    eye = np.eye(kzb, dtype=np.float32)
    yf = np.einsum("bypjmq,kh->bjypkqhm", yt, eye).reshape(nb, nb, yrows * 2 * kzb, 2 * kzb * kyb)
    yi_t = np_complex(yc, ys, -1).reshape(nb, yrows, 2, nb, kyb, 2)
    yi = np.einsum("bypjmq,kh->jbqhmypk", yi_t, eye).reshape(nb, nb, 2 * kzb * kyb, yrows * 2 * kzb)
    xt = np_complex(xc, xs, -1).reshape(nb, xrows, 2, MX, 2)
    four = np.eye(4, dtype=np.float32)
    xf = np.einsum("bxplq,cd->bpcxqdl", xt, four).reshape(nb, 2, 4 * xrows, 8 * MX)
    xr = np.einsum("bxplq,cd,r->bpcxdqrl", xt, four, np.ones(4, np.float32))
    xr = xr.reshape(nb, 2, 4 * xrows, 32 * MX)
    both = np.stack([xc, xs]).reshape(2, nb, xrows, MX)
    xi = np.einsum("tbxl,r->bxtrl", both, np.ones(4, np.float32)).reshape(nb, xrows, 8 * MX)
    xd = np.einsum("tbxl,cd->bcxtdl", both, four).reshape(nb, 4 * xrows, 8 * MX)
    bf = ml_dtypes.bfloat16
    return [np.asarray(t).astype(bf) for t in (zf, zi, yf, yi, xf, xr)] + [
        xi.astype(bf).astype(np.float32),
        xd.astype(bf),
    ]


def dot(a, b):
    return lax.dot_general(a, b, (((1,), (0,)), ((), ())), preferred_element_type=jnp.float32)


def dot_nt(a, b):
    return lax.dot_general(a, b, (((1,), (1,)), ((), ())), preferred_element_type=jnp.float32)


BF = jnp.bfloat16
F32 = jnp.float32
STEPS = (0, 2, 3, 1)


def z_forward_kernel(rows, yrows, zlen, idx, field, zf, o0, o1, o2, o3, held, tab, wide, sem):
    first = pltpu.make_async_copy(field, held, sem.at[0])
    first.start()
    second = pltpu.make_async_copy(zf, tab, sem.at[1])
    second.start()
    first.wait()
    wide[...] = held[...].astype(F32)
    side = jnp.concatenate(
        [wide[pl.ds(y, rows, stride=yrows), :].astype(BF) for y in range(yrows)], axis=1
    )
    second.wait()
    table = jnp.concatenate([tab[idx[0] ^ STEPS[s]] for s in range(4)], axis=1)
    out = dot(side, table).astype(BF)
    for s, o in enumerate((o0, o1, o2, o3)):
        o[...] = out[:, s * 128 : (s + 1) * 128]


def lane_kernel(idx, r0, r1, r2, r3, table, after, o0, o1, o2, o3):
    side = jnp.concatenate([r0[...], r1[...], r2[...], r3[...]], axis=1)
    known = table[...] if len(table.shape) == 2 else lane_table(idx, 0, 1, table)
    out = dot(side, known).astype(BF)
    for t, o in enumerate((o0, o1, o2, o3)):
        o[...] = out[:, t * 128 : (t + 1) * 128]


def x_side(idx, refs, tab):
    parts = []
    for g in range(8):
        block = jnp.concatenate([r[g * 32 : (g + 1) * 32, :] for r in refs], axis=0)
        turned = block.astype(F32).T.astype(BF)
        parts.append(jnp.concatenate([turned[:64, :], turned[64:, :]], axis=1))
    side = jnp.concatenate(parts, axis=0)
    table = jnp.concatenate([tab[idx[1] ^ STEPS[s], p] for p in range(2) for s in range(4)], axis=0)
    return side, table


def add_products(total, weight, modes, o, first):
    real, imag = total
    for g in range(weight.shape[0]):
        wr, wi = weight[g, 0, o].astype(F32), weight[g, 1, o].astype(F32)
        mr, mi = modes[first + g, 0].astype(F32), modes[first + g, 1].astype(F32)
        real = real + wr * mr - wi * mi
        imag = imag + wr * mi + wi * mr
    return real, imag


def mix_forward_kernel(
    idx, r0, r1, r2, r3, xf, xi, early, late, weight, modes, o0, o1, o2, o3, last,
    total, held, sem,
):
    known = early.shape[0] + late.shape[0]
    copies = pack_copies(known, weight, held, sem)
    side, table = x_side(idx, (r0, r1, r2, r3), xf)
    got = dot(side, table).astype(BF)
    for g in range(8):
        for p in range(2):
            part = got[g * 64 : (g + 1) * 64, p * 128 : (p + 1) * 128]
            modes[g, p] = part
    left = jnp.concatenate([xi[idx[1] ^ STEPS[s]] for s in range(4)], axis=0).astype(BF)
    outs = (o0, o1, o2, o3)
    zero = jnp.zeros((64, 128), F32)

    def begin(o, carry):
        got = add_products((zero, zero), early, modes, o, 0)
        total[o, 0], total[o, 1] = add_products(got, late, modes, o, early.shape[0])
        return carry

    lax.fori_loop(0, 32, begin, 0, unroll=2)
    pack_finish(copies, held, last)

    def pair(k, carry):
        rows = []
        for j in range(2):
            o = 2 * k + j
            real, imag = add_products((total[o, 0], total[o, 1]), last, modes, o, known)
            rows.append(jnp.concatenate([real.astype(BF), (-imag).astype(BF)], axis=1))
            rows.append(jnp.concatenate([imag.astype(BF), real.astype(BF)], axis=1))
        got = dot_nt(left, jnp.concatenate(rows, axis=0))
        for s in range(4):
            both = jnp.concatenate(
                [got[s * 8 : (s + 1) * 8, :128], got[s * 8 : (s + 1) * 8, 128:]], axis=0
            )
            outs[s][pl.ds(pl.multiple_of(k * 16, 16), 16), :] = both.astype(BF)
        return carry

    lax.fori_loop(0, 16, pair, 0, unroll=2)


def mix_backward_kernel(
    idx, r0, r1, r2, r3, xr, xd, early, late, last, pmodes, o0, o1, o2, o3
):
    side, table = x_side(idx, (r0, r1, r2, r3), xr)
    for d in range(4):
        got = dot(side, table[:, d * 256 : (d + 1) * 256]).astype(BF)
        for g in range(8):
            for p in range(2):
                part = got[g * 64 : (g + 1) * 64, p * 128 : (p + 1) * 128]
                pmodes[4 * g + d, p] = part
    left = jnp.concatenate([xd[idx[1] ^ STEPS[s]] for s in range(4)], axis=0)
    outs = (o0, o1, o2, o3)

    def group(weight, first, at, carry):
        g = first + at
        real = jnp.zeros((64, 128), F32)
        imag = jnp.zeros((64, 128), F32)
        for o in range(32):
            wr, wi = weight[at, 0, o].astype(F32), weight[at, 1, o].astype(F32)
            pr, pi = pmodes[o, 0].astype(F32), pmodes[o, 1].astype(F32)
            real = real + wr * pr + wi * pi
            imag = imag + wr * pi - wi * pr
        rows = [
            jnp.concatenate([real.astype(BF), (-imag).astype(BF)], axis=1),
            jnp.concatenate([imag.astype(BF), real.astype(BF)], axis=1),
        ]
        got = dot_nt(left, jnp.concatenate(rows, axis=0)).astype(BF)
        for s in range(4):
            outs[s][pl.ds(pl.multiple_of(g * 32, 32), 32), :] = got[s * 32 : (s + 1) * 32]
        return carry

    first = 0
    for weight in (early, late, last):
        lax.fori_loop(0, weight.shape[0], functools.partial(group, weight, first), 0)
        first += weight.shape[0]


def pack_copies(first, weight, held, sem):
    span = held.shape[3] // 4
    copies = []
    for g in range(held.shape[0]):
        for h in range(4):
            part = pl.ds(h * span, span)
            copies.append(
                pltpu.make_async_copy(
                    weight.at[:, pl.ds(4 * (first + g), 4), part],
                    held.at[g, :, :, part],
                    sem.at[g, h],
                )
            )
            copies[-1].start()
    return copies


def pack_finish(copies, held, packed):
    span = held.shape[3] // 4
    for g in range(held.shape[0]):
        for h in range(4):
            copies[4 * g + h].wait()

            def step(o, carry):
                for p in range(2):
                    packed[g, p, o] = jnp.concatenate(
                        [held[g, p, k, o] for k in range(4)], axis=1
                    )
                return carry

            lax.fori_loop(h * span, (h + 1) * span, step, 0, unroll=8)


def pack_kernel(first, weight, after, packed, token, held, sem):
    pack_finish(pack_copies(first, weight, held, sem), held, packed)
    token[...] = jnp.zeros_like(token)


def outer_start(start, modes, pmodes, grad, held, turned, sem):
    span = pmodes.shape[0] // 4
    copies = []
    for g in range(held.shape[0]):
        for p in range(2):
            m = modes[start + g, p].astype(F32)
            for k in range(4):
                turned[k, p] = (pltpu.roll(m, (128 - 32 * k) % 128, 1) if k else m).astype(BF)
        for h in range(4):

            def step(o, carry):
                pr, pi = pmodes[o, 0], pmodes[o, 1]
                for k in range(4):
                    mr, mi = turned[k, 0], turned[k, 1]
                    held[g, 0, k, o] = (mr * pr + mi * pi)[:, :32]
                    held[g, 1, k, o] = (mr * pi - mi * pr)[:, :32]
                return carry

            lax.fori_loop(h * span, (h + 1) * span, step, 0, unroll=8)
            part = pl.ds(h * span, span)
            copies.append(
                pltpu.make_async_copy(
                    held.at[g, :, :, part],
                    grad.at[:, pl.ds(4 * (start + g), 4), part],
                    sem.at[g, h],
                )
            )
            copies[-1].start()
    return copies


def outer_scratch(count, chans):
    return [
        pltpu.VMEM((count, 2, 4, chans, 64, 32), BF),
        pltpu.VMEM((4, 2, 64, 128), BF),
        pltpu.SemaphoreType.DMA((count, 4)),
    ]


def outer_kernel(start, modes, pmodes, *rest):
    grad, token, held, turned, sem = rest[-5:]
    for copy in outer_start(start, modes, pmodes, grad, held, turned, sem):
        copy.wait()
    token[...] = jnp.zeros_like(token)


def gelu_pair(value):
    square = value * value
    half = 0.5 + 0.5 * jnp.tanh(value * (KAPPA + (KAPPA * CUBIC) * square))
    tail = (1.0 - half) * value * (2.0 * KAPPA + (6.0 * KAPPA * CUBIC) * square)
    return value * half, half + half * tail


def turn(value):
    return value.astype(F32).T.astype(BF)


def spread(block, count):
    rows, lanes = block.shape
    wide = jnp.concatenate([block.astype(F32)] * count, axis=1)
    tall = jnp.concatenate([wide] * count, axis=0)
    at_row = lax.broadcasted_iota(jnp.int32, tall.shape, 0) // rows
    at_lane = lax.broadcasted_iota(jnp.int32, tall.shape, 1) // lanes
    return jnp.where(at_row == at_lane, tall, 0.0).astype(BF)


def by_step(idx, at, table, axis):
    return jnp.concatenate([table[idx[at] ^ STEPS[s]] for s in range(4)], axis=axis)


def lane_table(idx, near, far, table):
    cols = []
    for t in range(4):
        rows = [table[idx[near] ^ STEPS[s], idx[far] ^ STEPS[t]] for s in range(4)]
        cols.append(jnp.concatenate(rows, axis=0))
    return jnp.concatenate(cols, axis=1)


def cells_kernel(
    idx, field, cotangent, skip, lift_t, proj, zf, zi, yf, yi,
    fx, cx, skipped, backed, dskip_t, dlift, dlift_t, zfp, zip_, yfp, yip, wide,
):
    for src, dst in ((field, fx), (cotangent, cx)):
        wide[...] = src[...].astype(F32)

        def step(k, carry):
            parts = []
            for sub in range(8):
                first = 16 * k + 2 * sub
                parts.append(
                    jnp.concatenate(
                        [wide[pl.ds(first + j, 32, stride=64), :] for j in range(2)], axis=1
                    ).astype(BF)
                )
            dst[k] = jnp.concatenate(parts, axis=0)
            return carry

        lax.fori_loop(0, 4, step, 0)
    dskip = spread(skip[...], 8)
    dproj = spread(turn(proj[...]), 8)
    for k in range(4):
        skipped[k] = dot(dskip, fx[k])
        backed[k] = dot(dproj, cx[k])
    zfp[...] = by_step(idx, 0, zf, 1)
    zip_[...] = by_step(idx, 0, zi, 0)
    yfp[...] = lane_table(idx, 0, 1, yf)
    yip[...] = lane_table(idx, 1, 0, yi)
    dskip_t[...] = spread(turn(skip[...]), 8)
    dlift[...] = spread(turn(lift_t[...]), 8)
    dlift_t[...] = spread(lift_t[...], 2)


def inverse_z(refs, back, spectral):
    side = jnp.concatenate([r[...] for r in refs], axis=1)
    for y in range(4):
        got = dot(side, back[:, y * 256 : (y + 1) * 256])
        spectral[2 * y] = got[:, :128]
        spectral[2 * y + 1] = got[:, 128:]


def cell_rows(spectral, k):
    parts = []
    for sub in range(8):
        rows = pl.ds(2 * k + sub // 4, 32, stride=8)
        parts.append(
            jnp.concatenate([spectral[2 * (sub % 4) + j, rows, :] for j in range(2)], axis=1)
        )
    return jnp.concatenate(parts, axis=0)


def point_kernel(
    r0, r1, r2, r3, back, table, cx, skipped, backed, dlift, dlift_t,
    o0, o1, o2, o3, pg, act, hid, lif, spectral, wide,
):
    inverse_z((r0, r1, r2, r3), back, spectral)

    def step(k, carry):
        grads = cx[k]
        pre = cell_rows(spectral, k) + skipped[k]
        lifted, slope_pre = gelu_pair(pre)
        lifted = lifted.astype(BF)
        lif[k] = lifted
        hidden = dot(dlift[...], lifted)
        up = []
        for q in range(4):
            part = slice(q * 256, (q + 1) * 256)
            activated, slope_hid = gelu_pair(hidden[part])
            hidden_grad = (backed[k, part] * slope_hid).astype(BF)
            act[k, part] = activated.astype(BF)
            hid[k, part] = hidden_grad
            up.append(dot(dlift_t[...], hidden_grad))
        pre_grad = (grads.astype(F32) + jnp.concatenate(up, axis=0)) * slope_pre
        pg[k] = pre_grad.astype(BF)
        for sub in range(8):
            rows = pl.ds(2 * k + sub // 4, 32, stride=8)
            for j in range(2):
                wide[2 * (sub % 4) + j, rows, :] = pre_grad[
                    sub * 32 : (sub + 1) * 32, j * 128 : (j + 1) * 128
                ]
        return carry

    lax.fori_loop(0, 4, step, 0, unroll=2)
    side = jnp.concatenate([wide[y].astype(BF) for y in range(8)], axis=1)
    out = dot(side, table[...]).astype(BF)
    for s, o in enumerate((o0, o1, o2, o3)):
        o[...] = out[:, s * 128 : (s + 1) * 128]


def sums_kernel(fx, cx, pg, act, hid, lif, sums):
    def step(k, carry):
        proj, lift, skip = carry
        for sub in range(8):
            c = slice(sub * 32, (sub + 1) * 32)
            h = slice(sub * 128, (sub + 1) * 128)
            proj = proj + dot_nt(cx[k, c], act[k, h])
            lift = lift + dot_nt(lif[k, c], hid[k, h])
            skip = skip + dot_nt(pg[k, c], fx[k, c])
        return proj, lift, skip

    zero = jnp.zeros((32, 128), F32)
    got = lax.fori_loop(0, 4, step, (zero, zero, jnp.zeros((32, 32), F32)))
    sums[0:32] = got[0]
    sums[32:64] = got[1]
    sums[64:96] = jnp.concatenate([got[2]] * 4, axis=1)


def finish_kernel(
    r0, r1, r2, r3, back, pg, dskip_t, part, other, out, proj, lift, skip, spectral, wide
):
    sums = part[...] + other[...]
    proj[...] = sums[:32]
    lift[...] = sums[32:64]
    skip[...] = sums[64:, :32]
    inverse_z((r0, r1, r2, r3), back, spectral)

    def step(k, carry):
        got = cell_rows(spectral, k) + dot(dskip_t[...], pg[k])
        for sub in range(8):
            first = 16 * k + 2 * sub
            for j in range(2):
                wide[pl.ds(first + j, 32, stride=64), :] = got[
                    sub * 32 : (sub + 1) * 32, j * 128 : (j + 1) * 128
                ]
        return carry

    lax.fori_loop(0, 4, step, 0, unroll=2)
    out[...] = wide[...].astype(BF)


PACK = (2, 3, 3)
OUTER = (4, 4)
VM = pl.BlockSpec(memory_space=pltpu.VMEM)
ANY = pl.BlockSpec(memory_space=pl.ANY)
HBM = pl.BlockSpec(memory_space=pltpu.HBM)
SM = pl.BlockSpec(memory_space=pltpu.SMEM)
BLOCK = jax.ShapeDtypeStruct((256, 128), BF)
MIB = 1024 * 1024


def cost(us):
    return pl.CostEstimate(flops=0, bytes_accessed=int(us * 3.0e6), transcendentals=0)


def call(
    kernel, ins, outs, scratch=(), name=None, mib=8, us=1.0, smem=1, free=0, far_out=(), alias={}
):
    return pl.pallas_call(
        kernel,
        out_shape=outs,
        in_specs=[SM] * smem + [VM] * (len(ins) - smem - free) + [ANY] * free,
        out_specs=[ANY if at in far_out else VM for at in range(len(outs))],
        scratch_shapes=list(scratch),
        input_output_aliases=alias,
        compiler_params=pltpu.CompilerParams(vmem_limit_bytes=mib * MIB),
        cost_estimate=cost(us),
        name=name,
    )(*ins)


TOKEN = jax.ShapeDtypeStruct((8, 128), F32)


def pack(weight, first, count, after, us):
    chans = weight.shape[1]
    return pl.pallas_call(
        functools.partial(pack_kernel, first),
        out_shape=[jax.ShapeDtypeStruct((count, 2, chans, 64, 128), BF), TOKEN],
        in_specs=[ANY, ANY],
        out_specs=[VM, VM],
        scratch_shapes=[
            pltpu.VMEM((count, 2, 4, chans, 64, 32), BF),
            pltpu.SemaphoreType.DMA((count, 4)),
        ],
        compiler_params=pltpu.CompilerParams(vmem_limit_bytes=36 * MIB),
        cost_estimate=cost(us),
        name="pack",
    )(weight, after)


def exchange(blocks, axes):
    got = [
        lax.ppermute(block, axes, [(a, a ^ step) for a in range(4)])
        for block, step in zip(blocks[1:], STEPS[1:])
    ]
    return [blocks[0]] + got


def swap(part, axis, step):
    size = lax.axis_size(axis)
    return lax.ppermute(part, axis, [(a, a ^ step) for a in range(size)])


def fast(field, cotangent, mode_weight, skip_weight, lift_weight, proj_weight):
    chans, xrows, yrows, zlen = field.shape
    tables = make_tables(zlen, yrows * 4, xrows * 4, 4, xrows, yrows)
    zf, zi, yf, yi, xf, xr, xi, xd = [jnp.asarray(t) for t in tables]
    gyc = ("gy", "col")
    idx = jnp.stack([lax.axis_index(gyc), lax.axis_index("gx")]).astype(jnp.int32)
    four = [BLOCK] * 4
    cells = chans * xrows * yrows
    flat_field = field.reshape(cells, zlen)
    flat_cot = cotangent.reshape(cells, zlen)
    rows = chans * xrows
    wide = pltpu.VMEM((cells, zlen), F32)
    tall = pltpu.VMEM((yrows, rows, zlen), F32)
    weight = mode_weight.reshape(2, chans, chans, 64, 32)
    lift_t = lift_weight.T

    def bf(*shape):
        return jax.ShapeDtypeStruct(shape, BF)

    def lanes(got, table, after, name):
        return call(lane_kernel, (idx, *got, table, after), four, (), name, 4, 1.0, free=1)

    sent = call(
        functools.partial(z_forward_kernel, rows, yrows, zlen),
        (idx, flat_field, zf), four,
        [
            pltpu.VMEM((cells, zlen), BF),
            pltpu.VMEM(zf.shape, BF),
            wide,
            pltpu.SemaphoreType.DMA((2,)),
        ],
        "z_forward", 8, 2.0, free=2,
    )
    got = exchange(sent, gyc)
    one, two, three = PACK
    early, token = pack(weight, 0, one, sent[0], 3.0)
    sent = lanes(got, yf, token, "y_forward")
    got = exchange(sent, "gx")
    late, _ = pack(weight, one, two, sent[0], 5.0)
    modes, *sent, last = call(
        mix_forward_kernel, (idx, *got, xf, xi, early, late, weight),
        [bf(8, 2, 64, 128)] + four + [bf(three, 2, chans, 64, 128)],
        [
            pltpu.VMEM((chans, 2, 64, 128), F32),
            pltpu.VMEM((three, 2, 4, chans, 64, 32), BF),
            pltpu.SemaphoreType.DMA((three, 4)),
        ],
        "mix_forward", 36, 8.0, free=1,
    )
    got = exchange(sent, "gx")
    fx, cx, skipped, backed, dskip_t, dlift, dlift_t, zfp, zip_, yfp, yip = call(
        cells_kernel,
        (idx, flat_field, flat_cot, skip_weight, lift_t, proj_weight, zf, zi, yf, yi),
        [bf(4, 256, 256)] * 2
        + [jax.ShapeDtypeStruct((4, 256, 256), F32), jax.ShapeDtypeStruct((4, 1024, 256), F32)]
        + [bf(256, 256), bf(1024, 256), bf(64, 256)]
        + [bf(1024, 512), bf(512, 1024), bf(512, 512), bf(512, 512)],
        [wide], "cells", 8, 3.0,
    )
    sent = lanes(got, yip, fx, "y_inverse")
    got = exchange(sent, gyc)
    *sent, pg, act, hid, lif = call(
        point_kernel,
        (*got, zip_, zfp, cx, skipped, backed, dlift, dlift_t),
        four + [bf(4, 256, 256), bf(4, 1024, 256), bf(4, 1024, 256), bf(4, 256, 256)],
        [tall, tall], "point", 8, 6.0, 0,
    )
    got = exchange(sent, gyc)
    (part,) = call(
        sums_kernel, (fx, cx, pg, act, hid, lif),
        [jax.ShapeDtypeStruct((96, 128), F32)], (), "sums", 4, 2.5, 0,
    )
    sent = lanes(got, yfp, part, "y_forward")
    got = exchange(sent, "gx")
    for axis in ("col", "gy", "gx"):
        part = part + swap(part, axis, 1)
    other = swap(part, "gx", 2)
    grads = bf(2, chans, chans, 64, 32)
    begin, end = OUTER
    pmodes, *sent = call(
        mix_backward_kernel, (idx, *got, xr, xd, early, late, last),
        [bf(32, 2, 64, 128)] + four, (), "mix_backward", 12, 5.0,
    )
    got = exchange(sent, "gx")
    grad, token = call(
        functools.partial(outer_kernel, 0), (modes, pmodes), [grads, TOKEN],
        outer_scratch(begin, chans), "outer", 20, 5.0, 0, far_out=(0,),
    )
    sent = lanes(got, yip, token, "y_inverse")
    got = exchange(sent, gyc)
    mode_grad, _ = call(
        functools.partial(outer_kernel, begin), (modes, pmodes, sent[0], grad),
        [grads, TOKEN], outer_scratch(end, chans), "outer", 20, 4.0, 0, free=2,
        far_out=(0,), alias={3: 0},
    )
    field_grad, proj_grad, lift_grad, skip_grad = call(
        finish_kernel, (*got, zip_, pg, dskip_t, part, other),
        [bf(cells, zlen)]
        + [jax.ShapeDtypeStruct((chans, n), F32) for n in (128, 128, 32)],
        [tall, wide], "finish", 8, 3.0, 0,
    )
    return (
        field_grad.reshape(field.shape),
        mode_grad.reshape(mode_weight.shape),
        skip_grad,
        lift_grad.T,
        proj_grad,
    )


def fits(field, mode_weight):
    sizes = [lax.axis_size(a) for a in ("gx", "gy", "col")]
    return (
        sizes == [4, 2, 2]
        and field.shape == (32, 8, 8, 128)
        and mode_weight.shape == (2, 32, 32, 8, 8, 32)
    )


def on_device(*args):
    return fast(*args) if fits(args[0], args[2]) else general(*args)


def solution(mesh):
    in_specs = (
        P("grp", "gx", ("gy", "col"), None),
        P("grp", "gx", ("gy", "col"), None),
        P(None, None, None, ("gy", "col"), "gx", None),
        P(),
        P(),
        P(),
    )
    out_specs = (
        P("grp", "gx", ("gy", "col"), None),
        P("grp", None, None, ("gy", "col"), "gx", None),
        P("grp", None),
        P("grp", None),
        P("grp", None),
    )
    return jax.shard_map(
        on_device, mesh=mesh, in_specs=in_specs, out_specs=out_specs, check_vma=False
    )
```

```python
import functools
import math

import jax
import jax.numpy as jnp
import ml_dtypes
import numpy as np
from jax import lax
from jax.experimental import pallas as pl
from jax.experimental.pallas import tpu as pltpu
from jax.sharding import PartitionSpec as P

MX = 32
MY = 32
MZ = 32


KAPPA = 0.7978845608028654
CUBIC = 0.044715


def gelu_slope(value):
    inner = KAPPA * (value + CUBIC * value * value * value)
    tangent = jnp.tanh(inner)
    result = 0.5 * value * (1.0 + tangent)
    slope = 0.5 * (1.0 + tangent) + 0.5 * value * (1.0 - tangent * tangent) * KAPPA * (
        1.0 + 3.0 * CUBIC * value * value
    )
    return (result, slope)


def trig_pair(freqs, length):
    positions = jnp.arange(length, dtype=jnp.int32)
    turns = positions[:, None] * (freqs[None, :] % length) % length
    angle = turns.astype(jnp.float32) * (2.0 * math.pi / length)
    factor = 1.0 / math.sqrt(length)
    return (jnp.cos(angle) * factor, jnp.sin(angle) * factor)


def real_table(freqs, length):
    cosine, sine = trig_pair(freqs, length)
    return jnp.stack([cosine.T, -sine.T]).astype(jnp.bfloat16)


def complex_table(freqs, length):
    cosine, sine = trig_pair(freqs, length)
    upper = jnp.stack([cosine, -sine], axis=1)
    lower = jnp.stack([sine, cosine], axis=1)
    return jnp.stack([upper, lower]).astype(jnp.bfloat16)


def centered(count):
    return jnp.arange(count, dtype=jnp.int32) - count // 2


def to_modes(values, tables):
    z_table, y_table, x_table = tables
    chans, xrows, yrows, zlen = values.shape
    first = jnp.einsum("cxyn,qkn->qkycx", values, z_table, preferred_element_type=jnp.float32)
    first = first.astype(jnp.bfloat16).reshape(2, MZ, yrows, chans * xrows)
    moved = lax.all_to_all(first, ("gy", "col"), split_axis=1, concat_axis=2, tiled=True)
    second = jnp.einsum("pkyr,pyqj->qkjr", moved, y_table, preferred_element_type=jnp.float32)
    second = second.astype(jnp.bfloat16)[:, :, :, None, :]
    crossed = lax.all_to_all(second, "gx", split_axis=2, concat_axis=3, tiled=True)
    crossed = crossed.reshape(crossed.shape[:4] + (chans, xrows))
    third = jnp.einsum("pkjgcx,pgxql->qckjl", crossed, x_table, preferred_element_type=jnp.float32)
    return third.astype(jnp.bfloat16).reshape(2, chans, -1)


def to_grid(spec, tables, shape, local_modes):
    z_table, y_table, x_table = tables
    chans, xrows, yrows, zlen = shape
    spec = spec.reshape((2, chans) + local_modes)
    first = jnp.einsum("pckjl,qgxpl->qkjgcx", spec, x_table, preferred_element_type=jnp.float32)
    first = first.astype(jnp.bfloat16)
    first = first.reshape(first.shape[:4] + (chans * xrows,))
    joined = lax.all_to_all(first, "gx", split_axis=3, concat_axis=2, tiled=True)
    joined = joined.reshape(joined.shape[:3] + (chans * xrows,))
    second = jnp.einsum("pkjr,qypj->qkyr", joined, y_table, preferred_element_type=jnp.float32)
    second = second.astype(jnp.bfloat16)
    returned = lax.all_to_all(second, ("gy", "col"), split_axis=2, concat_axis=1, tiled=True)
    grid = jnp.einsum("pkyr,pkn->ryn", returned, z_table, preferred_element_type=jnp.float32)
    return grid.reshape(chans, xrows, yrows, zlen)


def mix(weight, modes):
    real = jnp.einsum("iok,ik->ok", weight[0], modes[0], preferred_element_type=jnp.float32)
    real = real - jnp.einsum("iok,ik->ok", weight[1], modes[1], preferred_element_type=jnp.float32)
    imag = jnp.einsum("iok,ik->ok", weight[0], modes[1], preferred_element_type=jnp.float32)
    imag = imag + jnp.einsum("iok,ik->ok", weight[1], modes[0], preferred_element_type=jnp.float32)
    return jnp.stack([real, imag]).astype(jnp.bfloat16)


def general(field, cotangent, mode_weight, skip_weight, lift_weight, proj_weight):
    chans, xrows, yrows, zlen = field.shape
    groups_x = lax.axis_size("gx")
    groups_y = lax.axis_size("gy")
    groups_c = lax.axis_size("col")
    span_x = xrows * groups_x
    span_y = yrows * groups_y * groups_c
    column = jnp.arange(MZ, dtype=jnp.int32)
    z_table = real_table(column, zlen)
    y_table = complex_table(centered(MY), span_y)
    x_table = complex_table(centered(MX), span_x).reshape(2, groups_x, xrows, 2, MX)
    tables = (z_table, y_table, x_table)
    local_modes = (mode_weight.shape[3], mode_weight.shape[4], mode_weight.shape[5])
    weight_flat = mode_weight.reshape(2, chans, chans, -1)
    modes = to_modes(field, tables)
    spectral = to_grid(mix(weight_flat, modes), tables, field.shape, local_modes).reshape(chans, -1)
    flat_field = field.reshape(chans, -1)
    flat_grad = cotangent.reshape(chans, -1)
    pre = spectral + jnp.dot(skip_weight, flat_field, preferred_element_type=jnp.float32)
    lifted, slope_pre = gelu_slope(pre)
    lifted = lifted.astype(jnp.bfloat16)
    hidden = jnp.dot(lift_weight, lifted, preferred_element_type=jnp.float32)
    activated, slope_hid = gelu_slope(hidden)
    activated = activated.astype(jnp.bfloat16)
    back_hidden = jnp.dot(proj_weight.T, flat_grad, preferred_element_type=jnp.float32)
    hidden_grad = (back_hidden * slope_hid).astype(jnp.bfloat16)
    grad_up = flat_grad.astype(jnp.float32) + jnp.dot(
        lift_weight.T, hidden_grad, preferred_element_type=jnp.float32
    )
    pre_grad = (grad_up * slope_pre).astype(jnp.bfloat16)
    proj_part = jnp.einsum("cr,hr->ch", flat_grad, activated, preferred_element_type=jnp.float32)
    lift_part = jnp.einsum("hr,cr->hc", hidden_grad, lifted, preferred_element_type=jnp.float32)
    skip_part = jnp.einsum("or,ir->oi", pre_grad, flat_field, preferred_element_type=jnp.float32)
    proj_grad, lift_grad, skip_grad = lax.psum(
        (proj_part, lift_part, skip_part), ("gx", "gy", "col")
    )
    pre_modes = to_modes(pre_grad.reshape(field.shape), tables)
    grad_real = jnp.einsum("ik,ok->iok", modes[0], pre_modes[0], preferred_element_type=jnp.float32)
    grad_real = grad_real + jnp.einsum(
        "ik,ok->iok", modes[1], pre_modes[1], preferred_element_type=jnp.float32
    )
    grad_imag = jnp.einsum("ik,ok->iok", modes[0], pre_modes[1], preferred_element_type=jnp.float32)
    grad_imag = grad_imag - jnp.einsum(
        "ik,ok->iok", modes[1], pre_modes[0], preferred_element_type=jnp.float32
    )
    mode_grad = jnp.stack([grad_real, grad_imag]).astype(jnp.bfloat16).reshape(mode_weight.shape)
    back_real = jnp.einsum(
        "iok,ok->ik", weight_flat[0], pre_modes[0], preferred_element_type=jnp.float32
    )
    back_real = back_real + jnp.einsum(
        "iok,ok->ik", weight_flat[1], pre_modes[1], preferred_element_type=jnp.float32
    )
    back_imag = jnp.einsum(
        "iok,ok->ik", weight_flat[0], pre_modes[1], preferred_element_type=jnp.float32
    )
    back_imag = back_imag - jnp.einsum(
        "iok,ok->ik", weight_flat[1], pre_modes[0], preferred_element_type=jnp.float32
    )
    modes_grad = jnp.stack([back_real, back_imag]).astype(jnp.bfloat16)
    spectral_grad = to_grid(modes_grad, tables, field.shape, local_modes).reshape(chans, -1)
    skip_back = jnp.dot(skip_weight.T, pre_grad, preferred_element_type=jnp.float32)
    field_grad = (spectral_grad + skip_back).astype(jnp.bfloat16).reshape(field.shape)
    return (field_grad, mode_grad, skip_grad, lift_grad, proj_grad)


def np_trig(freqs, length):
    positions = np.arange(length)
    turns = positions[:, None] * (freqs[None, :] % length) % length
    angle = turns.astype(np.float32) * np.float32(2.0 * math.pi / length)
    factor = np.float32(1.0 / math.sqrt(length))
    return np.cos(angle) * factor, np.sin(angle) * factor


def np_complex(cosine, sine, sign):
    table = np.zeros((cosine.shape[0], 2, cosine.shape[1], 2), np.float32)
    table[:, 0, :, 0] = cosine
    table[:, 1, :, 0] = -sign * sine
    table[:, 1, :, 1] = cosine
    table[:, 0, :, 1] = sign * sine
    return table


def make_tables(zlen, span_y, span_x, nb, xrows, yrows):
    kzb, kyb = MZ // nb, MY // nb
    zc, zs = np_trig(np.arange(MZ), zlen)
    yc, ys = np_trig(np.arange(MY) - MY // 2, span_y)
    xc, xs = np_trig(np.arange(MX) - MX // 2, span_x)
    zpart = np.stack([zc, -zs]).reshape(2, zlen, nb, kzb)
    zf = np.einsum("pzbk,yw->yzbwpk", zpart, np.eye(yrows, dtype=np.float32))
    zf = zf.reshape(yrows * zlen, nb, yrows * 2 * kzb).transpose(1, 0, 2)
    zi = np.ascontiguousarray(zf.transpose(0, 2, 1))
    yt = np_complex(yc, ys, -1).reshape(nb, yrows, 2, nb, kyb, 2)
    eye = np.eye(kzb, dtype=np.float32)
    yf = np.einsum("bypjmq,kh->bjypkqhm", yt, eye).reshape(nb, nb, yrows * 2 * kzb, 2 * kzb * kyb)
    yi_t = np_complex(yc, ys, -1).reshape(nb, yrows, 2, nb, kyb, 2)
    yi = np.einsum("bypjmq,kh->jbqhmypk", yi_t, eye).reshape(nb, nb, 2 * kzb * kyb, yrows * 2 * kzb)
    xt = np_complex(xc, xs, -1).reshape(nb, xrows, 2, MX, 2)
    four = np.eye(4, dtype=np.float32)
    xf = np.einsum("bxplq,cd->bpcxqdl", xt, four).reshape(nb, 2, 4 * xrows, 8 * MX)
    xr = np.einsum("bxplq,cd,r->bpcxdqrl", xt, four, np.ones(4, np.float32))
    xr = xr.reshape(nb, 2, 4 * xrows, 32 * MX)
    both = np.stack([xc, xs]).reshape(2, nb, xrows, MX)
    xi = np.einsum("tbxl,r->bxtrl", both, np.ones(4, np.float32)).reshape(nb, xrows, 8 * MX)
    xd = np.einsum("tbxl,cd->bcxtdl", both, four).reshape(nb, 4 * xrows, 8 * MX)
    bf = ml_dtypes.bfloat16
    return [np.asarray(t).astype(bf) for t in (zf, zi, yf, yi, xf, xr)] + [
        xi.astype(bf).astype(np.float32),
        xd.astype(bf),
    ]


def place():
    return lax.axis_index("gy") * lax.axis_size("col") + lax.axis_index("col"), lax.axis_index("gx")


def dot(a, b):
    return lax.dot_general(a, b, (((1,), (0,)), ((), ())), preferred_element_type=jnp.float32)


def dot_nt(a, b):
    return lax.dot_general(a, b, (((1,), (1,)), ((), ())), preferred_element_type=jnp.float32)


BF = jnp.bfloat16
F32 = jnp.float32
STEPS = (0, 2, 3, 1)


def z_table(own):
    z, lane = (lax.broadcasted_iota(jnp.int32, (128, 64), axis) for axis in (0, 1))
    block = jnp.zeros_like(lane)
    for s, step in enumerate(STEPS):
        block = jnp.where(lane // 16 == s, own ^ step, block)
    turns = ((8 * block + lane % 8) * z + 32 * (lane // 8 % 2)) % 128
    values = jnp.cos(turns.astype(F32) * (2.0 * math.pi / 128)) * (1.0 / math.sqrt(128))
    row, at = (lax.broadcasted_iota(jnp.int32, (64, 512), axis) for axis in (0, 1))
    copies = jnp.where((row // 16 == at // 128) & (row % 16 == at % 16), 1.0, 0.0)
    every = dot(values.astype(BF), copies.astype(BF))
    cell = lax.broadcasted_iota(jnp.int32, (128, 512), 1) // 16 % 8
    return jnp.concatenate([jnp.where(cell == y, every, 0.0).astype(BF) for y in range(8)], axis=0)


def z_forward_kernel(rows, yrows, field, o0, o1, o2, o3, wide):
    wide[...] = field[...].astype(F32)
    side = jnp.concatenate(
        [wide[pl.ds(y, rows, stride=yrows), :].astype(BF) for y in range(yrows)], axis=1
    )
    out = dot(side, z_table(place()[0])).astype(BF)
    for s, o in enumerate((o0, o1, o2, o3)):
        o[...] = out[:, s * 128 : (s + 1) * 128]


def lane_kernel(r0, r1, r2, r3, table, after, o0, o1, o2, o3):
    side = jnp.concatenate([r0[...], r1[...], r2[...], r3[...]], axis=1)
    known = table[...] if len(table.shape) == 2 else lane_table(place(), 0, 1, table)
    out = dot(side, known).astype(BF)
    for t, o in enumerate((o0, o1, o2, o3)):
        o[...] = out[:, t * 128 : (t + 1) * 128]


def x_side(idx, refs, tab):
    parts = []
    for g in range(8):
        block = jnp.concatenate([r[g * 32 : (g + 1) * 32, :] for r in refs], axis=0)
        turned = block.astype(F32).T.astype(BF)
        parts.append(jnp.concatenate([turned[:64, :], turned[64:, :]], axis=1))
    side = jnp.concatenate(parts, axis=0)
    table = jnp.concatenate([tab[idx[1] ^ STEPS[s], p] for p in range(2) for s in range(4)], axis=0)
    return side, table


def add_products(total, weight, modes, o, first):
    real, imag = total
    for g in range(weight.shape[0]):
        wr, wi = weight[g, 0, o].astype(F32), weight[g, 1, o].astype(F32)
        mr, mi = modes[first + g, 0].astype(F32), modes[first + g, 1].astype(F32)
        real = real + wr * mr - wi * mi
        imag = imag + wr * mi + wi * mr
    return real, imag


def mix_forward_kernel(
    r0, r1, r2, r3, xf, xi, early, late, weight, modes, o0, o1, o2, o3, last,
    total, held, sem,
):
    idx = place()
    known = early.shape[0] + late.shape[0]
    copies = pack_copies(known, weight, held, sem)
    side, table = x_side(idx, (r0, r1, r2, r3), xf)
    got = dot(side, table).astype(BF)
    for g in range(8):
        for p in range(2):
            part = got[g * 64 : (g + 1) * 64, p * 128 : (p + 1) * 128]
            modes[g, p] = part
    left = jnp.concatenate([xi[idx[1] ^ STEPS[s]] for s in range(4)], axis=0).astype(BF)
    outs = (o0, o1, o2, o3)
    zero = jnp.zeros((64, 128), F32)

    def begin(o, carry):
        got = add_products((zero, zero), early, modes, o, 0)
        total[o, 0], total[o, 1] = add_products(got, late, modes, o, early.shape[0])
        return carry

    lax.fori_loop(0, 32, begin, 0, unroll=16)
    pack_finish(copies, held, last)

    def pair(k, carry):
        rows = []
        for j in range(2):
            o = 2 * k + j
            real, imag = add_products((total[o, 0], total[o, 1]), last, modes, o, known)
            rows.append(jnp.concatenate([real.astype(BF), (-imag).astype(BF)], axis=1))
            rows.append(jnp.concatenate([imag.astype(BF), real.astype(BF)], axis=1))
        got = dot_nt(left, jnp.concatenate(rows, axis=0))
        for s in range(4):
            both = jnp.concatenate(
                [got[s * 8 : (s + 1) * 8, :128], got[s * 8 : (s + 1) * 8, 128:]], axis=0
            )
            outs[s][pl.ds(pl.multiple_of(k * 16, 16), 16), :] = both.astype(BF)
        return carry

    lax.fori_loop(0, 16, pair, 0, unroll=8)


def mix_backward_kernel(
    r0, r1, r2, r3, xr, xd, early, late, last, pmodes, o0, o1, o2, o3
):
    idx = place()
    side, table = x_side(idx, (r0, r1, r2, r3), xr)
    for d in range(4):
        got = dot(side, table[:, d * 256 : (d + 1) * 256]).astype(BF)
        for g in range(8):
            for p in range(2):
                part = got[g * 64 : (g + 1) * 64, p * 128 : (p + 1) * 128]
                pmodes[4 * g + d, p] = part
    left = jnp.concatenate([xd[idx[1] ^ STEPS[s]] for s in range(4)], axis=0)
    outs = (o0, o1, o2, o3)

    def group(weight, first, at, carry):
        g = first + at
        real = jnp.zeros((64, 128), F32)
        imag = jnp.zeros((64, 128), F32)
        for o in range(32):
            wr, wi = weight[at, 0, o].astype(F32), weight[at, 1, o].astype(F32)
            pr, pi = pmodes[o, 0].astype(F32), pmodes[o, 1].astype(F32)
            real = real + wr * pr + wi * pi
            imag = imag + wr * pi - wi * pr
        rows = [
            jnp.concatenate([real.astype(BF), (-imag).astype(BF)], axis=1),
            jnp.concatenate([imag.astype(BF), real.astype(BF)], axis=1),
        ]
        got = dot_nt(left, jnp.concatenate(rows, axis=0)).astype(BF)
        for s in range(4):
            outs[s][pl.ds(pl.multiple_of(g * 32, 32), 32), :] = got[s * 32 : (s + 1) * 32]
        return carry

    first = 0
    for weight in (early, late, last):
        lax.fori_loop(0, weight.shape[0], functools.partial(group, weight, first), 0)
        first += weight.shape[0]


def pack_copies(first, weight, held, sem):
    span = held.shape[3] // 4
    copies = []
    for g in range(held.shape[0]):
        for h in range(4):
            part = pl.ds(h * span, span)
            copies.append(
                pltpu.make_async_copy(
                    weight.at[:, pl.ds(4 * (first + g), 4), part],
                    held.at[g, :, :, part],
                    sem.at[g, h],
                )
            )
            copies[-1].start()
    return copies


def pack_finish(copies, held, packed):
    span = held.shape[3] // 4
    for g in range(held.shape[0]):
        for h in range(4):
            copies[4 * g + h].wait()

            def step(o, carry):
                for p in range(2):
                    packed[g, p, o] = jnp.concatenate(
                        [held[g, p, k, o] for k in range(4)], axis=1
                    )
                return carry

            lax.fori_loop(h * span, (h + 1) * span, step, 0, unroll=8)


def pack_kernel(first, weight, after, packed, token, held, sem):
    pack_finish(pack_copies(first, weight, held, sem), held, packed)
    token[...] = jnp.zeros_like(token)


def outer_start(start, modes, pmodes, grad, held, turned, sem):
    span = pmodes.shape[0] // 4
    copies = []
    for g in range(held.shape[0]):
        for p in range(2):
            m = modes[start + g, p].astype(F32)
            for k in range(4):
                turned[k, p] = (pltpu.roll(m, (128 - 32 * k) % 128, 1) if k else m).astype(BF)
        for h in range(4):

            def step(o, carry):
                pr, pi = pmodes[o, 0], pmodes[o, 1]
                for k in range(4):
                    mr, mi = turned[k, 0], turned[k, 1]
                    held[g, 0, k, o] = (mr * pr + mi * pi)[:, :32]
                    held[g, 1, k, o] = (mr * pi - mi * pr)[:, :32]
                return carry

            lax.fori_loop(h * span, (h + 1) * span, step, 0, unroll=8)
            part = pl.ds(h * span, span)
            copies.append(
                pltpu.make_async_copy(
                    held.at[g, :, :, part],
                    grad.at[:, pl.ds(4 * (start + g), 4), part],
                    sem.at[g, h],
                )
            )
            copies[-1].start()
    return copies


def outer_scratch(count, chans):
    return [
        pltpu.VMEM((count, 2, 4, chans, 64, 32), BF),
        pltpu.VMEM((4, 2, 64, 128), BF),
        pltpu.SemaphoreType.DMA((count, 4)),
    ]


def outer_kernel(start, modes, pmodes, *rest):
    grad, token, held, turned, sem = rest[-5:]
    for copy in outer_start(start, modes, pmodes, grad, held, turned, sem):
        copy.wait()
    token[...] = jnp.zeros_like(token)


def gelu_pair(value):
    square = value * value
    half = 0.5 + 0.5 * jnp.tanh(value * (KAPPA + (KAPPA * CUBIC) * square))
    tail = (1.0 - half) * value * (2.0 * KAPPA + (6.0 * KAPPA * CUBIC) * square)
    return value * half, half + half * tail


def turn(value):
    return value.astype(F32).T.astype(BF)


def spread(block, count):
    rows, lanes = block.shape
    wide = jnp.concatenate([block.astype(F32)] * count, axis=1)
    tall = jnp.concatenate([wide] * count, axis=0)
    at_row = lax.broadcasted_iota(jnp.int32, tall.shape, 0) // rows
    at_lane = lax.broadcasted_iota(jnp.int32, tall.shape, 1) // lanes
    return jnp.where(at_row == at_lane, tall, 0.0).astype(BF)


def by_step(idx, at, table, axis):
    return jnp.concatenate([table[idx[at] ^ STEPS[s]] for s in range(4)], axis=axis)


def lane_table(idx, near, far, table):
    cols = []
    for t in range(4):
        rows = [table[idx[near] ^ STEPS[s], idx[far] ^ STEPS[t]] for s in range(4)]
        cols.append(jnp.concatenate(rows, axis=0))
    return jnp.concatenate(cols, axis=1)


def cells_kernel(
    field, cotangent, skip, lift_t, proj, zf, zi, yf, yi,
    fx, cx, skipped, backed, dskip_t, dlift, dlift_t, zfp, zip_, yfp, yip, wide,
):
    idx = place()
    for src, dst in ((field, fx), (cotangent, cx)):
        wide[...] = src[...].astype(F32)

        def step(k, carry):
            parts = []
            for sub in range(8):
                first = 16 * k + 2 * sub
                parts.append(
                    jnp.concatenate(
                        [wide[pl.ds(first + j, 32, stride=64), :] for j in range(2)], axis=1
                    ).astype(BF)
                )
            dst[k] = jnp.concatenate(parts, axis=0)
            return carry

        lax.fori_loop(0, 4, step, 0)
    dskip = spread(skip[...], 8)
    dproj = spread(turn(proj[...]), 8)
    for k in range(4):
        skipped[k] = dot(dskip, fx[k])
        backed[k] = dot(dproj, cx[k])
    zfp[...] = by_step(idx, 0, zf, 1)
    zip_[...] = by_step(idx, 0, zi, 0)
    yfp[...] = lane_table(idx, 0, 1, yf)
    yip[...] = lane_table(idx, 1, 0, yi)
    dskip_t[...] = spread(turn(skip[...]), 8)
    dlift[...] = spread(turn(lift_t[...]), 8)
    dlift_t[...] = spread(lift_t[...], 2)


def inverse_z(refs, back, spectral):
    side = jnp.concatenate([r[...] for r in refs], axis=1)
    for y in range(4):
        got = dot(side, back[:, y * 256 : (y + 1) * 256])
        spectral[2 * y] = got[:, :128]
        spectral[2 * y + 1] = got[:, 128:]


def cell_rows(spectral, k):
    parts = []
    for sub in range(8):
        rows = pl.ds(2 * k + sub // 4, 32, stride=8)
        parts.append(
            jnp.concatenate([spectral[2 * (sub % 4) + j, rows, :] for j in range(2)], axis=1)
        )
    return jnp.concatenate(parts, axis=0)


def point_kernel(
    r0, r1, r2, r3, back, table, cx, skipped, backed, dlift, dlift_t,
    o0, o1, o2, o3, pg, act, hid, lif, spectral, wide,
):
    inverse_z((r0, r1, r2, r3), back, spectral)

    def step(k, carry):
        grads = cx[k]
        pre = cell_rows(spectral, k) + skipped[k]
        lifted, slope_pre = gelu_pair(pre)
        lifted = lifted.astype(BF)
        lif[k] = lifted
        hidden = dot(dlift[...], lifted)
        up = []
        for q in range(4):
            part = slice(q * 256, (q + 1) * 256)
            activated, slope_hid = gelu_pair(hidden[part])
            hidden_grad = (backed[k, part] * slope_hid).astype(BF)
            act[k, part] = activated.astype(BF)
            hid[k, part] = hidden_grad
            up.append(dot(dlift_t[...], hidden_grad))
        pre_grad = (grads.astype(F32) + jnp.concatenate(up, axis=0)) * slope_pre
        pg[k] = pre_grad.astype(BF)
        for sub in range(8):
            rows = pl.ds(2 * k + sub // 4, 32, stride=8)
            for j in range(2):
                wide[2 * (sub % 4) + j, rows, :] = pre_grad[
                    sub * 32 : (sub + 1) * 32, j * 128 : (j + 1) * 128
                ]
        return carry

    lax.fori_loop(0, 4, step, 0, unroll=2)
    side = jnp.concatenate([wide[y].astype(BF) for y in range(8)], axis=1)
    out = dot(side, table[...]).astype(BF)
    for s, o in enumerate((o0, o1, o2, o3)):
        o[...] = out[:, s * 128 : (s + 1) * 128]


def sums_kernel(fx, cx, pg, act, hid, lif, sums):
    def step(k, carry):
        proj, lift, skip = carry
        for sub in range(8):
            c = slice(sub * 32, (sub + 1) * 32)
            h = slice(sub * 128, (sub + 1) * 128)
            proj = proj + dot_nt(cx[k, c], act[k, h])
            lift = lift + dot_nt(lif[k, c], hid[k, h])
            skip = skip + dot_nt(pg[k, c], fx[k, c])
        return proj, lift, skip

    zero = jnp.zeros((32, 128), F32)
    got = lax.fori_loop(0, 4, step, (zero, zero, jnp.zeros((32, 32), F32)))
    sums[0:32] = got[0]
    sums[32:64] = got[1]
    sums[64:96] = jnp.concatenate([got[2]] * 4, axis=1)


def finish_kernel(
    start, r0, r1, r2, r3, back, pg, dskip_t, part, other, modes, pmodes, so_far,
    out, proj, lift, skip, grad, spectral, wide, held, turned, sem,
):
    copies = outer_start(start, modes, pmodes, grad, held, turned, sem)
    sums = part[...] + other[...]
    proj[...] = sums[:32]
    lift[...] = sums[32:64]
    skip[...] = sums[64:, :32]
    inverse_z((r0, r1, r2, r3), back, spectral)

    def step(k, carry):
        got = cell_rows(spectral, k) + dot(dskip_t[...], pg[k])
        for sub in range(8):
            first = 16 * k + 2 * sub
            for j in range(2):
                wide[pl.ds(first + j, 32, stride=64), :] = got[
                    sub * 32 : (sub + 1) * 32, j * 128 : (j + 1) * 128
                ]
        return carry

    lax.fori_loop(0, 4, step, 0, unroll=2)
    out[...] = wide[...].astype(BF)
    for copy in copies:
        copy.wait()


PACK = (2, 3, 3)
OUTER = (3, 2, 3)
VM = pl.BlockSpec(memory_space=pltpu.VMEM)
ANY = pl.BlockSpec(memory_space=pl.ANY)
HBM = pl.BlockSpec(memory_space=pltpu.HBM)
BLOCK = jax.ShapeDtypeStruct((256, 128), BF)
MIB = 1024 * 1024


def cost(us):
    return pl.CostEstimate(flops=0, bytes_accessed=int(us * 3.0e6), transcendentals=0)


def call(
    kernel, ins, outs, scratch=(), name=None, mib=8, us=1.0, free=0, far_out=(), alias={}
):
    return pl.pallas_call(
        kernel,
        out_shape=outs,
        in_specs=[VM] * (len(ins) - free) + [ANY] * free,
        out_specs=[ANY if at in far_out else VM for at in range(len(outs))],
        scratch_shapes=list(scratch),
        input_output_aliases=alias,
        compiler_params=pltpu.CompilerParams(vmem_limit_bytes=mib * MIB),
        cost_estimate=cost(us),
        name=name,
    )(*ins)


TOKEN = jax.ShapeDtypeStruct((8, 128), F32)


def pack(weight, first, count, after, us):
    chans = weight.shape[1]
    return pl.pallas_call(
        functools.partial(pack_kernel, first),
        out_shape=[jax.ShapeDtypeStruct((count, 2, chans, 64, 128), BF), TOKEN],
        in_specs=[ANY, ANY],
        out_specs=[VM, VM],
        scratch_shapes=[
            pltpu.VMEM((count, 2, 4, chans, 64, 32), BF),
            pltpu.SemaphoreType.DMA((count, 4)),
        ],
        compiler_params=pltpu.CompilerParams(vmem_limit_bytes=36 * MIB),
        cost_estimate=cost(us),
        name="pack",
    )(weight, after)


def exchange(blocks, axes):
    got = [
        lax.ppermute(block, axes, [(a, a ^ step) for a in range(4)])
        for block, step in zip(blocks[1:], STEPS[1:])
    ]
    return [blocks[0]] + got


def swap(part, axis, step):
    size = lax.axis_size(axis)
    return lax.ppermute(part, axis, [(a, a ^ step) for a in range(size)])


def fast(field, cotangent, mode_weight, skip_weight, lift_weight, proj_weight):
    chans, xrows, yrows, zlen = field.shape
    tables = make_tables(zlen, yrows * 4, xrows * 4, 4, xrows, yrows)
    zf, zi, yf, yi, xf, xr, xi, xd = [jnp.asarray(t) for t in tables]
    gyc = ("gy", "col")
    four = [BLOCK] * 4
    cells = chans * xrows * yrows
    flat_field = field.reshape(cells, zlen)
    flat_cot = cotangent.reshape(cells, zlen)
    rows = chans * xrows
    wide = pltpu.VMEM((cells, zlen), F32)
    tall = pltpu.VMEM((yrows, rows, zlen), F32)
    weight = mode_weight.reshape(2, chans, chans, 64, 32)
    lift_t = lift_weight.T

    def bf(*shape):
        return jax.ShapeDtypeStruct(shape, BF)

    def lanes(got, table, after, name):
        return call(lane_kernel, (*got, table, after), four, (), name, 4, 1.0, free=1)

    sent = call(
        functools.partial(z_forward_kernel, rows, yrows), (flat_field,), four, [wide],
        "z_forward", 8, 2.0,
    )
    got = exchange(sent, gyc)
    one, two, three = PACK
    early, token = pack(weight, 0, one, sent[0], 3.0)
    sent = lanes(got, yf, token, "y_forward")
    got = exchange(sent, "gx")
    late, _ = pack(weight, one, two, sent[0], 5.0)
    modes, *sent, last = call(
        mix_forward_kernel, (*got, xf, xi, early, late, weight),
        [bf(8, 2, 64, 128)] + four + [bf(three, 2, chans, 64, 128)],
        [
            pltpu.VMEM((chans, 2, 64, 128), F32),
            pltpu.VMEM((three, 2, 4, chans, 64, 32), BF),
            pltpu.SemaphoreType.DMA((three, 4)),
        ],
        "mix_forward", 36, 8.0, free=1,
    )
    got = exchange(sent, "gx")
    fx, cx, skipped, backed, dskip_t, dlift, dlift_t, zfp, zip_, yfp, yip = call(
        cells_kernel,
        (flat_field, flat_cot, skip_weight, lift_t, proj_weight, zf, zi, yf, yi),
        [bf(4, 256, 256)] * 2
        + [jax.ShapeDtypeStruct((4, 256, 256), F32), jax.ShapeDtypeStruct((4, 1024, 256), F32)]
        + [bf(256, 256), bf(1024, 256), bf(64, 256)]
        + [bf(1024, 512), bf(512, 1024), bf(512, 512), bf(512, 512)],
        [wide], "cells", 8, 3.0,
    )
    sent = lanes(got, yip, fx, "y_inverse")
    got = exchange(sent, gyc)
    *sent, pg, act, hid, lif = call(
        point_kernel,
        (*got, zip_, zfp, cx, skipped, backed, dlift, dlift_t),
        four + [bf(4, 256, 256), bf(4, 1024, 256), bf(4, 1024, 256), bf(4, 256, 256)],
        [tall, tall], "point", 8, 6.0,
    )
    got = exchange(sent, gyc)
    (part,) = call(
        sums_kernel, (fx, cx, pg, act, hid, lif),
        [jax.ShapeDtypeStruct((96, 128), F32)], (), "sums", 4, 2.5,
    )
    sent = lanes(got, yfp, part, "y_forward")
    got = exchange(sent, "gx")
    for axis in ("col", "gy", "gx"):
        part = part + swap(part, axis, 1)
    other = swap(part, "gx", 2)
    grads = bf(2, chans, chans, 64, 32)
    begin, middle, end = OUTER
    pmodes, *sent = call(
        mix_backward_kernel, (*got, xr, xd, early, late, last),
        [bf(32, 2, 64, 128)] + four, (), "mix_backward", 12, 5.0,
    )
    got = exchange(sent, "gx")
    grad, token = call(
        functools.partial(outer_kernel, 0), (modes, pmodes), [grads, TOKEN],
        outer_scratch(begin, chans), "outer", 20, 5.0, far_out=(0,),
    )
    sent = lanes(got, yip, token, "y_inverse")
    got = exchange(sent, gyc)
    grad, _ = call(
        functools.partial(outer_kernel, begin), (modes, pmodes, sent[0], grad),
        [grads, TOKEN], outer_scratch(middle, chans), "outer", 20, 4.0, free=2,
        far_out=(0,), alias={3: 0},
    )
    field_grad, proj_grad, lift_grad, skip_grad, mode_grad = call(
        functools.partial(finish_kernel, begin + middle),
        (*got, zip_, pg, dskip_t, part, other, modes, pmodes, grad),
        [bf(cells, zlen)]
        + [jax.ShapeDtypeStruct((chans, n), F32) for n in (128, 128, 32)]
        + [grads],
        [tall, wide] + outer_scratch(end, chans), "finish", 24, 4.0, free=1,
        far_out=(4,), alias={11: 4},
    )
    return (
        field_grad.reshape(field.shape),
        mode_grad.reshape(mode_weight.shape),
        skip_grad,
        lift_grad.T,
        proj_grad,
    )


def fits(field, mode_weight):
    sizes = [lax.axis_size(a) for a in ("gx", "gy", "col")]
    return (
        sizes == [4, 2, 2]
        and field.shape == (32, 8, 8, 128)
        and mode_weight.shape == (2, 32, 32, 8, 8, 32)
    )


def on_device(*args):
    return fast(*args) if fits(args[0], args[2]) else general(*args)


def solution(mesh):
    in_specs = (
        P("grp", "gx", ("gy", "col"), None),
        P("grp", "gx", ("gy", "col"), None),
        P(None, None, None, ("gy", "col"), "gx", None),
        P(),
        P(),
        P(),
    )
    out_specs = (
        P("grp", "gx", ("gy", "col"), None),
        P("grp", None, None, ("gy", "col"), "gx", None),
        P("grp", None),
        P("grp", None),
        P("grp", None),
    )
    return jax.shard_map(
        on_device, mesh=mesh, in_specs=in_specs, out_specs=out_specs, check_vma=False
    )
```

```python
import functools
import math

import jax
import jax.numpy as jnp
import ml_dtypes
import numpy as np
from jax import lax
from jax.experimental import pallas as pl
from jax.experimental.pallas import tpu as pltpu
from jax.sharding import PartitionSpec as P

MX = 32
MY = 32
MZ = 32


KAPPA = 0.7978845608028654
CUBIC = 0.044715


def gelu_slope(value):
    inner = KAPPA * (value + CUBIC * value * value * value)
    tangent = jnp.tanh(inner)
    result = 0.5 * value * (1.0 + tangent)
    slope = 0.5 * (1.0 + tangent) + 0.5 * value * (1.0 - tangent * tangent) * KAPPA * (
        1.0 + 3.0 * CUBIC * value * value
    )
    return (result, slope)


def trig_pair(freqs, length):
    positions = jnp.arange(length, dtype=jnp.int32)
    turns = positions[:, None] * (freqs[None, :] % length) % length
    angle = turns.astype(jnp.float32) * (2.0 * math.pi / length)
    factor = 1.0 / math.sqrt(length)
    return (jnp.cos(angle) * factor, jnp.sin(angle) * factor)


def real_table(freqs, length):
    cosine, sine = trig_pair(freqs, length)
    return jnp.stack([cosine.T, -sine.T]).astype(jnp.bfloat16)


def complex_table(freqs, length):
    cosine, sine = trig_pair(freqs, length)
    upper = jnp.stack([cosine, -sine], axis=1)
    lower = jnp.stack([sine, cosine], axis=1)
    return jnp.stack([upper, lower]).astype(jnp.bfloat16)


def centered(count):
    return jnp.arange(count, dtype=jnp.int32) - count // 2


def to_modes(values, tables):
    z_table, y_table, x_table = tables
    chans, xrows, yrows, zlen = values.shape
    first = jnp.einsum("cxyn,qkn->qkycx", values, z_table, preferred_element_type=jnp.float32)
    first = first.astype(jnp.bfloat16).reshape(2, MZ, yrows, chans * xrows)
    moved = lax.all_to_all(first, ("gy", "col"), split_axis=1, concat_axis=2, tiled=True)
    second = jnp.einsum("pkyr,pyqj->qkjr", moved, y_table, preferred_element_type=jnp.float32)
    second = second.astype(jnp.bfloat16)[:, :, :, None, :]
    crossed = lax.all_to_all(second, "gx", split_axis=2, concat_axis=3, tiled=True)
    crossed = crossed.reshape(crossed.shape[:4] + (chans, xrows))
    third = jnp.einsum("pkjgcx,pgxql->qckjl", crossed, x_table, preferred_element_type=jnp.float32)
    return third.astype(jnp.bfloat16).reshape(2, chans, -1)


def to_grid(spec, tables, shape, local_modes):
    z_table, y_table, x_table = tables
    chans, xrows, yrows, zlen = shape
    spec = spec.reshape((2, chans) + local_modes)
    first = jnp.einsum("pckjl,qgxpl->qkjgcx", spec, x_table, preferred_element_type=jnp.float32)
    first = first.astype(jnp.bfloat16)
    first = first.reshape(first.shape[:4] + (chans * xrows,))
    joined = lax.all_to_all(first, "gx", split_axis=3, concat_axis=2, tiled=True)
    joined = joined.reshape(joined.shape[:3] + (chans * xrows,))
    second = jnp.einsum("pkjr,qypj->qkyr", joined, y_table, preferred_element_type=jnp.float32)
    second = second.astype(jnp.bfloat16)
    returned = lax.all_to_all(second, ("gy", "col"), split_axis=2, concat_axis=1, tiled=True)
    grid = jnp.einsum("pkyr,pkn->ryn", returned, z_table, preferred_element_type=jnp.float32)
    return grid.reshape(chans, xrows, yrows, zlen)


def mix(weight, modes):
    real = jnp.einsum("iok,ik->ok", weight[0], modes[0], preferred_element_type=jnp.float32)
    real = real - jnp.einsum("iok,ik->ok", weight[1], modes[1], preferred_element_type=jnp.float32)
    imag = jnp.einsum("iok,ik->ok", weight[0], modes[1], preferred_element_type=jnp.float32)
    imag = imag + jnp.einsum("iok,ik->ok", weight[1], modes[0], preferred_element_type=jnp.float32)
    return jnp.stack([real, imag]).astype(jnp.bfloat16)


def general(field, cotangent, mode_weight, skip_weight, lift_weight, proj_weight):
    chans, xrows, yrows, zlen = field.shape
    groups_x = lax.axis_size("gx")
    groups_y = lax.axis_size("gy")
    groups_c = lax.axis_size("col")
    span_x = xrows * groups_x
    span_y = yrows * groups_y * groups_c
    column = jnp.arange(MZ, dtype=jnp.int32)
    z_table = real_table(column, zlen)
    y_table = complex_table(centered(MY), span_y)
    x_table = complex_table(centered(MX), span_x).reshape(2, groups_x, xrows, 2, MX)
    tables = (z_table, y_table, x_table)
    local_modes = (mode_weight.shape[3], mode_weight.shape[4], mode_weight.shape[5])
    weight_flat = mode_weight.reshape(2, chans, chans, -1)
    modes = to_modes(field, tables)
    spectral = to_grid(mix(weight_flat, modes), tables, field.shape, local_modes).reshape(chans, -1)
    flat_field = field.reshape(chans, -1)
    flat_grad = cotangent.reshape(chans, -1)
    pre = spectral + jnp.dot(skip_weight, flat_field, preferred_element_type=jnp.float32)
    lifted, slope_pre = gelu_slope(pre)
    lifted = lifted.astype(jnp.bfloat16)
    hidden = jnp.dot(lift_weight, lifted, preferred_element_type=jnp.float32)
    activated, slope_hid = gelu_slope(hidden)
    activated = activated.astype(jnp.bfloat16)
    back_hidden = jnp.dot(proj_weight.T, flat_grad, preferred_element_type=jnp.float32)
    hidden_grad = (back_hidden * slope_hid).astype(jnp.bfloat16)
    grad_up = flat_grad.astype(jnp.float32) + jnp.dot(
        lift_weight.T, hidden_grad, preferred_element_type=jnp.float32
    )
    pre_grad = (grad_up * slope_pre).astype(jnp.bfloat16)
    proj_part = jnp.einsum("cr,hr->ch", flat_grad, activated, preferred_element_type=jnp.float32)
    lift_part = jnp.einsum("hr,cr->hc", hidden_grad, lifted, preferred_element_type=jnp.float32)
    skip_part = jnp.einsum("or,ir->oi", pre_grad, flat_field, preferred_element_type=jnp.float32)
    proj_grad, lift_grad, skip_grad = lax.psum(
        (proj_part, lift_part, skip_part), ("gx", "gy", "col")
    )
    pre_modes = to_modes(pre_grad.reshape(field.shape), tables)
    grad_real = jnp.einsum("ik,ok->iok", modes[0], pre_modes[0], preferred_element_type=jnp.float32)
    grad_real = grad_real + jnp.einsum(
        "ik,ok->iok", modes[1], pre_modes[1], preferred_element_type=jnp.float32
    )
    grad_imag = jnp.einsum("ik,ok->iok", modes[0], pre_modes[1], preferred_element_type=jnp.float32)
    grad_imag = grad_imag - jnp.einsum(
        "ik,ok->iok", modes[1], pre_modes[0], preferred_element_type=jnp.float32
    )
    mode_grad = jnp.stack([grad_real, grad_imag]).astype(jnp.bfloat16).reshape(mode_weight.shape)
    back_real = jnp.einsum(
        "iok,ok->ik", weight_flat[0], pre_modes[0], preferred_element_type=jnp.float32
    )
    back_real = back_real + jnp.einsum(
        "iok,ok->ik", weight_flat[1], pre_modes[1], preferred_element_type=jnp.float32
    )
    back_imag = jnp.einsum(
        "iok,ok->ik", weight_flat[0], pre_modes[1], preferred_element_type=jnp.float32
    )
    back_imag = back_imag - jnp.einsum(
        "iok,ok->ik", weight_flat[1], pre_modes[0], preferred_element_type=jnp.float32
    )
    modes_grad = jnp.stack([back_real, back_imag]).astype(jnp.bfloat16)
    spectral_grad = to_grid(modes_grad, tables, field.shape, local_modes).reshape(chans, -1)
    skip_back = jnp.dot(skip_weight.T, pre_grad, preferred_element_type=jnp.float32)
    field_grad = (spectral_grad + skip_back).astype(jnp.bfloat16).reshape(field.shape)
    return (field_grad, mode_grad, skip_grad, lift_grad, proj_grad)


def np_trig(freqs, length):
    positions = np.arange(length)
    turns = positions[:, None] * (freqs[None, :] % length) % length
    angle = turns.astype(np.float32) * np.float32(2.0 * math.pi / length)
    factor = np.float32(1.0 / math.sqrt(length))
    return np.cos(angle) * factor, np.sin(angle) * factor


def np_complex(cosine, sine, sign):
    table = np.zeros((cosine.shape[0], 2, cosine.shape[1], 2), np.float32)
    table[:, 0, :, 0] = cosine
    table[:, 1, :, 0] = -sign * sine
    table[:, 1, :, 1] = cosine
    table[:, 0, :, 1] = sign * sine
    return table


def make_tables(zlen, span_y, span_x, nb, xrows, yrows):
    kzb, kyb = MZ // nb, MY // nb
    zc, zs = np_trig(np.arange(MZ), zlen)
    yc, ys = np_trig(np.arange(MY) - MY // 2, span_y)
    xc, xs = np_trig(np.arange(MX) - MX // 2, span_x)
    zpart = np.stack([zc, -zs]).reshape(2, zlen, nb, kzb)
    zf = np.einsum("pzbk,yw->yzbwpk", zpart, np.eye(yrows, dtype=np.float32))
    zf = zf.reshape(yrows * zlen, nb, yrows * 2 * kzb).transpose(1, 0, 2)
    zi = np.ascontiguousarray(zf.transpose(0, 2, 1))
    yt = np_complex(yc, ys, -1).reshape(nb, yrows, 2, nb, kyb, 2)
    eye = np.eye(kzb, dtype=np.float32)
    yf = np.einsum("bypjmq,kh->bjypkqhm", yt, eye).reshape(nb, nb, yrows * 2 * kzb, 2 * kzb * kyb)
    yi_t = np_complex(yc, ys, -1).reshape(nb, yrows, 2, nb, kyb, 2)
    yi = np.einsum("bypjmq,kh->jbqhmypk", yi_t, eye).reshape(nb, nb, 2 * kzb * kyb, yrows * 2 * kzb)
    xt = np_complex(xc, xs, -1).reshape(nb, xrows, 2, MX, 2)
    four = np.eye(4, dtype=np.float32)
    xf = np.einsum("bxplq,cd->bpcxqdl", xt, four).reshape(nb, 2, 4 * xrows, 8 * MX)
    xr = np.einsum("bxplq,cd,r->bpcxdqrl", xt, four, np.ones(4, np.float32))
    xr = xr.reshape(nb, 2, 4 * xrows, 32 * MX)
    both = np.stack([xc, xs]).reshape(2, nb, xrows, MX)
    xi = np.einsum("tbxl,r->bxtrl", both, np.ones(4, np.float32)).reshape(nb, xrows, 8 * MX)
    xd = np.einsum("tbxl,cd->bcxtdl", both, four).reshape(nb, 4 * xrows, 8 * MX)
    bf = ml_dtypes.bfloat16
    return [np.asarray(t).astype(bf) for t in (zf, zi, yf, yi, xf, xr)] + [
        xi.astype(bf).astype(np.float32),
        xd.astype(bf),
    ]


def place():
    return lax.axis_index("gy") * lax.axis_size("col") + lax.axis_index("col"), lax.axis_index("gx")


def dot(a, b):
    return lax.dot_general(a, b, (((1,), (0,)), ((), ())), preferred_element_type=jnp.float32)


def dot_nt(a, b):
    return lax.dot_general(a, b, (((1,), (1,)), ((), ())), preferred_element_type=jnp.float32)


BF = jnp.bfloat16
F32 = jnp.float32
STEPS = (0, 2, 3, 1)


def z_table(own):
    z, lane = (lax.broadcasted_iota(jnp.int32, (128, 64), axis) for axis in (0, 1))
    block = jnp.zeros_like(lane)
    for s, step in enumerate(STEPS):
        block = jnp.where(lane // 16 == s, own ^ step, block)
    turns = ((8 * block + lane % 8) * z + 32 * (lane // 8 % 2)) % 128
    values = jnp.cos(turns.astype(F32) * (2.0 * math.pi / 128)) * (1.0 / math.sqrt(128))
    row, at = (lax.broadcasted_iota(jnp.int32, (64, 512), axis) for axis in (0, 1))
    copies = jnp.where((row // 16 == at // 128) & (row % 16 == at % 16), 1.0, 0.0)
    every = dot(values.astype(BF), copies.astype(BF))
    cell = lax.broadcasted_iota(jnp.int32, (128, 512), 1) // 16 % 8
    return jnp.concatenate([jnp.where(cell == y, every, 0.0).astype(BF) for y in range(8)], axis=0)


def z_forward_kernel(rows, yrows, field, o0, o1, o2, o3, wide):
    wide[...] = field[...].astype(F32)
    side = jnp.concatenate(
        [wide[pl.ds(y, rows, stride=yrows), :].astype(BF) for y in range(yrows)], axis=1
    )
    out = dot(side, z_table(place()[0])).astype(BF)
    for s, o in enumerate((o0, o1, o2, o3)):
        o[...] = out[:, s * 128 : (s + 1) * 128]


def lane_kernel(r0, r1, r2, r3, table, after, o0, o1, o2, o3):
    side = jnp.concatenate([r0[...], r1[...], r2[...], r3[...]], axis=1)
    known = table[...] if len(table.shape) == 2 else lane_table(place(), 0, 1, table)
    out = dot(side, known).astype(BF)
    for t, o in enumerate((o0, o1, o2, o3)):
        o[...] = out[:, t * 128 : (t + 1) * 128]


def x_side(idx, refs, tab):
    parts = []
    for g in range(8):
        block = jnp.concatenate([r[g * 32 : (g + 1) * 32, :] for r in refs], axis=0)
        turned = block.astype(F32).T.astype(BF)
        parts.append(jnp.concatenate([turned[:64, :], turned[64:, :]], axis=1))
    side = jnp.concatenate(parts, axis=0)
    table = jnp.concatenate([tab[idx[1] ^ STEPS[s], p] for p in range(2) for s in range(4)], axis=0)
    return side, table


def add_products(total, weight, modes, o, first):
    real, imag = total
    for g in range(weight.shape[0]):
        wr, wi = weight[g, 0, o].astype(F32), weight[g, 1, o].astype(F32)
        mr, mi = modes[first + g, 0].astype(F32), modes[first + g, 1].astype(F32)
        real = real + wr * mr - wi * mi
        imag = imag + wr * mi + wi * mr
    return real, imag


def mix_forward_kernel(
    r0, r1, r2, r3, xf, xi, early, late, weight, modes, o0, o1, o2, o3, last,
    total, held, sem,
):
    idx = place()
    known = early.shape[0] + late.shape[0]
    copies = pack_copies(known, weight, held, sem)
    side, table = x_side(idx, (r0, r1, r2, r3), xf)
    got = dot(side, table).astype(BF)
    for g in range(8):
        for p in range(2):
            part = got[g * 64 : (g + 1) * 64, p * 128 : (p + 1) * 128]
            modes[g, p] = part
    left = jnp.concatenate([xi[idx[1] ^ STEPS[s]] for s in range(4)], axis=0).astype(BF)
    outs = (o0, o1, o2, o3)
    zero = jnp.zeros((64, 128), F32)

    def begin(o, carry):
        got = add_products((zero, zero), early, modes, o, 0)
        total[o, 0], total[o, 1] = add_products(got, late, modes, o, early.shape[0])
        return carry

    lax.fori_loop(0, 32, begin, 0, unroll=16)
    pack_finish(copies, held, last)

    def pair(k, carry):
        rows = []
        for j in range(2):
            o = 2 * k + j
            real, imag = add_products((total[o, 0], total[o, 1]), last, modes, o, known)
            rows.append(jnp.concatenate([real.astype(BF), (-imag).astype(BF)], axis=1))
            rows.append(jnp.concatenate([imag.astype(BF), real.astype(BF)], axis=1))
        got = dot_nt(left, jnp.concatenate(rows, axis=0))
        for s in range(4):
            both = jnp.concatenate(
                [got[s * 8 : (s + 1) * 8, :128], got[s * 8 : (s + 1) * 8, 128:]], axis=0
            )
            outs[s][pl.ds(pl.multiple_of(k * 16, 16), 16), :] = both.astype(BF)
        return carry

    lax.fori_loop(0, 16, pair, 0, unroll=8)


def mix_backward_kernel(
    r0, r1, r2, r3, xr, xd, early, late, last, pmodes, o0, o1, o2, o3
):
    idx = place()
    side, table = x_side(idx, (r0, r1, r2, r3), xr)
    for d in range(4):
        got = dot(side, table[:, d * 256 : (d + 1) * 256]).astype(BF)
        for g in range(8):
            for p in range(2):
                part = got[g * 64 : (g + 1) * 64, p * 128 : (p + 1) * 128]
                pmodes[4 * g + d, p] = part
    left = jnp.concatenate([xd[idx[1] ^ STEPS[s]] for s in range(4)], axis=0)
    outs = (o0, o1, o2, o3)

    def group(weight, first, at, carry):
        g = first + at
        real = jnp.zeros((64, 128), F32)
        imag = jnp.zeros((64, 128), F32)
        for o in range(32):
            wr, wi = weight[at, 0, o].astype(F32), weight[at, 1, o].astype(F32)
            pr, pi = pmodes[o, 0].astype(F32), pmodes[o, 1].astype(F32)
            real = real + wr * pr + wi * pi
            imag = imag + wr * pi - wi * pr
        rows = [
            jnp.concatenate([real.astype(BF), (-imag).astype(BF)], axis=1),
            jnp.concatenate([imag.astype(BF), real.astype(BF)], axis=1),
        ]
        got = dot_nt(left, jnp.concatenate(rows, axis=0)).astype(BF)
        for s in range(4):
            outs[s][pl.ds(pl.multiple_of(g * 32, 32), 32), :] = got[s * 32 : (s + 1) * 32]
        return carry

    first = 0
    for weight in (early, late, last):
        lax.fori_loop(0, weight.shape[0], functools.partial(group, weight, first), 0)
        first += weight.shape[0]


def pack_copies(first, weight, held, sem):
    span = held.shape[3] // 4
    copies = []
    for g in range(held.shape[0]):
        for h in range(4):
            part = pl.ds(h * span, span)
            copies.append(
                pltpu.make_async_copy(
                    weight.at[:, pl.ds(4 * (first + g), 4), part],
                    held.at[g, :, :, part],
                    sem.at[g, h],
                )
            )
            copies[-1].start()
    return copies


def pack_finish(copies, held, packed):
    row, lane = (lax.broadcasted_iota(jnp.int32, (32, 128), axis) for axis in (0, 1))
    moved = jnp.where(lane == row + 96, 1.0, 0.0).astype(BF)
    span = held.shape[3] // 4
    for g in range(held.shape[0]):
        for h in range(4):
            copies[4 * g + h].wait()

            def step(o, carry):
                for p in range(2):
                    three = [held[g, p, k, o] for k in range(3)] + [jnp.zeros((64, 32), BF)]
                    fourth = dot(held[g, p, 3, o], moved).astype(BF)
                    packed[g, p, o] = jnp.concatenate(three, axis=1) + fourth
                return carry

            lax.fori_loop(h * span, (h + 1) * span, step, 0, unroll=8)


def pack_kernel(first, weight, after, packed, token, held, sem):
    pack_finish(pack_copies(first, weight, held, sem), held, packed)
    token[...] = jnp.zeros_like(token)


def outer_start(start, modes, pmodes, grad, held, turned, sem):
    span = pmodes.shape[0] // 4
    copies = []
    for g in range(held.shape[0]):
        for p in range(2):
            m = modes[start + g, p].astype(F32)
            for k in range(3):
                turned[k, p] = (pltpu.roll(m, (128 - 32 * k) % 128, 1) if k else m).astype(BF)
        for h in range(4):

            def step(o, carry):
                pr, pi = pmodes[o, 0], pmodes[o, 1]
                for k in range(3):
                    mr, mi = turned[k, 0], turned[k, 1]
                    both = mr * pr + mi * pi, mr * pi - mi * pr
                    for p in range(2):
                        held[g, p, k, o] = both[p][:, :32]
                        if k == 1:
                            held[g, p, 3, o] = pltpu.roll(both[p], 64, 1)[:, :32]
                return carry

            lax.fori_loop(h * span, (h + 1) * span, step, 0, unroll=8)
            part = pl.ds(h * span, span)
            copies.append(
                pltpu.make_async_copy(
                    held.at[g, :, :, part],
                    grad.at[:, pl.ds(4 * (start + g), 4), part],
                    sem.at[g, h],
                )
            )
            copies[-1].start()
    return copies


def outer_scratch(count, chans):
    return [
        pltpu.VMEM((count, 2, 4, chans, 64, 32), BF),
        pltpu.VMEM((3, 2, 64, 128), BF),
        pltpu.SemaphoreType.DMA((count, 4)),
    ]


def outer_kernel(start, modes, pmodes, *rest):
    grad, token, held, turned, sem = rest[-5:]
    for copy in outer_start(start, modes, pmodes, grad, held, turned, sem):
        copy.wait()
    token[...] = jnp.zeros_like(token)


def gelu_pair(value):
    square = value * value
    half = 0.5 + 0.5 * jnp.tanh(value * (KAPPA + (KAPPA * CUBIC) * square))
    tail = (1.0 - half) * value * (2.0 * KAPPA + (6.0 * KAPPA * CUBIC) * square)
    return value * half, half + half * tail


def turn(value):
    return value.astype(F32).T.astype(BF)


def spread(block, count):
    rows, lanes = block.shape
    wide = jnp.concatenate([block.astype(F32)] * count, axis=1)
    tall = jnp.concatenate([wide] * count, axis=0)
    at_row = lax.broadcasted_iota(jnp.int32, tall.shape, 0) // rows
    at_lane = lax.broadcasted_iota(jnp.int32, tall.shape, 1) // lanes
    return jnp.where(at_row == at_lane, tall, 0.0).astype(BF)


def by_step(idx, at, table, axis):
    return jnp.concatenate([table[idx[at] ^ STEPS[s]] for s in range(4)], axis=axis)


def lane_table(idx, near, far, table):
    cols = []
    for t in range(4):
        rows = [table[idx[near] ^ STEPS[s], idx[far] ^ STEPS[t]] for s in range(4)]
        cols.append(jnp.concatenate(rows, axis=0))
    return jnp.concatenate(cols, axis=1)


def cells_kernel(
    field, cotangent, skip, lift_t, proj, zf, zi, yf, yi,
    fx, cx, skipped, backed, dskip_t, dlift, dlift_t, zfp, zip_, yfp, yip, wide,
):
    idx = place()
    for src, dst in ((field, fx), (cotangent, cx)):
        wide[...] = src[...].astype(F32)

        def step(k, carry):
            parts = []
            for sub in range(8):
                first = 16 * k + 2 * sub
                parts.append(
                    jnp.concatenate(
                        [wide[pl.ds(first + j, 32, stride=64), :] for j in range(2)], axis=1
                    ).astype(BF)
                )
            dst[k] = jnp.concatenate(parts, axis=0)
            return carry

        lax.fori_loop(0, 4, step, 0)
    dskip = spread(skip[...], 8)
    dproj = spread(turn(proj[...]), 8)
    for k in range(4):
        skipped[k] = dot(dskip, fx[k])
        backed[k] = dot(dproj, cx[k])
    zfp[...] = by_step(idx, 0, zf, 1)
    zip_[...] = by_step(idx, 0, zi, 0)
    yfp[...] = lane_table(idx, 0, 1, yf)
    yip[...] = lane_table(idx, 1, 0, yi)
    dskip_t[...] = spread(turn(skip[...]), 8)
    dlift[...] = spread(turn(lift_t[...]), 8)
    dlift_t[...] = spread(lift_t[...], 2)


def inverse_z(refs, back, spectral):
    side = jnp.concatenate([r[...] for r in refs], axis=1)
    for y in range(4):
        got = dot(side, back[:, y * 256 : (y + 1) * 256])
        spectral[2 * y] = got[:, :128]
        spectral[2 * y + 1] = got[:, 128:]


def cell_rows(spectral, k):
    parts = []
    for sub in range(8):
        rows = pl.ds(2 * k + sub // 4, 32, stride=8)
        parts.append(
            jnp.concatenate([spectral[2 * (sub % 4) + j, rows, :] for j in range(2)], axis=1)
        )
    return jnp.concatenate(parts, axis=0)


def point_kernel(
    r0, r1, r2, r3, back, table, cx, skipped, backed, dlift, dlift_t,
    o0, o1, o2, o3, pg, act, hid, lif, spectral, wide,
):
    inverse_z((r0, r1, r2, r3), back, spectral)

    def step(k, carry):
        grads = cx[k]
        pre = cell_rows(spectral, k) + skipped[k]
        lifted, slope_pre = gelu_pair(pre)
        lifted = lifted.astype(BF)
        lif[k] = lifted
        hidden = dot(dlift[...], lifted)
        up = []
        for q in range(4):
            part = slice(q * 256, (q + 1) * 256)
            activated, slope_hid = gelu_pair(hidden[part])
            hidden_grad = (backed[k, part] * slope_hid).astype(BF)
            act[k, part] = activated.astype(BF)
            hid[k, part] = hidden_grad
            up.append(dot(dlift_t[...], hidden_grad))
        pre_grad = (grads.astype(F32) + jnp.concatenate(up, axis=0)) * slope_pre
        pg[k] = pre_grad.astype(BF)
        for sub in range(8):
            rows = pl.ds(2 * k + sub // 4, 32, stride=8)
            for j in range(2):
                wide[2 * (sub % 4) + j, rows, :] = pre_grad[
                    sub * 32 : (sub + 1) * 32, j * 128 : (j + 1) * 128
                ]
        return carry

    lax.fori_loop(0, 4, step, 0, unroll=4)
    side = jnp.concatenate([wide[y].astype(BF) for y in range(8)], axis=1)
    out = dot(side, table[...]).astype(BF)
    for s, o in enumerate((o0, o1, o2, o3)):
        o[...] = out[:, s * 128 : (s + 1) * 128]


def sums_kernel(fx, cx, pg, act, hid, lif, sums):
    def step(k, carry):
        proj, lift, skip = carry
        for sub in range(8):
            c = slice(sub * 32, (sub + 1) * 32)
            h = slice(sub * 128, (sub + 1) * 128)
            proj = proj + dot_nt(cx[k, c], act[k, h])
            lift = lift + dot_nt(lif[k, c], hid[k, h])
            skip = skip + dot_nt(pg[k, c], fx[k, c])
        return proj, lift, skip

    zero = jnp.zeros((32, 128), F32)
    got = lax.fori_loop(0, 4, step, (zero, zero, jnp.zeros((32, 32), F32)))
    sums[0:32] = got[0]
    sums[32:64] = got[1]
    sums[64:96] = jnp.concatenate([got[2]] * 4, axis=1)


def finish_kernel(
    start, r0, r1, r2, r3, back, pg, dskip_t, part, other, modes, pmodes, so_far,
    out, proj, lift, skip, grad, spectral, wide, held, turned, sem,
):
    copies = outer_start(start, modes, pmodes, grad, held, turned, sem)
    sums = part[...] + other[...]
    proj[...] = sums[:32]
    lift[...] = sums[32:64]
    skip[...] = sums[64:, :32]
    inverse_z((r0, r1, r2, r3), back, spectral)

    def step(k, carry):
        got = cell_rows(spectral, k) + dot(dskip_t[...], pg[k])
        for sub in range(8):
            first = 16 * k + 2 * sub
            for j in range(2):
                wide[pl.ds(first + j, 32, stride=64), :] = got[
                    sub * 32 : (sub + 1) * 32, j * 128 : (j + 1) * 128
                ]
        return carry

    lax.fori_loop(0, 4, step, 0, unroll=4)
    out[...] = wide[...].astype(BF)
    for copy in copies:
        copy.wait()


PACK = (2, 3, 3)
OUTER = (3, 2, 3)
VM = pl.BlockSpec(memory_space=pltpu.VMEM)
ANY = pl.BlockSpec(memory_space=pl.ANY)
HBM = pl.BlockSpec(memory_space=pltpu.HBM)
BLOCK = jax.ShapeDtypeStruct((256, 128), BF)
MIB = 1024 * 1024


def cost(us):
    return pl.CostEstimate(flops=0, bytes_accessed=int(us * 3.0e6), transcendentals=0)


def call(
    kernel, ins, outs, scratch=(), name=None, mib=8, us=1.0, free=0, far_out=(), alias={}
):
    return pl.pallas_call(
        kernel,
        out_shape=outs,
        in_specs=[VM] * (len(ins) - free) + [ANY] * free,
        out_specs=[ANY if at in far_out else VM for at in range(len(outs))],
        scratch_shapes=list(scratch),
        input_output_aliases=alias,
        compiler_params=pltpu.CompilerParams(vmem_limit_bytes=mib * MIB),
        cost_estimate=cost(us),
        name=name,
    )(*ins)


TOKEN = jax.ShapeDtypeStruct((8, 128), F32)


def pack(weight, first, count, after, us):
    chans = weight.shape[1]
    return pl.pallas_call(
        functools.partial(pack_kernel, first),
        out_shape=[jax.ShapeDtypeStruct((count, 2, chans, 64, 128), BF), TOKEN],
        in_specs=[ANY, ANY],
        out_specs=[VM, VM],
        scratch_shapes=[
            pltpu.VMEM((count, 2, 4, chans, 64, 32), BF),
            pltpu.SemaphoreType.DMA((count, 4)),
        ],
        compiler_params=pltpu.CompilerParams(vmem_limit_bytes=36 * MIB),
        cost_estimate=cost(us),
        name="pack",
    )(weight, after)


def exchange(blocks, axes):
    got = [
        lax.ppermute(block, axes, [(a, a ^ step) for a in range(4)])
        for block, step in zip(blocks[1:], STEPS[1:])
    ]
    return [blocks[0]] + got


def swap(part, axis, step):
    size = lax.axis_size(axis)
    return lax.ppermute(part, axis, [(a, a ^ step) for a in range(size)])


def fast(field, cotangent, mode_weight, skip_weight, lift_weight, proj_weight):
    chans, xrows, yrows, zlen = field.shape
    tables = make_tables(zlen, yrows * 4, xrows * 4, 4, xrows, yrows)
    zf, zi, yf, yi, xf, xr, xi, xd = [jnp.asarray(t) for t in tables]
    gyc = ("gy", "col")
    four = [BLOCK] * 4
    cells = chans * xrows * yrows
    flat_field = field.reshape(cells, zlen)
    flat_cot = cotangent.reshape(cells, zlen)
    rows = chans * xrows
    wide = pltpu.VMEM((cells, zlen), F32)
    tall = pltpu.VMEM((yrows, rows, zlen), F32)
    weight = mode_weight.reshape(2, chans, chans, 64, 32)
    lift_t = lift_weight.T

    def bf(*shape):
        return jax.ShapeDtypeStruct(shape, BF)

    def lanes(got, table, after, name):
        return call(lane_kernel, (*got, table, after), four, (), name, 4, 1.0, free=1)

    sent = call(
        functools.partial(z_forward_kernel, rows, yrows), (flat_field,), four, [wide],
        "z_forward", 8, 2.0,
    )
    got = exchange(sent, gyc)
    one, two, three = PACK
    early, token = pack(weight, 0, one, sent[0], 3.0)
    sent = lanes(got, yf, token, "y_forward")
    got = exchange(sent, "gx")
    late, _ = pack(weight, one, two, sent[0], 5.0)
    modes, *sent, last = call(
        mix_forward_kernel, (*got, xf, xi, early, late, weight),
        [bf(8, 2, 64, 128)] + four + [bf(three, 2, chans, 64, 128)],
        [
            pltpu.VMEM((chans, 2, 64, 128), F32),
            pltpu.VMEM((three, 2, 4, chans, 64, 32), BF),
            pltpu.SemaphoreType.DMA((three, 4)),
        ],
        "mix_forward", 36, 8.0, free=1,
    )
    got = exchange(sent, "gx")
    fx, cx, skipped, backed, dskip_t, dlift, dlift_t, zfp, zip_, yfp, yip = call(
        cells_kernel,
        (flat_field, flat_cot, skip_weight, lift_t, proj_weight, zf, zi, yf, yi),
        [bf(4, 256, 256)] * 2
        + [jax.ShapeDtypeStruct((4, 256, 256), F32), jax.ShapeDtypeStruct((4, 1024, 256), F32)]
        + [bf(256, 256), bf(1024, 256), bf(64, 256)]
        + [bf(1024, 512), bf(512, 1024), bf(512, 512), bf(512, 512)],
        [wide], "cells", 8, 3.0,
    )
    sent = lanes(got, yip, fx, "y_inverse")
    got = exchange(sent, gyc)
    *sent, pg, act, hid, lif = call(
        point_kernel,
        (*got, zip_, zfp, cx, skipped, backed, dlift, dlift_t),
        four + [bf(4, 256, 256), bf(4, 1024, 256), bf(4, 1024, 256), bf(4, 256, 256)],
        [tall, tall], "point", 8, 6.0,
    )
    got = exchange(sent, gyc)
    (part,) = call(
        sums_kernel, (fx, cx, pg, act, hid, lif),
        [jax.ShapeDtypeStruct((96, 128), F32)], (), "sums", 4, 2.5,
    )
    sent = lanes(got, yfp, part, "y_forward")
    got = exchange(sent, "gx")
    for axis in ("col", "gy", "gx"):
        part = part + swap(part, axis, 1)
    other = swap(part, "gx", 2)
    grads = bf(2, chans, chans, 64, 32)
    begin, middle, end = OUTER
    pmodes, *sent = call(
        mix_backward_kernel, (*got, xr, xd, early, late, last),
        [bf(32, 2, 64, 128)] + four, (), "mix_backward", 12, 5.0,
    )
    got = exchange(sent, "gx")
    grad, token = call(
        functools.partial(outer_kernel, 0), (modes, pmodes), [grads, TOKEN],
        outer_scratch(begin, chans), "outer", 20, 5.0, far_out=(0,),
    )
    sent = lanes(got, yip, token, "y_inverse")
    got = exchange(sent, gyc)
    grad, _ = call(
        functools.partial(outer_kernel, begin), (modes, pmodes, sent[0], grad),
        [grads, TOKEN], outer_scratch(middle, chans), "outer", 20, 4.0, free=2,
        far_out=(0,), alias={3: 0},
    )
    field_grad, proj_grad, lift_grad, skip_grad, mode_grad = call(
        functools.partial(finish_kernel, begin + middle),
        (*got, zip_, pg, dskip_t, part, other, modes, pmodes, grad),
        [bf(cells, zlen)]
        + [jax.ShapeDtypeStruct((chans, n), F32) for n in (128, 128, 32)]
        + [grads],
        [tall, wide] + outer_scratch(end, chans), "finish", 24, 4.0, free=1,
        far_out=(4,), alias={11: 4},
    )
    return (
        field_grad.reshape(field.shape),
        mode_grad.reshape(mode_weight.shape),
        skip_grad,
        lift_grad.T,
        proj_grad,
    )


def fits(field, mode_weight):
    sizes = [lax.axis_size(a) for a in ("gx", "gy", "col")]
    return (
        sizes == [4, 2, 2]
        and field.shape == (32, 8, 8, 128)
        and mode_weight.shape == (2, 32, 32, 8, 8, 32)
    )


def on_device(*args):
    return fast(*args) if fits(args[0], args[2]) else general(*args)


def solution(mesh):
    in_specs = (
        P("grp", "gx", ("gy", "col"), None),
        P("grp", "gx", ("gy", "col"), None),
        P(None, None, None, ("gy", "col"), "gx", None),
        P(),
        P(),
        P(),
    )
    out_specs = (
        P("grp", "gx", ("gy", "col"), None),
        P("grp", None, None, ("gy", "col"), "gx", None),
        P("grp", None),
        P("grp", None),
        P("grp", None),
    )
    return jax.shard_map(
        on_device, mesh=mesh, in_specs=in_specs, out_specs=out_specs, check_vma=False
    )
```

```python
import functools
import math

import jax
import jax.numpy as jnp
import ml_dtypes
import numpy as np
from jax import lax
from jax.experimental import pallas as pl
from jax.experimental.pallas import tpu as pltpu
from jax.sharding import PartitionSpec as P

MX = 32
MY = 32
MZ = 32


KAPPA = 0.7978845608028654
CUBIC = 0.044715


def gelu_slope(value):
    inner = KAPPA * (value + CUBIC * value * value * value)
    tangent = jnp.tanh(inner)
    result = 0.5 * value * (1.0 + tangent)
    slope = 0.5 * (1.0 + tangent) + 0.5 * value * (1.0 - tangent * tangent) * KAPPA * (
        1.0 + 3.0 * CUBIC * value * value
    )
    return (result, slope)


def trig_pair(freqs, length):
    positions = jnp.arange(length, dtype=jnp.int32)
    turns = positions[:, None] * (freqs[None, :] % length) % length
    angle = turns.astype(jnp.float32) * (2.0 * math.pi / length)
    factor = 1.0 / math.sqrt(length)
    return (jnp.cos(angle) * factor, jnp.sin(angle) * factor)


def real_table(freqs, length):
    cosine, sine = trig_pair(freqs, length)
    return jnp.stack([cosine.T, -sine.T]).astype(jnp.bfloat16)


def complex_table(freqs, length):
    cosine, sine = trig_pair(freqs, length)
    upper = jnp.stack([cosine, -sine], axis=1)
    lower = jnp.stack([sine, cosine], axis=1)
    return jnp.stack([upper, lower]).astype(jnp.bfloat16)


def centered(count):
    return jnp.arange(count, dtype=jnp.int32) - count // 2


def to_modes(values, tables):
    z_table, y_table, x_table = tables
    chans, xrows, yrows, zlen = values.shape
    first = jnp.einsum("cxyn,qkn->qkycx", values, z_table, preferred_element_type=jnp.float32)
    first = first.astype(jnp.bfloat16).reshape(2, MZ, yrows, chans * xrows)
    moved = lax.all_to_all(first, ("gy", "col"), split_axis=1, concat_axis=2, tiled=True)
    second = jnp.einsum("pkyr,pyqj->qkjr", moved, y_table, preferred_element_type=jnp.float32)
    second = second.astype(jnp.bfloat16)[:, :, :, None, :]
    crossed = lax.all_to_all(second, "gx", split_axis=2, concat_axis=3, tiled=True)
    crossed = crossed.reshape(crossed.shape[:4] + (chans, xrows))
    third = jnp.einsum("pkjgcx,pgxql->qckjl", crossed, x_table, preferred_element_type=jnp.float32)
    return third.astype(jnp.bfloat16).reshape(2, chans, -1)


def to_grid(spec, tables, shape, local_modes):
    z_table, y_table, x_table = tables
    chans, xrows, yrows, zlen = shape
    spec = spec.reshape((2, chans) + local_modes)
    first = jnp.einsum("pckjl,qgxpl->qkjgcx", spec, x_table, preferred_element_type=jnp.float32)
    first = first.astype(jnp.bfloat16)
    first = first.reshape(first.shape[:4] + (chans * xrows,))
    joined = lax.all_to_all(first, "gx", split_axis=3, concat_axis=2, tiled=True)
    joined = joined.reshape(joined.shape[:3] + (chans * xrows,))
    second = jnp.einsum("pkjr,qypj->qkyr", joined, y_table, preferred_element_type=jnp.float32)
    second = second.astype(jnp.bfloat16)
    returned = lax.all_to_all(second, ("gy", "col"), split_axis=2, concat_axis=1, tiled=True)
    grid = jnp.einsum("pkyr,pkn->ryn", returned, z_table, preferred_element_type=jnp.float32)
    return grid.reshape(chans, xrows, yrows, zlen)


def mix(weight, modes):
    real = jnp.einsum("iok,ik->ok", weight[0], modes[0], preferred_element_type=jnp.float32)
    real = real - jnp.einsum("iok,ik->ok", weight[1], modes[1], preferred_element_type=jnp.float32)
    imag = jnp.einsum("iok,ik->ok", weight[0], modes[1], preferred_element_type=jnp.float32)
    imag = imag + jnp.einsum("iok,ik->ok", weight[1], modes[0], preferred_element_type=jnp.float32)
    return jnp.stack([real, imag]).astype(jnp.bfloat16)


def general(field, cotangent, mode_weight, skip_weight, lift_weight, proj_weight):
    chans, xrows, yrows, zlen = field.shape
    groups_x = lax.axis_size("gx")
    groups_y = lax.axis_size("gy")
    groups_c = lax.axis_size("col")
    span_x = xrows * groups_x
    span_y = yrows * groups_y * groups_c
    column = jnp.arange(MZ, dtype=jnp.int32)
    z_table = real_table(column, zlen)
    y_table = complex_table(centered(MY), span_y)
    x_table = complex_table(centered(MX), span_x).reshape(2, groups_x, xrows, 2, MX)
    tables = (z_table, y_table, x_table)
    local_modes = (mode_weight.shape[3], mode_weight.shape[4], mode_weight.shape[5])
    weight_flat = mode_weight.reshape(2, chans, chans, -1)
    modes = to_modes(field, tables)
    spectral = to_grid(mix(weight_flat, modes), tables, field.shape, local_modes).reshape(chans, -1)
    flat_field = field.reshape(chans, -1)
    flat_grad = cotangent.reshape(chans, -1)
    pre = spectral + jnp.dot(skip_weight, flat_field, preferred_element_type=jnp.float32)
    lifted, slope_pre = gelu_slope(pre)
    lifted = lifted.astype(jnp.bfloat16)
    hidden = jnp.dot(lift_weight, lifted, preferred_element_type=jnp.float32)
    activated, slope_hid = gelu_slope(hidden)
    activated = activated.astype(jnp.bfloat16)
    back_hidden = jnp.dot(proj_weight.T, flat_grad, preferred_element_type=jnp.float32)
    hidden_grad = (back_hidden * slope_hid).astype(jnp.bfloat16)
    grad_up = flat_grad.astype(jnp.float32) + jnp.dot(
        lift_weight.T, hidden_grad, preferred_element_type=jnp.float32
    )
    pre_grad = (grad_up * slope_pre).astype(jnp.bfloat16)
    proj_part = jnp.einsum("cr,hr->ch", flat_grad, activated, preferred_element_type=jnp.float32)
    lift_part = jnp.einsum("hr,cr->hc", hidden_grad, lifted, preferred_element_type=jnp.float32)
    skip_part = jnp.einsum("or,ir->oi", pre_grad, flat_field, preferred_element_type=jnp.float32)
    proj_grad, lift_grad, skip_grad = lax.psum(
        (proj_part, lift_part, skip_part), ("gx", "gy", "col")
    )
    pre_modes = to_modes(pre_grad.reshape(field.shape), tables)
    grad_real = jnp.einsum("ik,ok->iok", modes[0], pre_modes[0], preferred_element_type=jnp.float32)
    grad_real = grad_real + jnp.einsum(
        "ik,ok->iok", modes[1], pre_modes[1], preferred_element_type=jnp.float32
    )
    grad_imag = jnp.einsum("ik,ok->iok", modes[0], pre_modes[1], preferred_element_type=jnp.float32)
    grad_imag = grad_imag - jnp.einsum(
        "ik,ok->iok", modes[1], pre_modes[0], preferred_element_type=jnp.float32
    )
    mode_grad = jnp.stack([grad_real, grad_imag]).astype(jnp.bfloat16).reshape(mode_weight.shape)
    back_real = jnp.einsum(
        "iok,ok->ik", weight_flat[0], pre_modes[0], preferred_element_type=jnp.float32
    )
    back_real = back_real + jnp.einsum(
        "iok,ok->ik", weight_flat[1], pre_modes[1], preferred_element_type=jnp.float32
    )
    back_imag = jnp.einsum(
        "iok,ok->ik", weight_flat[0], pre_modes[1], preferred_element_type=jnp.float32
    )
    back_imag = back_imag - jnp.einsum(
        "iok,ok->ik", weight_flat[1], pre_modes[0], preferred_element_type=jnp.float32
    )
    modes_grad = jnp.stack([back_real, back_imag]).astype(jnp.bfloat16)
    spectral_grad = to_grid(modes_grad, tables, field.shape, local_modes).reshape(chans, -1)
    skip_back = jnp.dot(skip_weight.T, pre_grad, preferred_element_type=jnp.float32)
    field_grad = (spectral_grad + skip_back).astype(jnp.bfloat16).reshape(field.shape)
    return (field_grad, mode_grad, skip_grad, lift_grad, proj_grad)


def np_trig(freqs, length):
    positions = np.arange(length)
    turns = positions[:, None] * (freqs[None, :] % length) % length
    angle = turns.astype(np.float32) * np.float32(2.0 * math.pi / length)
    factor = np.float32(1.0 / math.sqrt(length))
    return np.cos(angle) * factor, np.sin(angle) * factor


def np_complex(cosine, sine, sign):
    table = np.zeros((cosine.shape[0], 2, cosine.shape[1], 2), np.float32)
    table[:, 0, :, 0] = cosine
    table[:, 1, :, 0] = -sign * sine
    table[:, 1, :, 1] = cosine
    table[:, 0, :, 1] = sign * sine
    return table


def make_tables(zlen, span_y, span_x, nb, xrows, yrows):
    kzb, kyb = MZ // nb, MY // nb
    zc, zs = np_trig(np.arange(MZ), zlen)
    yc, ys = np_trig(np.arange(MY) - MY // 2, span_y)
    xc, xs = np_trig(np.arange(MX) - MX // 2, span_x)
    zpart = np.stack([zc, -zs]).reshape(2, zlen, nb, kzb)
    zf = np.einsum("pzbk,yw->yzbwpk", zpart, np.eye(yrows, dtype=np.float32))
    zf = zf.reshape(yrows * zlen, nb, yrows * 2 * kzb).transpose(1, 0, 2)
    zi = np.ascontiguousarray(zf.transpose(0, 2, 1))
    yt = np_complex(yc, ys, -1).reshape(nb, yrows, 2, nb, kyb, 2)
    eye = np.eye(kzb, dtype=np.float32)
    yf = np.einsum("bypjmq,kh->bjypkqhm", yt, eye).reshape(nb, nb, yrows * 2 * kzb, 2 * kzb * kyb)
    yi_t = np_complex(yc, ys, -1).reshape(nb, yrows, 2, nb, kyb, 2)
    yi = np.einsum("bypjmq,kh->jbqhmypk", yi_t, eye).reshape(nb, nb, 2 * kzb * kyb, yrows * 2 * kzb)
    xt = np_complex(xc, xs, -1).reshape(nb, xrows, 2, MX, 2)
    four = np.eye(4, dtype=np.float32)
    xf = np.einsum("bxplq,cd->bpcxqdl", xt, four).reshape(nb, 2, 4 * xrows, 8 * MX)
    xr = np.einsum("bxplq,cd,r->bpcxdqrl", xt, four, np.ones(4, np.float32))
    xr = xr.reshape(nb, 2, 4 * xrows, 32 * MX)
    both = np.stack([xc, xs]).reshape(2, nb, xrows, MX)
    xi = np.einsum("tbxl,r->bxtrl", both, np.ones(4, np.float32)).reshape(nb, xrows, 8 * MX)
    xd = np.einsum("tbxl,cd->bcxtdl", both, four).reshape(nb, 4 * xrows, 8 * MX)
    bf = ml_dtypes.bfloat16
    return [np.asarray(t).astype(bf) for t in (zf, zi, yf, yi, xf, xr)] + [
        xi.astype(bf).astype(np.float32),
        xd.astype(bf),
    ]


def place():
    return lax.axis_index("gy") * lax.axis_size("col") + lax.axis_index("col"), lax.axis_index("gx")


def dot(a, b):
    return lax.dot_general(a, b, (((1,), (0,)), ((), ())), preferred_element_type=jnp.float32)


def dot_nt(a, b):
    return lax.dot_general(a, b, (((1,), (1,)), ((), ())), preferred_element_type=jnp.float32)


BF = jnp.bfloat16
F32 = jnp.float32
STEPS = (0, 2, 3, 1)


def z_table(own):
    z, lane = (lax.broadcasted_iota(jnp.int32, (128, 64), axis) for axis in (0, 1))
    block = jnp.zeros_like(lane)
    for s, step in enumerate(STEPS):
        block = jnp.where(lane // 16 == s, own ^ step, block)
    turns = ((8 * block + lane % 8) * z + 32 * (lane // 8 % 2)) % 128
    values = jnp.cos(turns.astype(F32) * (2.0 * math.pi / 128)) * (1.0 / math.sqrt(128))
    row, at = (lax.broadcasted_iota(jnp.int32, (64, 512), axis) for axis in (0, 1))
    copies = jnp.where((row // 16 == at // 128) & (row % 16 == at % 16), 1.0, 0.0)
    every = dot(values.astype(BF), copies.astype(BF))
    cell = lax.broadcasted_iota(jnp.int32, (128, 512), 1) // 16 % 8
    return jnp.concatenate([jnp.where(cell == y, every, 0.0).astype(BF) for y in range(8)], axis=0)


def z_forward_kernel(rows, yrows, field, o0, o1, o2, o3, wide):
    wide[: field.shape[0]] = field[...].astype(F32)
    side = jnp.concatenate(
        [wide[pl.ds(y, rows, stride=yrows), :].astype(BF) for y in range(yrows)], axis=1
    )
    out = dot(side, z_table(place()[0])).astype(BF)
    for s, o in enumerate((o0, o1, o2, o3)):
        o[...] = out[:, s * 128 : (s + 1) * 128]


def lane_kernel(r0, r1, r2, r3, table, after, o0, o1, o2, o3):
    side = jnp.concatenate([r0[...], r1[...], r2[...], r3[...]], axis=1)
    known = table[...] if len(table.shape) == 2 else lane_table(place(), 0, 1, table)
    out = dot(side, known).astype(BF)
    for t, o in enumerate((o0, o1, o2, o3)):
        o[...] = out[:, t * 128 : (t + 1) * 128]


def x_side(idx, refs, tab):
    parts = []
    for g in range(8):
        block = jnp.concatenate([r[g * 32 : (g + 1) * 32, :] for r in refs], axis=0)
        turned = block.astype(F32).T.astype(BF)
        parts.append(jnp.concatenate([turned[:64, :], turned[64:, :]], axis=1))
    side = jnp.concatenate(parts, axis=0)
    table = jnp.concatenate([tab[idx[1] ^ STEPS[s], p] for p in range(2) for s in range(4)], axis=0)
    return side, table


def add_products(total, weight, modes, o, first):
    real, imag = total
    for g in range(weight.shape[0]):
        wr, wi = weight[g, 0, o].astype(F32), weight[g, 1, o].astype(F32)
        mr, mi = modes[first + g, 0].astype(F32), modes[first + g, 1].astype(F32)
        real = real + wr * mr - wi * mi
        imag = imag + wr * mi + wi * mr
    return real, imag


def mix_forward_kernel(
    r0, r1, r2, r3, xf, xi, early, late, weight, modes, o0, o1, o2, o3, last,
    total, held, sem,
):
    idx = place()
    known = early.shape[0] + late.shape[0]
    copies = pack_copies(known, weight, held, sem)
    side, table = x_side(idx, (r0, r1, r2, r3), xf)
    got = dot(side, table).astype(BF)
    for g in range(8):
        for p in range(2):
            part = got[g * 64 : (g + 1) * 64, p * 128 : (p + 1) * 128]
            modes[g, p] = part
    left = jnp.concatenate([xi[idx[1] ^ STEPS[s]] for s in range(4)], axis=0).astype(BF)
    outs = (o0, o1, o2, o3)
    zero = jnp.zeros((64, 128), F32)

    def begin(o, carry):
        got = add_products((zero, zero), early, modes, o, 0)
        total[o, 0], total[o, 1] = add_products(got, late, modes, o, early.shape[0])
        return carry

    lax.fori_loop(0, 32, begin, 0, unroll=16)
    pack_finish(copies, held, last)

    def pair(k, carry):
        rows = []
        for j in range(2):
            o = 2 * k + j
            real, imag = add_products((total[o, 0], total[o, 1]), last, modes, o, known)
            rows.append(jnp.concatenate([real.astype(BF), (-imag).astype(BF)], axis=1))
            rows.append(jnp.concatenate([imag.astype(BF), real.astype(BF)], axis=1))
        got = dot_nt(left, jnp.concatenate(rows, axis=0))
        for s in range(4):
            both = jnp.concatenate(
                [got[s * 8 : (s + 1) * 8, :128], got[s * 8 : (s + 1) * 8, 128:]], axis=0
            )
            outs[s][pl.ds(pl.multiple_of(k * 16, 16), 16), :] = both.astype(BF)
        return carry

    lax.fori_loop(0, 16, pair, 0, unroll=8)


def mix_backward_kernel(
    r0, r1, r2, r3, xr, xd, early, late, last, pmodes, o0, o1, o2, o3
):
    idx = place()
    side, table = x_side(idx, (r0, r1, r2, r3), xr)
    for d in range(4):
        got = dot(side, table[:, d * 256 : (d + 1) * 256]).astype(BF)
        for g in range(8):
            for p in range(2):
                part = got[g * 64 : (g + 1) * 64, p * 128 : (p + 1) * 128]
                pmodes[4 * g + d, p] = part
    left = jnp.concatenate([xd[idx[1] ^ STEPS[s]] for s in range(4)], axis=0)
    outs = (o0, o1, o2, o3)

    def group(weight, first, at, carry):
        g = first + at
        real = jnp.zeros((64, 128), F32)
        imag = jnp.zeros((64, 128), F32)
        for o in range(32):
            wr, wi = weight[at, 0, o].astype(F32), weight[at, 1, o].astype(F32)
            pr, pi = pmodes[o, 0].astype(F32), pmodes[o, 1].astype(F32)
            real = real + wr * pr + wi * pi
            imag = imag + wr * pi - wi * pr
        rows = [
            jnp.concatenate([real.astype(BF), (-imag).astype(BF)], axis=1),
            jnp.concatenate([imag.astype(BF), real.astype(BF)], axis=1),
        ]
        got = dot_nt(left, jnp.concatenate(rows, axis=0)).astype(BF)
        for s in range(4):
            outs[s][pl.ds(pl.multiple_of(g * 32, 32), 32), :] = got[s * 32 : (s + 1) * 32]
        return carry

    first = 0
    for weight in (early, late, last):
        lax.fori_loop(0, weight.shape[0], functools.partial(group, weight, first), 0)
        first += weight.shape[0]


def pack_copies(first, weight, held, sem):
    span = held.shape[3] // 4
    copies = []
    for g in range(held.shape[0]):
        for h in range(4):
            part = pl.ds(h * span, span)
            copies.append(
                pltpu.make_async_copy(
                    weight.at[:, pl.ds(4 * (first + g), 4), part],
                    held.at[g, :, :, part],
                    sem.at[g, h],
                )
            )
            copies[-1].start()
    return copies


def pack_finish(copies, held, packed):
    row, lane = (lax.broadcasted_iota(jnp.int32, (32, 128), axis) for axis in (0, 1))
    moved = jnp.where(lane == row + 96, 1.0, 0.0).astype(BF)
    span = held.shape[3] // 4
    for g in range(held.shape[0]):
        for h in range(4):
            copies[4 * g + h].wait()

            def step(o, carry):
                for p in range(2):
                    three = [held[g, p, k, o] for k in range(3)] + [jnp.zeros((64, 32), BF)]
                    fourth = dot(held[g, p, 3, o], moved).astype(BF)
                    packed[g, p, o] = jnp.concatenate(three, axis=1) + fourth
                return carry

            lax.fori_loop(h * span, (h + 1) * span, step, 0, unroll=8)


def pack_kernel(first, weight, after, packed, token, held, sem):
    pack_finish(pack_copies(first, weight, held, sem), held, packed)
    token[...] = jnp.zeros_like(token)


def outer_start(start, modes, pmodes, grad, held, turned, sem):
    span = pmodes.shape[0] // 4
    copies = []
    for g in range(held.shape[0]):
        for p in range(2):
            m = modes[start + g, p].astype(F32)
            for k in range(3):
                turned[k, p] = (pltpu.roll(m, (128 - 32 * k) % 128, 1) if k else m).astype(BF)
        for h in range(4):

            def step(o, carry):
                pr, pi = pmodes[o, 0], pmodes[o, 1]
                for k in range(3):
                    mr, mi = turned[k, 0], turned[k, 1]
                    both = mr * pr + mi * pi, mr * pi - mi * pr
                    for p in range(2):
                        held[g, p, k, o] = both[p][:, :32]
                        if k == 1:
                            held[g, p, 3, o] = pltpu.roll(both[p], 64, 1)[:, :32]
                return carry

            lax.fori_loop(h * span, (h + 1) * span, step, 0, unroll=8)
            part = pl.ds(h * span, span)
            copies.append(
                pltpu.make_async_copy(
                    held.at[g, :, :, part],
                    grad.at[:, pl.ds(4 * (start + g), 4), part],
                    sem.at[g, h],
                )
            )
            copies[-1].start()
    return copies


def outer_scratch(count, chans):
    return [
        pltpu.VMEM((count, 2, 4, chans, 64, 32), BF),
        pltpu.VMEM((3, 2, 64, 128), BF),
        pltpu.SemaphoreType.DMA((count, 4)),
    ]


def outer_kernel(start, modes, pmodes, *rest):
    grad, token, held, turned, sem = rest[-5:]
    for copy in outer_start(start, modes, pmodes, grad, held, turned, sem):
        copy.wait()
    token[...] = jnp.zeros_like(token)


def gelu_pair(value):
    square = value * value
    half = 0.5 + 0.5 * jnp.tanh(value * (KAPPA + (KAPPA * CUBIC) * square))
    tail = (1.0 - half) * value * (2.0 * KAPPA + (6.0 * KAPPA * CUBIC) * square)
    return value * half, half + half * tail


def turn(value):
    return value.astype(F32).T.astype(BF)


def spread(block, count):
    rows, lanes = block.shape
    wide = jnp.concatenate([block.astype(F32)] * count, axis=1)
    tall = jnp.concatenate([wide] * count, axis=0)
    at_row = lax.broadcasted_iota(jnp.int32, tall.shape, 0) // rows
    at_lane = lax.broadcasted_iota(jnp.int32, tall.shape, 1) // lanes
    return jnp.where(at_row == at_lane, tall, 0.0).astype(BF)


def by_step(idx, at, table, axis):
    return jnp.concatenate([table[idx[at] ^ STEPS[s]] for s in range(4)], axis=axis)


def lane_table(idx, near, far, table):
    cols = []
    for t in range(4):
        rows = [table[idx[near] ^ STEPS[s], idx[far] ^ STEPS[t]] for s in range(4)]
        cols.append(jnp.concatenate(rows, axis=0))
    return jnp.concatenate(cols, axis=1)


def cells_kernel(
    field, cotangent, skip, lift_t, proj, zf, zi, yf, yi,
    fx, cx, skipped, backed, dskip_t, dlift, dlift_t, zfp, zip_, yfp, yip, wide,
):
    idx = place()
    for src, dst in ((field, fx), (cotangent, cx)):
        wide[: src.shape[0]] = src[...].astype(F32)

        def step(k, carry):
            parts = []
            for sub in range(8):
                first = 16 * k + 2 * sub
                parts.append(
                    jnp.concatenate(
                        [wide[pl.ds(first + j, 32, stride=64), :] for j in range(2)], axis=1
                    ).astype(BF)
                )
            dst[k] = jnp.concatenate(parts, axis=0)
            return carry

        lax.fori_loop(0, 4, step, 0)
    dskip = spread(skip[...], 8)
    dproj = spread(turn(proj[...]), 8)
    for k in range(4):
        skipped[k] = dot(dskip, fx[k])
        backed[k] = dot(dproj, cx[k])
    zfp[...] = by_step(idx, 0, zf, 1)
    zip_[...] = by_step(idx, 0, zi, 0)
    yfp[...] = lane_table(idx, 0, 1, yf)
    yip[...] = lane_table(idx, 1, 0, yi)
    dskip_t[...] = spread(turn(skip[...]), 8)
    dlift[...] = spread(turn(lift_t[...]), 8)
    dlift_t[...] = spread(lift_t[...], 2)


def inverse_z(refs, back, spectral):
    side = jnp.concatenate([r[...] for r in refs], axis=1)
    for y in range(4):
        got = dot(side, back[:, y * 256 : (y + 1) * 256])
        spectral[2 * y, : got.shape[0]] = got[:, :128]
        spectral[2 * y + 1, : got.shape[0]] = got[:, 128:]


def cell_rows(spectral, k):
    parts = []
    for sub in range(8):
        rows = pl.ds(2 * k + sub // 4, 32, stride=8)
        parts.append(
            jnp.concatenate([spectral[2 * (sub % 4) + j, rows, :] for j in range(2)], axis=1)
        )
    return jnp.concatenate(parts, axis=0)


def point_kernel(
    r0, r1, r2, r3, back, table, cx, skipped, backed, dlift, dlift_t,
    o0, o1, o2, o3, pg, act, hid, lif, spectral, wide,
):
    inverse_z((r0, r1, r2, r3), back, spectral)

    def step(k, carry):
        grads = cx[k]
        pre = cell_rows(spectral, k) + skipped[k]
        lifted, slope_pre = gelu_pair(pre)
        lifted = lifted.astype(BF)
        lif[k] = lifted
        hidden = dot(dlift[...], lifted)
        up = []
        for q in range(4):
            part = slice(q * 256, (q + 1) * 256)
            activated, slope_hid = gelu_pair(hidden[part])
            hidden_grad = (backed[k, part] * slope_hid).astype(BF)
            act[k, part] = activated.astype(BF)
            hid[k, part] = hidden_grad
            up.append(dot(dlift_t[...], hidden_grad))
        pre_grad = (grads.astype(F32) + jnp.concatenate(up, axis=0)) * slope_pre
        pg[k] = pre_grad.astype(BF)
        for sub in range(8):
            rows = pl.ds(2 * k + sub // 4, 32, stride=8)
            for j in range(2):
                wide[2 * (sub % 4) + j, rows, :] = pre_grad[
                    sub * 32 : (sub + 1) * 32, j * 128 : (j + 1) * 128
                ]
        return carry

    lax.fori_loop(0, 4, step, 0, unroll=4)
    side = jnp.concatenate([wide[y, :256].astype(BF) for y in range(8)], axis=1)
    out = dot(side, table[...]).astype(BF)
    for s, o in enumerate((o0, o1, o2, o3)):
        o[...] = out[:, s * 128 : (s + 1) * 128]


def sums_kernel(fx, cx, pg, act, hid, lif, sums):
    def step(k, carry):
        proj, lift, skip = carry
        for sub in range(8):
            c = slice(sub * 32, (sub + 1) * 32)
            h = slice(sub * 128, (sub + 1) * 128)
            proj = proj + dot_nt(cx[k, c], act[k, h])
            lift = lift + dot_nt(lif[k, c], hid[k, h])
            skip = skip + dot_nt(pg[k, c], fx[k, c])
        return proj, lift, skip

    zero = jnp.zeros((32, 128), F32)
    got = lax.fori_loop(0, 4, step, (zero, zero, jnp.zeros((32, 32), F32)))
    sums[0:32] = got[0]
    sums[32:64] = got[1]
    sums[64:96] = jnp.concatenate([got[2]] * 4, axis=1)


def finish_kernel(
    start, r0, r1, r2, r3, back, pg, dskip_t, part, other, modes, pmodes, so_far,
    out, proj, lift, skip, grad, spectral, wide, held, turned, sem,
):
    copies = outer_start(start, modes, pmodes, grad, held, turned, sem)
    sums = part[...] + other[...]
    proj[...] = sums[:32]
    lift[...] = sums[32:64]
    skip[...] = sums[64:, :32]
    inverse_z((r0, r1, r2, r3), back, spectral)

    def step(k, carry):
        got = cell_rows(spectral, k) + dot(dskip_t[...], pg[k])
        for sub in range(8):
            first = 16 * k + 2 * sub
            for j in range(2):
                wide[pl.ds(first + j, 32, stride=64), :] = got[
                    sub * 32 : (sub + 1) * 32, j * 128 : (j + 1) * 128
                ]
        return carry

    lax.fori_loop(0, 4, step, 0, unroll=4)
    out[...] = wide[: out.shape[0]].astype(BF)
    for copy in copies:
        copy.wait()


PACK = (2, 3, 3)
OUTER = (3, 2, 3)
VM = pl.BlockSpec(memory_space=pltpu.VMEM)
ANY = pl.BlockSpec(memory_space=pl.ANY)
HBM = pl.BlockSpec(memory_space=pltpu.HBM)
BLOCK = jax.ShapeDtypeStruct((256, 128), BF)
MIB = 1024 * 1024


def cost(us):
    return pl.CostEstimate(flops=0, bytes_accessed=int(us * 3.0e6), transcendentals=0)


def call(
    kernel, ins, outs, scratch=(), name=None, mib=8, us=1.0, free=0, far_out=(), alias={}
):
    return pl.pallas_call(
        kernel,
        out_shape=outs,
        in_specs=[VM] * (len(ins) - free) + [ANY] * free,
        out_specs=[ANY if at in far_out else VM for at in range(len(outs))],
        scratch_shapes=list(scratch),
        input_output_aliases=alias,
        compiler_params=pltpu.CompilerParams(vmem_limit_bytes=mib * MIB),
        cost_estimate=cost(us),
        name=name,
    )(*ins)


TOKEN = jax.ShapeDtypeStruct((8, 128), F32)


def pack(weight, first, count, after, us):
    chans = weight.shape[1]
    return pl.pallas_call(
        functools.partial(pack_kernel, first),
        out_shape=[jax.ShapeDtypeStruct((count, 2, chans, 64, 128), BF), TOKEN],
        in_specs=[ANY, ANY],
        out_specs=[VM, VM],
        scratch_shapes=[
            pltpu.VMEM((count, 2, 4, chans, 64, 32), BF),
            pltpu.SemaphoreType.DMA((count, 4)),
        ],
        compiler_params=pltpu.CompilerParams(vmem_limit_bytes=36 * MIB),
        cost_estimate=cost(us),
        name="pack",
    )(weight, after)


def exchange(blocks, axes):
    got = [
        lax.ppermute(block, axes, [(a, a ^ step) for a in range(4)])
        for block, step in zip(blocks[1:], STEPS[1:])
    ]
    return [blocks[0]] + got


def swap(part, axis, step):
    size = lax.axis_size(axis)
    return lax.ppermute(part, axis, [(a, a ^ step) for a in range(size)])


def fast(field, cotangent, mode_weight, skip_weight, lift_weight, proj_weight):
    chans, xrows, yrows, zlen = field.shape
    tables = make_tables(zlen, yrows * 4, xrows * 4, 4, xrows, yrows)
    zf, zi, yf, yi, xf, xr, xi, xd = [jnp.asarray(t) for t in tables]
    gyc = ("gy", "col")
    four = [BLOCK] * 4
    cells = chans * xrows * yrows
    flat_field = field.reshape(cells, zlen)
    flat_cot = cotangent.reshape(cells, zlen)
    rows = chans * xrows
    wide = pltpu.VMEM((cells + 64, zlen), F32)
    tall = pltpu.VMEM((yrows, rows + 8, zlen), F32)
    weight = mode_weight.reshape(2, chans, chans, 64, 32)
    lift_t = lift_weight.T

    def bf(*shape):
        return jax.ShapeDtypeStruct(shape, BF)

    def lanes(got, table, after, name):
        return call(lane_kernel, (*got, table, after), four, (), name, 4, 1.0, free=1)

    sent = call(
        functools.partial(z_forward_kernel, rows, yrows), (flat_field,), four, [wide],
        "z_forward", 8, 2.0,
    )
    got = exchange(sent, gyc)
    one, two, three = PACK
    early, token = pack(weight, 0, one, sent[0], 3.0)
    sent = lanes(got, yf, token, "y_forward")
    got = exchange(sent, "gx")
    late, _ = pack(weight, one, two, sent[0], 5.0)
    modes, *sent, last = call(
        mix_forward_kernel, (*got, xf, xi, early, late, weight),
        [bf(8, 2, 64, 128)] + four + [bf(three, 2, chans, 64, 128)],
        [
            pltpu.VMEM((chans, 2, 64, 128), F32),
            pltpu.VMEM((three, 2, 4, chans, 64, 32), BF),
            pltpu.SemaphoreType.DMA((three, 4)),
        ],
        "mix_forward", 36, 8.0, free=1,
    )
    got = exchange(sent, "gx")
    fx, cx, skipped, backed, dskip_t, dlift, dlift_t, zfp, zip_, yfp, yip = call(
        cells_kernel,
        (flat_field, flat_cot, skip_weight, lift_t, proj_weight, zf, zi, yf, yi),
        [bf(4, 256, 256)] * 2
        + [jax.ShapeDtypeStruct((4, 256, 256), F32), jax.ShapeDtypeStruct((4, 1024, 256), F32)]
        + [bf(256, 256), bf(1024, 256), bf(64, 256)]
        + [bf(1024, 512), bf(512, 1024), bf(512, 512), bf(512, 512)],
        [wide], "cells", 8, 3.0,
    )
    sent = lanes(got, yip, fx, "y_inverse")
    got = exchange(sent, gyc)
    *sent, pg, act, hid, lif = call(
        point_kernel,
        (*got, zip_, zfp, cx, skipped, backed, dlift, dlift_t),
        four + [bf(4, 256, 256), bf(4, 1024, 256), bf(4, 1024, 256), bf(4, 256, 256)],
        [tall, tall], "point", 8, 6.0,
    )
    got = exchange(sent, gyc)
    (part,) = call(
        sums_kernel, (fx, cx, pg, act, hid, lif),
        [jax.ShapeDtypeStruct((96, 128), F32)], (), "sums", 4, 2.5,
    )
    sent = lanes(got, yfp, part, "y_forward")
    got = exchange(sent, "gx")
    for axis in ("col", "gy", "gx"):
        part = part + swap(part, axis, 1)
    other = swap(part, "gx", 2)
    grads = bf(2, chans, chans, 64, 32)
    begin, middle, end = OUTER
    pmodes, *sent = call(
        mix_backward_kernel, (*got, xr, xd, early, late, last),
        [bf(32, 2, 64, 128)] + four, (), "mix_backward", 12, 5.0,
    )
    got = exchange(sent, "gx")
    grad, token = call(
        functools.partial(outer_kernel, 0), (modes, pmodes), [grads, TOKEN],
        outer_scratch(begin, chans), "outer", 20, 5.0, far_out=(0,),
    )
    sent = lanes(got, yip, token, "y_inverse")
    got = exchange(sent, gyc)
    grad, _ = call(
        functools.partial(outer_kernel, begin), (modes, pmodes, sent[0], grad),
        [grads, TOKEN], outer_scratch(middle, chans), "outer", 20, 4.0, free=2,
        far_out=(0,), alias={3: 0},
    )
    field_grad, proj_grad, lift_grad, skip_grad, mode_grad = call(
        functools.partial(finish_kernel, begin + middle),
        (*got, zip_, pg, dskip_t, part, other, modes, pmodes, grad),
        [bf(cells, zlen)]
        + [jax.ShapeDtypeStruct((chans, n), F32) for n in (128, 128, 32)]
        + [grads],
        [tall, wide] + outer_scratch(end, chans), "finish", 24, 4.0, free=1,
        far_out=(4,), alias={11: 4},
    )
    return (
        field_grad.reshape(field.shape),
        mode_grad.reshape(mode_weight.shape),
        skip_grad,
        lift_grad.T,
        proj_grad,
    )


def fits(field, mode_weight):
    sizes = [lax.axis_size(a) for a in ("gx", "gy", "col")]
    return (
        sizes == [4, 2, 2]
        and field.shape == (32, 8, 8, 128)
        and mode_weight.shape == (2, 32, 32, 8, 8, 32)
    )


def on_device(*args):
    return fast(*args) if fits(args[0], args[2]) else general(*args)


def solution(mesh):
    in_specs = (
        P("grp", "gx", ("gy", "col"), None),
        P("grp", "gx", ("gy", "col"), None),
        P(None, None, None, ("gy", "col"), "gx", None),
        P(),
        P(),
        P(),
    )
    out_specs = (
        P("grp", "gx", ("gy", "col"), None),
        P("grp", None, None, ("gy", "col"), "gx", None),
        P("grp", None),
        P("grp", None),
        P("grp", None),
    )
    return jax.shard_map(
        on_device, mesh=mesh, in_specs=in_specs, out_specs=out_specs, check_vma=False
    )
```
